32 devices in a mesh: seq: 8 (over y, x, core), section: 4 (over z).
Axes of the slice: x: 2, y: 2, z: 4, core: 2. Of those that a mesh axis runs over, the one named last changes fastest.
Arguments:
- tokens: bfloat16 [4096, 1024], P('seq'), may hold values from -6 to 6
- input_gain: float32 [4, 1024], P('section'), may hold values from 0.5 to 2
- main_weight: bfloat16 [4, 1024, 4096], P('section'), may hold values from -0.1875 to 0.1875
- side_weight: bfloat16 [4, 1024, 288], P('section'), may hold values from -0.1875 to 0.1875
- conv_kernel: float32 [4, 4, 2304], P('section'), may hold values from -3 to 3
- step_bias: float32 [4, 32], P('section'), may hold values from -4 to 1
- decay_rate: float32 [4, 32], P('section'), may hold values from 0.0001 to 0.04, as said below
- skip_gain: float32 [4, 32], P('section'), may hold values from 1 to 4
- output_gain: float32 [4, 2048], P('section'), may hold values from 0.5 to 2
- output_weight: bfloat16 [4, 2048, 1024], P('section', 'seq'), may hold values from -0.09375 to 0.09375
Outputs:
- layer_outputs: bfloat16 [4, 4096, 1024], P('section', 'seq')
The draws below stay inside these ranges and needn't reach their ends.
Inputs may be any that keep to these rules, and one draw needn't show every extreme that they name: `decay_rate`: positive.
All inputs are finite; a program needn't handle non-finite values.
Results may differ from the reference program's by a relative error of at most 0.0074.
Values may be sent and summed in bfloat16 or wider, within the bound.
No kernel may reach another device: no remote copies, remote signals or barrier semaphores. Data moves between devices by JAX's collectives and lax.ppermute only.
A program may use at most 128 MiB of HBM per device.

```python
import math
import jax
import jax.numpy as jnp
from jax import lax

D = 1024
HEADS = 32
STATE = 128
BLOCK = 256
CONV = 4
INNER = 2048
LAYERS = 2
TOKENS = 4096


def slow_heads(key, slow_share):
    return jax.random.bernoulli(jax.random.fold_in(key, 977), slow_share, (2 * LAYERS, HEADS))


def draw_step_bias(key, part):
    slow_share = 0.5
    is_slow = slow_heads(key, slow_share)
    key = jax.random.fold_in(key, 11)
    spread = jax.random.uniform(key, (2 * LAYERS, HEADS), jnp.float32)
    return jnp.where(is_slow, spread - 4.0, spread)


def draw_decay_rate(key, part):
    slow_share = 0.5
    is_slow = slow_heads(key, slow_share)
    key = jax.random.fold_in(key, 23)
    spread = jax.random.uniform(key, (2 * LAYERS, HEADS), jnp.float32)
    slow_rate = (0.2 + 0.8 * spread) * 20.0 / TOKENS
    fast_rate = 0.015 + 0.025 * spread
    return jnp.where(is_slow, slow_rate, fast_rate)


def steps_of(rng, extent, cuts, smallest, top_value):
    def one(dim, blocks):
        heights = jax.random.uniform(jax.random.fold_in(jax.random.fold_in(rng, 6), dim), (blocks,), jnp.float32, smallest / len(cuts), top_value / len(cuts))
        return jnp.repeat(jnp.exp(heights), extent[dim] // blocks).reshape((-1,) + (1,) * (len(extent) - dim - 1))

    gain = one(*cuts[0])
    for cut in cuts[1:]:
        gain = gain * one(*cut)
    return gain


def bell_draw(own_key, dims, scale, limit, cuts=(), kind=jnp.bfloat16):
    loudness = steps_of(own_key, dims, cuts, -0.22, 0.18) if cuts else 1.0
    entries = jax.random.normal(own_key, dims, jnp.float32) * scale * loudness
    return jnp.minimum(jnp.maximum(entries, -limit), limit).astype(kind)


def setup_inputs(seed: int = 0) -> dict:
    seeds = jax.random.split(jax.random.key(seed), 11)
    tokens = bell_draw(seeds[0], (TOKENS, D), 1.0, 6.0, ((0, 8),))
    input_gain = jnp.clip(jnp.exp(math.log(2.0) - 1.3862944 * jax.random.uniform(seeds[1], (2 * LAYERS, D), jnp.float32) ** steps_of(seeds[1], (2 * LAYERS, D), ((0, 4),), -0.2, 0.2)), 0.5, 2.0)
    main_weight = bell_draw(seeds[2], (2 * LAYERS, D, 2 * INNER), D ** -0.5, 0.1875, ((0, 4),))
    side_weight = bell_draw(seeds[3], (2 * LAYERS, D, 2 * STATE + HEADS), D ** -0.5, 0.1875, ((0, 4),))
    conv_kernel = bell_draw(seeds[4], (2 * LAYERS, CONV, INNER + 2 * STATE), CONV ** -0.5, 3.0, ((0, 4),), jnp.float32)
    step_bias = draw_step_bias(jax.random.fold_in(seeds[10], 71), 0)
    decay_rate = draw_decay_rate(jax.random.fold_in(seeds[10], 71), 0)
    skip_gain = jnp.clip(jnp.exp(math.log(4.0) - 1.3862944 * jax.random.uniform(seeds[7], (2 * LAYERS, HEADS), jnp.float32) ** steps_of(seeds[7], (2 * LAYERS, HEADS), ((0, 4),), -0.2, 0.2)), 1.0, 4.0)
    output_gain = jnp.clip(jnp.exp(math.log(2.0) - 1.3862944 * jax.random.uniform(seeds[8], (2 * LAYERS, INNER), jnp.float32) ** steps_of(seeds[8], (2 * LAYERS, INNER), ((0, 4),), -0.2, 0.2)), 0.5, 2.0)
    output_weight = bell_draw(seeds[9], (2 * LAYERS, INNER, D), (2 * INNER) ** -0.5, 0.09375, ((0, 4), (1, 8)))
    return {"tokens": tokens, "input_gain": input_gain, "main_weight": main_weight, "side_weight": side_weight, "conv_kernel": conv_kernel, "step_bias": step_bias, "decay_rate": decay_rate, "skip_gain": skip_gain, "output_gain": output_gain, "output_weight": output_weight}


EPSILON = 1e-05

def norm_rows(values, gain_row):
    widened = values.astype(jnp.float32)
    inverse_rms = lax.rsqrt(lax.optimization_barrier(jnp.mean(widened * widened, axis=-1, keepdims=True)) + EPSILON)
    return (widened * inverse_rms * gain_row).astype(jnp.bfloat16)

def gate_norm(convolved, gate_in, gain_row):
    gated = convolved * jax.nn.silu(gate_in.astype(jnp.float32))
    inverse_rms = lax.rsqrt(lax.optimization_barrier(jnp.mean(gated * gated, axis=-1, keepdims=True)) + EPSILON)
    return (gated * inverse_rms * gain_row).astype(jnp.bfloat16)

def project(normed, main_weight, side_weight, inner_size, state_size):
    projected = jnp.dot(normed, main_weight, preferred_element_type=jnp.float32).astype(jnp.bfloat16)
    side_columns = jnp.dot(normed, side_weight, preferred_element_type=jnp.float32).astype(jnp.bfloat16)
    channel = jnp.concatenate([projected[:, inner_size:], side_columns[:, :2 * state_size]], axis=1)
    return (projected[:, :inner_size], channel, side_columns[:, 2 * state_size:])

def causal_filter(channel, before, kernel):
    length = channel.shape[0]
    padded = jnp.concatenate([before, channel], axis=0).astype(jnp.float32)
    running = kernel[0] * padded[0:length]
    for offset in range(1, kernel.shape[0]):
        running = running + kernel[offset] * padded[offset:offset + length]
    return jax.nn.silu(running).astype(jnp.bfloat16)

def block_terms(inner_rows, input_coef, output_coef, step_size, log_decay, head_count):
    blocks, length, inner_size = inner_rows.shape
    inner_heads = inner_rows.reshape(blocks, length, head_count, inner_size // head_count)
    cumulative = jnp.cumsum(log_decay, axis=1)
    scores = jnp.einsum('ctn,csn->cts', output_coef.astype(jnp.float32), input_coef.astype(jnp.float32))
    cum_heads = jnp.transpose(cumulative, (0, 2, 1))
    decay_gap = cum_heads[:, :, :, None] - cum_heads[:, :, None, :]
    position = jnp.arange(length)
    causal = position[:, None] >= position[None, :]
    kept_share = jnp.where(causal, jnp.exp(jnp.minimum(decay_gap, 0.0)), 0.0)
    step_heads = jnp.transpose(step_size, (0, 2, 1))
    weights = (scores[:, None, :, :] * kept_share * step_heads[:, :, None, :]).astype(jnp.bfloat16)
    within = jnp.einsum('chts,cshp->cthp', weights.astype(jnp.float32), inner_heads.astype(jnp.float32))
    block_end = cumulative[:, -1:, :]
    weighted = inner_heads.astype(jnp.float32) * (jnp.exp(block_end - cumulative) * step_size)[..., None]
    states = jnp.einsum('clhp,cln->chpn', weighted, input_coef.astype(jnp.float32), precision=lax.Precision.HIGHEST)
    totals = jnp.exp(block_end[:, 0, :])
    return (within, states, totals, cumulative)

def carried_terms(output_coef, cumulative, entering):
    product = jnp.einsum('ctn,chpn->cthp', output_coef.astype(jnp.float32), entering, precision=lax.Precision.HIGHEST)
    return product * jnp.exp(cumulative)[..., None]

def scan_direction(channel, raw_step, kernel, step_shift, decay, skip_row, head_count, inner_size, state_size):
    length = channel.shape[0]
    head_dim = inner_size // head_count
    before = jnp.zeros((kernel.shape[0] - 1, channel.shape[1]), jnp.bfloat16)
    convolved = causal_filter(channel, before, kernel)
    step_size = jax.nn.softplus(raw_step.astype(jnp.float32) + step_shift)
    log_decay = -step_size * decay
    blocks = length // BLOCK
    pieces = (convolved[:, :inner_size].reshape(blocks, BLOCK, inner_size), convolved[:, inner_size:inner_size + state_size].reshape(blocks, BLOCK, state_size), convolved[:, inner_size + state_size:].reshape(blocks, BLOCK, state_size), step_size.reshape(blocks, BLOCK, head_count), log_decay.reshape(blocks, BLOCK, head_count))

    def advance(entering, members):
        inner_one, input_one, output_one, step_one, decay_one = [member[None] for member in members]
        within, states, totals, cumulative = block_terms(inner_one, input_one, output_one, step_one, decay_one, head_count)
        output = within + carried_terms(output_one, cumulative, entering[None])
        following = totals[0][:, None, None] * entering + states[0]
        return (following, output[0])
    initial = jnp.zeros((head_count, head_dim, state_size), jnp.float32)
    ending, outputs = lax.scan(advance, initial, pieces)
    inner_heads = convolved[:, :inner_size].astype(jnp.float32).reshape(length, head_count, head_dim)
    combined = outputs.reshape(length, head_count, head_dim) + inner_heads * skip_row[None, :, None]
    return combined.reshape(length, inner_size)

def reference(tokens, input_gain, main_weight, side_weight, conv_kernel, step_bias, decay_rate, skip_gain, output_gain, output_weight):
    head_count = decay_rate.shape[-1]
    inner_size = output_weight.shape[1]
    state_size = (side_weight.shape[2] - head_count) // 2
    current = tokens
    outputs = []
    for layer_index in range(LAYERS):
        terms = []
        for direction in range(2):
            entry = 2 * layer_index + direction
            normed = norm_rows(current, input_gain[entry])
            gate_in, channel, raw_step = project(normed, main_weight[entry], side_weight[entry], inner_size, state_size)
            if direction == 1:
                channel = jnp.flip(channel, 0)
                raw_step = jnp.flip(raw_step, 0)
                gate_in = jnp.flip(gate_in, 0)
            mixed_rows = scan_direction(channel, raw_step, conv_kernel[entry], step_bias[entry], decay_rate[entry], skip_gain[entry], head_count, inner_size, state_size)
            normed_out = gate_norm(mixed_rows, gate_in, output_gain[entry])
            if direction == 1:
                normed_out = jnp.flip(normed_out, 0)
            terms.append(jnp.dot(normed_out, output_weight[entry], preferred_element_type=jnp.float32))
        current = (current.astype(jnp.float32) + (terms[0] + terms[1])).astype(jnp.bfloat16)
        outputs.append(current)
        outputs.append(current)
    return jnp.stack(outputs)
```

```python
import functools

import jax
import jax.numpy as jnp
import numpy as np
from jax import lax
from jax.experimental import pallas as pl
from jax.experimental.pallas import tpu as pltpu
from jax.sharding import PartitionSpec as P

EPSILON = 1e-05
CHUNK = 128
WIDTH = 512
HALO = 16
LOG2E = 1.4426950408889634
F32 = jnp.float32
BF16 = jnp.bfloat16


def silu(value):
    half = 0.5 * value
    return half + half * jnp.tanh(half)


def dot(left, right):
    return jnp.dot(left, right, preferred_element_type=F32)


def order_matrix(size, reverse):
    row = lax.broadcasted_iota(jnp.int32, (size, size), 0)
    column = lax.broadcasted_iota(jnp.int32, (size, size), 1)
    target = jnp.where(reverse == 1, size - 1 - row, row)
    return jnp.where(column == target, 1.0, 0.0).astype(BF16)


def high_low(value):
    high = value.astype(BF16)
    low = (value - high.astype(F32)).astype(BF16)
    return jnp.concatenate([high, low], axis=1)


def norm_block(values, gain_row):
    widened = values.astype(F32)
    inverse_rms = lax.rsqrt(jnp.mean(widened * widened, axis=-1, keepdims=True) + EPSILON)
    return (widened * inverse_rms * gain_row).astype(BF16)


def prep_kernel(
    info,
    rows,
    halo,
    gain,
    wide,
    side_weight,
    taps,
    side_taps,
    bias,
    decay,
    spread,
    normed_out,
    x_out,
    b_out,
    c_out,
    cum_out,
    shifted_out,
    reach_out,
    local_out,
    state_out,
    extended,
    buffer,
    turned,
    shares,
    wide_shares,
    running,
):
    step_index = pl.program_id(0)
    reverse = info[0]
    length = rows.shape[0]
    heads = bias.shape[1]
    state = b_out.shape[1]
    chunks = length // CHUNK
    margin = taps.shape[0] - 1
    width = wide.shape[1]
    heads_here = cum_out.shape[2]

    def filtered(kernel, start, size, lanes):
        total = None
        for k in range(margin + 1):
            part = buffer[HALO - margin + k + start : HALO - margin + k + start + size, lanes]
            term = kernel[k : k + 1, lanes] * part
            total = term if total is None else total + term
        return silu(total).astype(BF16)

    @pl.when(step_index == 0)
    def _():
        turn = order_matrix(2 * CHUNK, reverse)
        small_turn = order_matrix(HALO, reverse)
        edge = norm_block(halo[...], gain[...])
        extended[0:HALO] = dot(small_turn, edge).astype(BF16)
        pairs = length // (2 * CHUNK)
        for pair in range(pairs):
            source = jnp.where(reverse == 1, pairs - 1 - pair, pair) * (2 * CHUNK)
            source = pl.multiple_of(source, 2 * CHUNK)
            piece = norm_block(rows[pl.ds(source, 2 * CHUNK), :], gain[...])
            start = HALO + pair * 2 * CHUNK
            extended[start : start + 2 * CHUNK] = dot(turn, piece).astype(BF16)
        normed_out[...] = extended[HALO:]
        side = dot(extended[...], side_weight[...]).astype(BF16).astype(F32)
        buffer[:, 0 : 2 * state] = side[:, 0 : 2 * state]
        raw = side[HALO:, 2 * state :] + bias[...]
        step = jnp.maximum(raw, 0.0) + jnp.log1p(jnp.exp(-jnp.abs(raw)))
        change = step * (decay[...] * (-LOG2E))
        row = lax.broadcasted_iota(jnp.int32, (CHUNK, CHUNK), 0)
        column = lax.broadcasted_iota(jnp.int32, (CHUNK, CHUNK), 1)
        triangle = jnp.where(row >= column, 1.0, 0.0).astype(F32)
        before = jnp.zeros((1, heads), F32)
        totals = []
        befores = []
        for c in range(chunks):
            here = slice(c * CHUNK, (c + 1) * CHUNK)
            cumulative = jnp.dot(
                triangle, change[here], preferred_element_type=F32, precision=lax.Precision.HIGHEST
            )
            last = cumulative[CHUNK - 1 :, :]
            befores.append(before)
            totals.append(last)
            before = before + last
            for j in range(heads // heads_here):
                cum_out[j, here, :] = cumulative[:, j * heads_here : (j + 1) * heads_here]
            moved = cumulative - jnp.log2(step[here])
            padded = jnp.concatenate([moved, jnp.zeros((CHUNK, 128 - heads), F32)], axis=1)
            shifted_out[:, here] = padded.T[0:heads]
            shares[here, :] = high_low(jnp.exp2(last - cumulative) * step[here])
            reach_out[here, :] = high_low(jnp.exp2(cumulative))
        befores.append(before)
        zero_rows = jnp.zeros((HALO - chunks, heads), F32)
        shares[length:, :] = high_low(jnp.exp2(jnp.concatenate(totals + [zero_rows], axis=0)))
        zero_rows = jnp.zeros((HALO - chunks - 1, heads), F32)
        reach_out[length:, :] = high_low(jnp.exp2(jnp.concatenate(befores + [zero_rows], axis=0)))
        for c in range(chunks):
            start = c * CHUNK
            here = slice(start, start + CHUNK)
            in_part = filtered(side_taps, start, CHUNK, slice(0, state))
            b_out[here] = in_part
            turned[:, here] = in_part.astype(F32).T.astype(BF16)
            c_out[here] = filtered(side_taps, start, CHUNK, slice(state, 2 * state))

    buffer[...] = dot(extended[...], wide[...]).astype(BF16).astype(F32)
    wide_shares[...] = dot(shares[...], spread[...])
    sub = 64
    running[...] = jnp.zeros_like(running)
    for c in range(chunks):
        here = slice(c * CHUNK, (c + 1) * CHUNK)
        for lane in range(0, width, 256):
            lanes = slice(lane, lane + 256)
            weighted = []
            for start in range(c * CHUNK, (c + 1) * CHUNK, sub):
                piece = filtered(taps, start, sub, lanes)
                x_out[start : start + sub, lanes] = piece
                weighted.append(
                    (piece.astype(F32) * wide_shares[start : start + sub, lanes]).astype(BF16)
                )
            states = dot(turned[:, here], jnp.concatenate(weighted, axis=0))
            entering = running[:, lanes]
            local_out[c, :, lanes] = entering.astype(BF16)
            total = wide_shares[length + c : length + c + 1, lanes]
            running[:, lanes] = total * entering + states
    state_out[0:state, :] = running[...].astype(BF16)
    through = wide_shares[length : length + 1, :]
    for c in range(1, chunks):
        through = through * wide_shares[length + c : length + c + 1, :]
    high = through.astype(BF16)
    low = (through - high.astype(F32)).astype(BF16)
    tail = jnp.concatenate(
        [high.astype(F32), low.astype(F32), jnp.zeros((HALO - 2, width), F32)], axis=0
    )
    state_out[state:, :] = tail.astype(BF16)


def mid_kernel(normed, gate_weight, x, b, c_rows, cumulative, shifted, skip, y_out, gate_out, scores):
    step_index = pl.program_id(0)
    length = x.shape[0]
    chunks = length // CHUNK
    heads_here = cumulative.shape[1]
    head_dim = x.shape[1] // heads_here
    row = lax.broadcasted_iota(jnp.int32, (CHUNK, CHUNK), 0)
    column = lax.broadcasted_iota(jnp.int32, (CHUNK, CHUNK), 1)
    causal = row >= column
    lane = lax.broadcasted_iota(jnp.int32, (CHUNK, 2 * head_dim), 1)

    @pl.when(step_index == 0)
    def _():
        for c in range(chunks):
            here = slice(c * CHUNK, (c + 1) * CHUNK)
            scores[here, :] = lax.dot_general(
                c_rows[here, :], b[here, :], (((1,), (1,)), ((), ())), preferred_element_type=F32
            )

    gate_out[...] = dot(normed[...], gate_weight[...]).astype(BF16)
    for c in range(chunks):
        here = slice(c * CHUNK, (c + 1) * CHUNK)
        score = scores[here, :]
        for pair in range(heads_here // 2):
            lanes = slice(2 * pair * head_dim, (2 * pair + 2) * head_dim)
            parts = []
            for h in (2 * pair, 2 * pair + 1):
                gap = cumulative[here, h : h + 1] - shifted[h : h + 1, here]
                parts.append((score * jnp.exp2(jnp.where(causal, gap, -jnp.inf))).astype(BF16))
            values = x[here, lanes]
            zero = jnp.zeros_like(values)
            stacked = jnp.concatenate(
                [jnp.where(lane < head_dim, values, zero), jnp.where(lane < head_dim, zero, values)],
                axis=0,
            )
            within = dot(jnp.concatenate(parts, axis=1), stacked)
            y_out[here, lanes] = within + skip[:, lanes] * values.astype(F32)


def finish_kernel(
    pieces,
    info,
    rows,
    y,
    gate,
    c_rows,
    reach,
    reach_tail,
    local,
    entering,
    gain,
    spread,
    *rest,
):
    weights = rest[:pieces]
    sent_out, base_out, normed = rest[pieces:]
    reverse = info[1]
    inner = y.shape[1]
    width = weights[0].shape[0]
    tail = dot(reach_tail[...], spread[...])
    pick = lax.broadcasted_iota(jnp.int32, (HALO, 1), 0) == info[0]
    before = jnp.sum(jnp.where(pick, tail, 0.0), axis=0, keepdims=True)
    squares = jnp.zeros((CHUNK, 1), F32)
    gated = []
    block = 256
    for start in range(0, inner, block):
        lanes = slice(start, start + block)
        full = (local[:, lanes].astype(F32) + before[:, lanes] * entering[:, lanes].astype(F32)).astype(BF16)
        carried = dot(c_rows[...], full) * dot(reach[...], spread[:, lanes])
        part = (y[:, lanes] + carried) * silu(gate[:, lanes].astype(F32))
        squares = squares + jnp.sum(part * part, axis=-1, keepdims=True)
        gated.append(part)
    inverse_rms = lax.rsqrt(squares * (1.0 / inner) + EPSILON)
    turn = order_matrix(CHUNK, reverse)
    for index, start in enumerate(range(0, inner, block)):
        lanes = slice(start, start + block)
        piece = (gated[index] * inverse_rms * gain[:, lanes]).astype(BF16)
        piece = dot(turn, piece).astype(BF16)
        if width == block:
            normed[index] = piece
        else:
            normed[0, :, lanes] = piece
    total = None
    for p in range(pieces):
        term = dot(normed[info[2 + p]], weights[p][...])
        total = term if total is None else total + term
    sent_out[...] = total.astype(BF16)
    base_out[...] = rows[...].astype(F32) + total


def whole_block(shape):
    return pl.BlockSpec(shape, lambda *_: (0,) * len(shape))


def prep(info, rows, halo, gain, main, side, conv, bias, decay, spread, inner, state):
    length, features = rows.shape
    heads = bias.shape[1]
    steps = inner // WIDTH
    heads_here = heads // steps
    chunks = length // CHUNK
    margin = conv.shape[1]
    side_taps = conv[0, :, inner:]
    grid_spec = pltpu.PrefetchScalarGridSpec(
        num_scalar_prefetch=1,
        grid=(steps,),
        in_specs=[
            whole_block((length, features)),
            whole_block((HALO, features)),
            whole_block((1, features)),
            pl.BlockSpec((None, features, WIDTH), lambda j, _: (0, 0, steps + j)),
            pl.BlockSpec((None, features, side.shape[2]), lambda j, _: (0, 0, 0)),
            pl.BlockSpec((None, margin, WIDTH), lambda j, _: (0, 0, j)),
            whole_block(side_taps.shape),
            whole_block((1, heads)),
            whole_block((1, heads)),
            pl.BlockSpec((2 * heads, WIDTH), lambda j, _: (0, j)),
        ],
        out_specs=[
            whole_block((length, features)),
            pl.BlockSpec((length, WIDTH), lambda j, _: (0, j)),
            whole_block((length, state)),
            whole_block((length, state)),
            whole_block((steps, length, heads_here)),
            whole_block((heads, length)),
            whole_block((length + HALO, 2 * heads)),
            pl.BlockSpec((chunks, state, WIDTH), lambda j, _: (0, 0, j)),
            pl.BlockSpec((state + HALO, WIDTH), lambda j, _: (0, j)),
        ],
        scratch_shapes=[
            pltpu.VMEM((length + HALO, features), BF16),
            pltpu.VMEM((length + HALO, WIDTH), F32),
            pltpu.VMEM((state, length), BF16),
            pltpu.VMEM((length + HALO, 2 * heads), BF16),
            pltpu.VMEM((length + HALO, WIDTH), F32),
            pltpu.VMEM((state, WIDTH), F32),
        ],
    )
    shape = jax.ShapeDtypeStruct
    return pl.pallas_call(
        prep_kernel,
        grid_spec=grid_spec,
        out_shape=[
            shape((length, features), BF16),
            shape((length, inner), BF16),
            shape((length, state), BF16),
            shape((length, state), BF16),
            shape((steps, length, heads_here), F32),
            shape((heads, length), F32),
            shape((length + HALO, 2 * heads), BF16),
            shape((chunks, state, inner), BF16),
            shape((state + HALO, inner), BF16),
        ],
        compiler_params=pltpu.CompilerParams(
            vmem_limit_bytes=40 * 2**20, dimension_semantics=("arbitrary",)
        ),
        cost_estimate=pl.CostEstimate(
            flops=2 * length * features * inner, bytes_accessed=12 * 2**20, transcendentals=0
        ),
        name="prep",
    )(info, rows, halo, gain, main, side, conv, side_taps, bias, decay, spread)


def mid(normed, main, x, b, c_rows, cumulative, shifted, skip, inner):
    length, features = normed.shape
    state = b.shape[1]
    steps = inner // WIDTH
    heads_here = cumulative.shape[2]
    return pl.pallas_call(
        mid_kernel,
        grid=(steps,),
        in_specs=[
            whole_block((length, features)),
            pl.BlockSpec((None, features, WIDTH), lambda j: (0, 0, j)),
            pl.BlockSpec((length, WIDTH), lambda j: (0, j)),
            whole_block((length, state)),
            whole_block((length, state)),
            pl.BlockSpec((None, length, heads_here), lambda j: (j, 0, 0)),
            pl.BlockSpec((heads_here, length), lambda j: (j, 0)),
            pl.BlockSpec((1, WIDTH), lambda j: (0, j)),
        ],
        out_specs=[
            pl.BlockSpec((length, WIDTH), lambda j: (0, j)),
            pl.BlockSpec((length, WIDTH), lambda j: (0, j)),
        ],
        out_shape=[
            jax.ShapeDtypeStruct((length, inner), F32),
            jax.ShapeDtypeStruct((length, inner), BF16),
        ],
        scratch_shapes=[pltpu.VMEM((length, CHUNK), F32)],
        compiler_params=pltpu.CompilerParams(
            vmem_limit_bytes=40 * 2**20, dimension_semantics=("arbitrary",)
        ),
        cost_estimate=pl.CostEstimate(
            flops=2 * length * features * inner, bytes_accessed=12 * 2**20, transcendentals=0
        ),
        name="mid",
    )(normed, main, x, b, c_rows, cumulative, shifted, skip)


def finish(info, rows, index, y, gate, c_rows, reach, local, entering, gain, spread, weights):
    features = rows.shape[1]
    length, inner = y.shape
    state = c_rows.shape[1]
    count = len(weights)
    width = weights[0].shape[0]
    reach_width = reach.shape[1]
    tail = length // HALO
    grid_spec = pltpu.PrefetchScalarGridSpec(
        num_scalar_prefetch=1,
        grid=(1,),
        in_specs=[
            pl.BlockSpec((CHUNK, features), lambda j, s: (index, 0)),
            pl.BlockSpec((CHUNK, inner), lambda j, s: (s[0], 0)),
            pl.BlockSpec((CHUNK, inner), lambda j, s: (s[0], 0)),
            pl.BlockSpec((CHUNK, state), lambda j, s: (s[0], 0)),
            pl.BlockSpec((CHUNK, reach_width), lambda j, s: (s[0], 0)),
            pl.BlockSpec((HALO, reach_width), lambda j, s: (tail, 0)),
            pl.BlockSpec((None, state, inner), lambda j, s: (s[0], 0, 0)),
            whole_block((state, inner)),
            whole_block((1, inner)),
            whole_block(spread.shape),
        ]
        + [whole_block(weight.shape) for weight in weights],
        out_specs=[whole_block((CHUNK, features)), whole_block((CHUNK, features))],
        scratch_shapes=[pltpu.VMEM((inner // width, CHUNK, width), BF16)],
    )
    return pl.pallas_call(
        functools.partial(finish_kernel, count),
        grid_spec=grid_spec,
        out_shape=[
            jax.ShapeDtypeStruct((CHUNK, features), BF16),
            jax.ShapeDtypeStruct((CHUNK, features), F32),
        ],
        compiler_params=pltpu.CompilerParams(
            vmem_limit_bytes=40 * 2**20, dimension_semantics=("arbitrary",)
        ),
        cost_estimate=pl.CostEstimate(
            flops=2 * CHUNK * features * inner, bytes_accessed=8 * 2**20, transcendentals=0
        ),
        name="finish",
    )(info, rows, y, gate, c_rows, reach, reach, local, entering, gain, spread, *weights)


def gathered_pieces(shard, seq_index, seq_count):
    if seq_count != 8:
        return [lax.all_gather(shard, "seq", axis=0, tiled=True)], [jnp.int32(0)]

    def swap(value, mask):
        return lax.ppermute(value, "seq", [(i, i ^ mask) for i in range(seq_count)])

    half = shard.shape[0] // 2
    across = swap(shard, 2)
    along = swap(shard, 4)
    upper = swap(along[:half], 2)
    lower = swap(across[half:], 4)
    diagonal = jnp.concatenate([upper, lower], axis=0)
    mine = [(shard, 0), (across, 2), (along, 4), (diagonal, 6)]
    pieces = mine + [(swap(piece, 1), mask + 1) for piece, mask in mine]
    return [piece for piece, _ in pieces], [seq_index ^ mask for _, mask in pieces]


def split_state(packed):
    state = packed.shape[0] - HALO
    values = packed[:state].astype(F32)
    through = packed[state : state + 1].astype(F32) + packed[state + 1 : state + 2].astype(F32)
    return values, through


def joined_state(values, through):
    high = through.astype(BF16)
    low = (through - high.astype(F32)).astype(BF16)
    rest = jnp.zeros((HALO - 2, through.shape[1]), BF16)
    return jnp.concatenate([values.astype(BF16), high, low, rest], axis=0)


def after(earlier, later):
    return later[1] * earlier[0] + later[0], earlier[1] * later[1]


def chosen(condition, first, second):
    return tuple(jnp.where(condition, a, b) for a, b in zip(first, second))


def entering_state(packed, sections, seq_index, seq_count, reverse):
    bits = seq_count.bit_length() - 1
    section_count = lax.axis_size("section")

    def swap(value, mask):
        pairs = [
            (i * section_count + s, (i ^ mask) * section_count + s)
            for s in sections
            for i in range(seq_count)
        ]
        return lax.ppermute(value, ("seq", "section"), pairs)

    def forward(value, mask, low_bit):
        pairs = []
        for s in sections:
            for i in range(seq_count):
                later = (i ^ mask) >> low_bit > i >> low_bit
                if later == (s % 2 == 0):
                    pairs.append((i * section_count + s, (i ^ mask) * section_count + s))
        return lax.ppermute(value, ("seq", "section"), pairs)

    inner = packed.shape[1]
    half = inner // 2
    partner = swap(packed, 1)
    upper = seq_index % 2 == 1
    first = jnp.logical_xor(upper, reverse) == 0
    mine_here = jnp.where(upper, packed[:, half:], packed[:, :half])
    other_here = jnp.where(upper, partner[:, half:], partner[:, :half])
    mine = split_state(mine_here)
    other = split_state(other_here)
    total = after(chosen(first, mine, other), chosen(first, other, mine))
    identity = (jnp.zeros_like(total[0]), jnp.ones_like(total[1]))
    entering = identity
    bit = 1
    while bit < bits:
        group = min(2, bits - bit)
        last = bit + group == bits
        packed_total = joined_state(*total)
        members = {}
        for code in range(1, 2**group):
            mask = code << bit
            send = forward(packed_total, mask, bit) if last else swap(packed_total, mask)
            members[code] = split_state(send)
        position = (seq_index >> bit) % 2**group
        rank = jnp.where(reverse, 2**group - 1 - position, position)
        before = identity
        whole = identity
        for place in range(2**group):
            value = total
            for code in range(1, 2**group):
                value = chosen((rank ^ code) == place, members[code], value)
            if place < 2**group - 1:
                step = after(before, value)
                before = chosen(place < rank, step, before)
            if not last:
                whole = after(whole, value)
        entering = after(before, entering) if bit > 1 else before
        if not last:
            total = whole
        bit += group
    return entering[0], packed, partner, upper, first, swap


def device_state(entering_half, packed, partner, upper, first, swap):
    half_state = entering_half.astype(BF16)
    other_half = swap(half_state, 1)
    left = jnp.where(upper, other_half, half_state)
    right = jnp.where(upper, half_state, other_half)
    full = jnp.concatenate([left, right], axis=1)
    values, through = split_state(partner)
    moved = (through * full.astype(F32) + values).astype(BF16)
    return jnp.where(first, full, moved)


def per_device(
    tokens,
    input_gain,
    main_weight,
    side_weight,
    conv_kernel,
    step_bias,
    decay_rate,
    skip_gain,
    output_gain,
    output_weight,
):
    length, features = tokens.shape
    inner = main_weight.shape[2] // 2
    heads = decay_rate.shape[1]
    state = (side_weight.shape[2] - heads) // 2
    head_dim = inner // heads
    chunks = length // CHUNK
    seq_count = lax.axis_size("seq")
    section_count = lax.axis_size("section")
    section_index = lax.axis_index("section")
    seq_index = lax.axis_index("seq")
    reverse = section_index % 2
    layer_here = section_index // 2
    weights, owners = gathered_pieces(output_weight[0], seq_index, seq_count)
    expand = np.repeat(np.eye(heads, dtype=np.float32), head_dim, axis=1)
    spread = jnp.asarray(np.concatenate([expand, expand], axis=0), BF16)
    skip_row = jnp.repeat(skip_gain, head_dim, axis=1)
    info = reverse.astype(jnp.int32).reshape(1)
    order = [chunks - 1, 0] + list(range(1, chunks - 1))

    def edges(first_rows, last_rows, sections):
        pairs = []
        for s in sections:
            for i in range(seq_count):
                target = i + 1 if s % 2 == 0 else i - 1
                if 0 <= target < seq_count:
                    pairs.append((i * section_count + s, target * section_count + s))
        value = jnp.where(reverse == 1, first_rows, last_rows)
        return lax.ppermute(value, ("seq", "section"), pairs)

    rounds = section_count // 2
    current = tokens
    halo = edges(tokens[:HALO], tokens[length - HALO :], (0, 1))
    finished = None
    for round_index in range(rounds):
        active = (2 * round_index, 2 * round_index + 1)
        normed, x, b, c_rows, cumulative, shifted, reach, local, packed = prep(
            info,
            current,
            halo,
            input_gain,
            main_weight,
            side_weight,
            conv_kernel,
            step_bias,
            decay_rate,
            spread,
            inner,
            state,
        )
        y, gate = mid(normed, main_weight, x, b, c_rows, cumulative, shifted, skip_row, inner)
        parts = entering_state(packed, active, seq_index, seq_count, reverse == 1)
        entering = device_state(*parts)
        here = layer_here == round_index
        sections = [active]
        done_rows = [None] * chunks
        next_rows = [None] * chunks
        last_round = round_index + 1 == rounds
        for index in order:
            chunk = jnp.where(reverse == 1, chunks - 1 - index, index).astype(jnp.int32)
            chunk_info = jnp.stack([chunk, info[0]] + [owner.astype(jnp.int32) for owner in owners])
            sent, base = finish(
                chunk_info, current, index, y, gate, c_rows, reach, local, entering,
                output_gain, spread, weights,
            )
            low, high = active
            other = lax.ppermute(sent, "section", [(low, high), (high, low)])
            layer_rows = (base + other.astype(F32)).astype(BF16)
            done_rows[index] = layer_rows
            if not last_round:
                near = lax.ppermute(layer_rows, "section", [(high, high + 1)])
                far = lax.ppermute(near, "section", [(high + 1, high + 2)])
                next_rows[index] = jnp.where(section_index == high + 2, far, near)
        result = jnp.concatenate(done_rows, axis=0)
        finished = result if finished is None else jnp.where(here, result, finished)
        if not last_round:
            next_active = (active[0] + 2, active[1] + 2)
            halo = edges(next_rows[0][:HALO], next_rows[chunks - 1][CHUNK - HALO :], next_active)
            current = jnp.concatenate(next_rows, axis=0)
    return finished[None]


def solution(mesh):
    placed = (
        P("seq", None),
        P("section", None),
        P("section", None, None),
        P("section", None, None),
        P("section", None, None),
        P("section", None),
        P("section", None),
        P("section", None),
        P("section", None),
        P("section", "seq", None),
    )
    return jax.shard_map(
        per_device, mesh=mesh, in_specs=placed, out_specs=P("section", "seq", None), check_vma=False
    )
```

```python
import functools

import jax
import jax.numpy as jnp
import numpy as np
from jax import lax
from jax.experimental import pallas as pl
from jax.experimental.pallas import tpu as pltpu
from jax.sharding import PartitionSpec as P

EPSILON = 1e-05
CHUNK = 128
WIDTH = 512
HALO = 16
LIMIT = 36 * 2**20
SMALL = 8 * 2**20
SKEW = 2
REVERSE, UPPER, FIRST, RANKS = 0, 1, 2, 3
LOG2E = 1.4426950408889634
F32 = jnp.float32
BF16 = jnp.bfloat16


def silu(value):
    half = 0.5 * value
    return half + half * jnp.tanh(half)


def dot(left, right):
    return jnp.dot(left, right, preferred_element_type=F32)


def order_matrix(size, reverse):
    row = lax.broadcasted_iota(jnp.int32, (size, size), 0)
    column = lax.broadcasted_iota(jnp.int32, (size, size), 1)
    target = jnp.where(reverse == 1, size - 1 - row, row)
    return jnp.where(column == target, 1.0, 0.0).astype(BF16)


def high_low(value):
    high = value.astype(BF16)
    low = (value - high.astype(F32)).astype(BF16)
    return jnp.concatenate([high, low], axis=1)


def norm_block(values, gain_row):
    widened = values.astype(F32)
    inverse_rms = lax.rsqrt(jnp.mean(widened * widened, axis=-1, keepdims=True) + EPSILON)
    return (widened * inverse_rms * gain_row).astype(BF16)


def prep_kernel(
    info,
    rows,
    halo,
    gain,
    wide,
    side_weight,
    taps,
    side_taps,
    bias,
    decay,
    spread,
    normed_out,
    x_out,
    b_out,
    c_out,
    cum_out,
    shifted_out,
    reach_out,
    local_out,
    state_out,
    extended,
    buffer,
    turned,
    shares,
    wide_shares,
    running,
):
    step_index = pl.program_id(0)
    reverse = info[REVERSE]
    length = rows.shape[0]
    heads = bias.shape[1]
    state = b_out.shape[1]
    chunks = length // CHUNK
    margin = taps.shape[0] - 1
    width = wide.shape[1]

    def filtered(kernel, start, size, lanes):
        total = None
        for k in range(margin + 1):
            part = buffer[HALO - margin + k + start : HALO - margin + k + start + size, lanes]
            term = kernel[k : k + 1, lanes] * part
            total = term if total is None else total + term
        return silu(total).astype(BF16)

    @pl.when(step_index == 0)
    def _():
        turn = order_matrix(2 * CHUNK, reverse)
        small_turn = order_matrix(HALO, reverse)
        edge = norm_block(halo[...], gain[...])
        extended[0:HALO] = dot(small_turn, edge).astype(BF16)
        pairs = length // (2 * CHUNK)
        for pair in range(pairs):
            source = jnp.where(reverse == 1, pairs - 1 - pair, pair) * (2 * CHUNK)
            source = pl.multiple_of(source, 2 * CHUNK)
            piece = norm_block(rows[pl.ds(source, 2 * CHUNK), :], gain[...])
            start = HALO + pair * 2 * CHUNK
            extended[start : start + 2 * CHUNK] = dot(turn, piece).astype(BF16)
        normed_out[...] = extended[HALO:]
        side = dot(extended[...], side_weight[...]).astype(BF16).astype(F32)
        buffer[:, 0 : 2 * state] = side[:, 0 : 2 * state]
        raw = side[HALO:, 2 * state :] + bias[...]
        step = jnp.maximum(raw, 0.0) + jnp.log1p(jnp.exp(-jnp.abs(raw)))
        change = step * (decay[...] * (-LOG2E))
        row = lax.broadcasted_iota(jnp.int32, (CHUNK, CHUNK), 0)
        column = lax.broadcasted_iota(jnp.int32, (CHUNK, CHUNK), 1)
        triangle = jnp.where(row >= column, 1.0, 0.0).astype(F32)
        before = jnp.zeros((1, heads), F32)
        totals = []
        befores = []
        for c in range(chunks):
            here = slice(c * CHUNK, (c + 1) * CHUNK)
            cumulative = jnp.dot(
                triangle, change[here], preferred_element_type=F32, precision=lax.Precision.HIGHEST
            )
            last = cumulative[CHUNK - 1 :, :]
            befores.append(before)
            totals.append(last)
            before = before + last
            moved = cumulative - jnp.log2(step[here])
            blank = jnp.zeros((CHUNK, 128 - 2 * heads), F32)
            flipped = jnp.concatenate([cumulative, moved, blank], axis=1).T
            cum_out[:, here] = flipped[0:heads]
            shifted_out[:, here] = flipped[heads : 2 * heads]
            shares[here, :] = high_low(jnp.exp2(last - cumulative) * step[here])
            reach_out[here, :] = high_low(jnp.exp2(cumulative))
        befores.append(before)
        zero_rows = jnp.zeros((HALO - chunks, heads), F32)
        shares[length:, :] = high_low(jnp.exp2(jnp.concatenate(totals + [zero_rows], axis=0)))
        zero_rows = jnp.zeros((HALO - chunks - 1, heads), F32)
        reach_out[length:, :] = high_low(jnp.exp2(jnp.concatenate(befores + [zero_rows], axis=0)))
        for c in range(chunks):
            start = c * CHUNK
            here = slice(start, start + CHUNK)
            in_part = filtered(side_taps, start, CHUNK, slice(0, state))
            b_out[here] = in_part
            turned[:, here] = in_part.astype(F32).T.astype(BF16)
            c_out[here] = filtered(side_taps, start, CHUNK, slice(state, 2 * state))

    buffer[...] = dot(extended[...], wide[...]).astype(BF16).astype(F32)
    wide_shares[...] = dot(shares[...], spread[...])
    sub = 64
    running[...] = jnp.zeros_like(running)
    for c in range(chunks):
        here = slice(c * CHUNK, (c + 1) * CHUNK)
        for lane in range(0, width, 256):
            lanes = slice(lane, lane + 256)
            weighted = []
            for start in range(c * CHUNK, (c + 1) * CHUNK, sub):
                piece = filtered(taps, start, sub, lanes)
                x_out[start : start + sub, lanes] = piece
                weighted.append(
                    (piece.astype(F32) * wide_shares[start : start + sub, lanes]).astype(BF16)
                )
            states = dot(turned[:, here], jnp.concatenate(weighted, axis=0))
            entering = running[:, lanes]
            local_out[c, :, lanes] = entering.astype(BF16)
            total = wide_shares[length + c : length + c + 1, lanes]
            running[:, lanes] = total * entering + states
    state_out[0:state, :] = running[...].astype(BF16)
    through = wide_shares[length : length + 1, :]
    for c in range(1, chunks):
        through = through * wide_shares[length + c : length + c + 1, :]
    high = through.astype(BF16)
    low = (through - high.astype(F32)).astype(BF16)
    tail = jnp.concatenate(
        [high.astype(F32), low.astype(F32), jnp.zeros((HALO - 2, width), F32)], axis=0
    )
    state_out[state:, :] = tail.astype(BF16)


def mid_kernel(normed, gate_weight, x, b, c_rows, cumulative, shifted, skip, y_out, gate_out, scores):
    step_index = pl.program_id(0)
    length = x.shape[0]
    chunks = length // CHUNK
    heads_here = cumulative.shape[0]
    head_dim = x.shape[1] // heads_here
    row = lax.broadcasted_iota(jnp.int32, (CHUNK, CHUNK), 0)
    column = lax.broadcasted_iota(jnp.int32, (CHUNK, CHUNK), 1)
    causal = row >= column
    lane = lax.broadcasted_iota(jnp.int32, (CHUNK, 2 * head_dim), 1)

    @pl.when(step_index == 0)
    def _():
        for c in range(chunks):
            here = slice(c * CHUNK, (c + 1) * CHUNK)
            scores[here, :] = lax.dot_general(
                c_rows[here, :], b[here, :], (((1,), (1,)), ((), ())), preferred_element_type=F32
            )

    gate_out[...] = dot(normed[...], gate_weight[...]).astype(BF16)
    for c in range(chunks):
        here = slice(c * CHUNK, (c + 1) * CHUNK)
        score = scores[here, :]
        blank = jnp.zeros((128 - heads_here, CHUNK), F32)
        columns = jnp.concatenate([cumulative[:, here], blank], axis=0).T
        for pair in range(heads_here // 2):
            lanes = slice(2 * pair * head_dim, (2 * pair + 2) * head_dim)
            parts = []
            for h in (2 * pair, 2 * pair + 1):
                gap = columns[:, h : h + 1] - shifted[h : h + 1, here]
                parts.append((score * jnp.exp2(jnp.where(causal, gap, -jnp.inf))).astype(BF16))
            values = x[here, lanes]
            zero = jnp.zeros_like(values)
            stacked = jnp.concatenate(
                [jnp.where(lane < head_dim, values, zero), jnp.where(lane < head_dim, zero, values)],
                axis=0,
            )
            within = dot(jnp.concatenate(parts, axis=1), stacked)
            y_out[here, lanes] = within + skip[:, lanes] * values.astype(F32)


def finish_kernel(
    count,
    mode,
    info,
    rows,
    y,
    gate,
    c_rows,
    reach,
    reach_tail,
    local,
    mine,
    other,
    partner,
    gain,
    spread,
    weight_far,
    *rest,
):
    outs = rest[:-4]
    normed, entering, weight, arrived = rest[-4:]
    step_index = pl.program_id(0)
    steps = pl.num_programs(0)
    reverse = info[REVERSE]
    size, inner = y.shape
    parts = size // CHUNK
    state = mine.shape[0]
    fetch = pltpu.make_async_copy(weight_far, weight, arrived)

    @pl.when(step_index == 0)
    def _():
        fetch.start()
        half = inner // 2
        upper = info[UPPER] == 1
        first = info[FIRST] == 1
        for start in range(0, inner, 256):
            lanes = slice(start, start + 256)
            inside = slice(start % half, start % half + 256)
            pair = (other, mine) if start < half else (mine, other)
            full = jnp.where(upper, pair[0][:, inside], pair[1][:, inside])
            tail = partner[state:, lanes].astype(F32)
            through = tail[0:1] + tail[1:2]
            moved = (through * full.astype(F32) + partner[:state, lanes].astype(F32)).astype(BF16)
            entering[:, lanes] = jnp.where(first, full, moved)

    position = jnp.where(reverse == 1, steps - 1 - step_index, step_index)
    tail = dot(reach_tail[...], spread[...])
    index_row = lax.broadcasted_iota(jnp.int32, (HALO, 1), 0)
    turn = order_matrix(size, reverse)
    block = 256
    befores = [
        jnp.sum(jnp.where(index_row == position * parts + p, tail, 0.0), axis=0, keepdims=True)
        for p in range(parts)
    ]
    squares = [jnp.zeros((CHUNK, 1), F32) for _ in range(parts)]
    gated = {}
    for start in range(0, inner, block):
        lanes = slice(start, start + block)
        for p in range(parts):
            here = slice(p * CHUNK, (p + 1) * CHUNK)
            full = local[p, :, lanes].astype(F32) + befores[p][:, lanes] * entering[:, lanes].astype(F32)
            carried = dot(c_rows[here, :], full.astype(BF16)) * dot(reach[here, :], spread[:, lanes])
            part = (y[here, lanes] + carried) * silu(gate[here, lanes].astype(F32))
            squares[p] = squares[p] + jnp.sum(part * part, axis=-1, keepdims=True)
            gated[p, start] = part
    inverse_rms = [lax.rsqrt(total * (1.0 / inner) + EPSILON) for total in squares]
    for start in range(0, inner, block):
        lanes = slice(start, start + block)
        piece = jnp.concatenate(
            [(gated[p, start] * inverse_rms[p] * gain[:, lanes]).astype(BF16) for p in range(parts)],
            axis=0,
        )
        piece = dot(turn, piece).astype(BF16)
        normed[:, lanes] = piece

    @pl.when(step_index == 0)
    def _():
        fetch.wait()

    total = dot(normed[...], weight[...])
    base = rows[...].astype(F32) + total
    if mode[0] == "exchange":
        earlier = outs[:count]
        sent = outs[count : 2 * count]
        outs[2 * count][...] = base
        for k in range(count):

            @pl.when(step_index == k // parts)
            def _(k=k):
                start = k % parts * CHUNK
                mine_now = total[start : start + CHUNK].astype(BF16)
                sent[k][...] = jnp.where(info[mode[1]] == 1, earlier[k][...], mine_now)

        return
    order, skew, place_slot = mode
    place = info[place_slot]

    @pl.when(step_index == 0)
    def _():
        for out in outs:
            out[...] = jnp.zeros_like(out)

    for k, index in enumerate(order):
        start = index % parts * CHUNK
        here = slice(start, start + CHUNK)

        @pl.when((step_index == index // parts) & (place == 0))
        def _(k=k, here=here):
            outs[k][...] = total[here].astype(outs[k].dtype)

        @pl.when((step_index == index // parts) & (place == 1))
        def _(k=k, here=here):
            outs[k + skew][...] = base[here]


def kept(shape, dtype):
    return pltpu.VMEM(shape, dtype)


def near(*values):
    return tuple(pltpu.with_memory_space_constraint(v, pltpu.VMEM) for v in values)


def far(value):
    return pltpu.with_memory_space_constraint(value, pltpu.HBM)


def whole_block(shape):
    return pl.BlockSpec(shape, lambda *_: (0,) * len(shape))


def prep(info, rows, halo, gain, main, side, conv, bias, decay, spread, inner, state):
    length, features = rows.shape
    heads = bias.shape[1]
    steps = inner // WIDTH
    chunks = length // CHUNK
    margin = conv.shape[1]
    side_taps = conv[0, :, inner:]
    grid_spec = pltpu.PrefetchScalarGridSpec(
        num_scalar_prefetch=1,
        grid=(steps,),
        in_specs=[
            whole_block((length, features)),
            whole_block((HALO, features)),
            whole_block((1, features)),
            pl.BlockSpec((None, features, WIDTH), lambda j, _: (0, 0, steps + j)),
            pl.BlockSpec((None, features, side.shape[2]), lambda j, _: (0, 0, 0)),
            pl.BlockSpec((None, margin, WIDTH), lambda j, _: (0, 0, j)),
            whole_block(side_taps.shape),
            whole_block((1, heads)),
            whole_block((1, heads)),
            pl.BlockSpec((2 * heads, WIDTH), lambda j, _: (0, j)),
        ],
        out_specs=[
            whole_block((length, features)),
            pl.BlockSpec((length, WIDTH), lambda j, _: (0, j)),
            whole_block((length, state)),
            whole_block((length, state)),
            whole_block((heads, length)),
            whole_block((heads, length)),
            whole_block((length + HALO, 2 * heads)),
            pl.BlockSpec((chunks, state, WIDTH), lambda j, _: (0, 0, j)),
            pl.BlockSpec((state + HALO, WIDTH), lambda j, _: (0, j)),
        ],
        scratch_shapes=[
            pltpu.VMEM((length + HALO, features), BF16),
            pltpu.VMEM((length + HALO, WIDTH), F32),
            pltpu.VMEM((state, length), BF16),
            pltpu.VMEM((length + HALO, 2 * heads), BF16),
            pltpu.VMEM((length + HALO, WIDTH), F32),
            pltpu.VMEM((state, WIDTH), F32),
        ],
    )
    shape = jax.ShapeDtypeStruct
    return pl.pallas_call(
        prep_kernel,
        grid_spec=grid_spec,
        out_shape=[
            kept((length, features), BF16),
            kept((length, inner), BF16),
            kept((length, state), BF16),
            kept((length, state), BF16),
            kept((heads, length), F32),
            kept((heads, length), F32),
            kept((length + HALO, 2 * heads), BF16),
            kept((chunks, state, inner), BF16),
            shape((state + HALO, inner), BF16),
        ],
        compiler_params=pltpu.CompilerParams(
            vmem_limit_bytes=LIMIT, dimension_semantics=("arbitrary",)
        ),
        cost_estimate=pl.CostEstimate(
            flops=2 * length * features * inner, bytes_accessed=12 * 2**20, transcendentals=0
        ),
        name="prep",
    )(info, rows, halo, gain, far(main), side, conv, side_taps, bias, decay, spread)


def mid(normed, main, x, b, c_rows, cumulative, shifted, skip, inner):
    length, features = normed.shape
    state = b.shape[1]
    steps = inner // WIDTH
    heads_here = cumulative.shape[0] // steps
    return pl.pallas_call(
        mid_kernel,
        grid=(steps,),
        in_specs=[
            whole_block((length, features)),
            pl.BlockSpec((None, features, WIDTH), lambda j: (0, 0, j)),
            pl.BlockSpec((length, WIDTH), lambda j: (0, j)),
            whole_block((length, state)),
            whole_block((length, state)),
            pl.BlockSpec((heads_here, length), lambda j: (j, 0)),
            pl.BlockSpec((heads_here, length), lambda j: (j, 0)),
            pl.BlockSpec((1, WIDTH), lambda j: (0, j)),
        ],
        out_specs=[
            pl.BlockSpec((length, WIDTH), lambda j: (0, j)),
            pl.BlockSpec((length, WIDTH), lambda j: (0, j)),
        ],
        out_shape=[
            kept((length, inner), F32),
            kept((length, inner), BF16),
        ],
        scratch_shapes=[pltpu.VMEM((length, CHUNK), F32)],
        compiler_params=pltpu.CompilerParams(
            vmem_limit_bytes=LIMIT, dimension_semantics=("arbitrary",)
        ),
        cost_estimate=pl.CostEstimate(
            flops=2 * length * features * inner, bytes_accessed=12 * 2**20, transcendentals=0
        ),
        name="mid",
    )(*near(normed), far(main), *near(x, b, c_rows, cumulative, shifted), skip)


def finish(mode, info, rows, y, gate, c_rows, reach, local, state_parts, gain, spread, weight, earlier):
    features = rows.shape[1]
    length, inner = y.shape
    state = c_rows.shape[1]
    mine, other, partner = state_parts
    reach_width = reach.shape[1]
    tail = length // HALO
    size = 2 * CHUNK
    steps = length // size
    chunks = length // CHUNK

    if mode[0] == "exchange":
        out_specs = [whole_block((CHUNK, features))] * chunks
        out_specs = out_specs + [pl.BlockSpec((size, features), lambda j, s: (j, 0))]
        out_shape = [jax.ShapeDtypeStruct((CHUNK, features), BF16)] * chunks
        out_shape = out_shape + [kept((length, features), F32)]
    else:
        skew = mode[1]
        out_specs = [whole_block((CHUNK, features))] * (chunks + skew)
        out_shape = [jax.ShapeDtypeStruct((CHUNK, features), BF16)] * skew
        out_shape = out_shape + [kept((CHUNK, features), F32)] * chunks

    def turned_block(shape):
        def place(j, s):
            return (jnp.where(s[0] == 1, steps - 1 - j, j),) + (0,) * (len(shape) - 1)

        return pl.BlockSpec(shape, place)

    grid_spec = pltpu.PrefetchScalarGridSpec(
        num_scalar_prefetch=1,
        grid=(steps,),
        in_specs=[
            pl.BlockSpec((size, features), lambda j, s: (j, 0)),
            turned_block((size, inner)),
            turned_block((size, inner)),
            turned_block((size, state)),
            turned_block((size, reach_width)),
            pl.BlockSpec((HALO, reach_width), lambda j, s: (tail, 0)),
            turned_block((size // CHUNK, state, inner)),
            whole_block(mine.shape),
            whole_block(other.shape),
            whole_block(partner.shape),
            whole_block((1, inner)),
            whole_block(spread.shape),
            pl.BlockSpec(memory_space=pl.ANY),
        ]
        + [whole_block(value.shape) for value in earlier],
        out_specs=out_specs,
        scratch_shapes=[
            pltpu.VMEM((size, inner), BF16),
            pltpu.VMEM((state, inner), BF16),
            pltpu.VMEM(weight.shape, BF16),
            pltpu.SemaphoreType.DMA,
        ],
    )
    return pl.pallas_call(
        functools.partial(finish_kernel, chunks, mode),
        grid_spec=grid_spec,
        out_shape=out_shape,
        compiler_params=pltpu.CompilerParams(
            vmem_limit_bytes=LIMIT, dimension_semantics=("arbitrary",)
        ),
        cost_estimate=pl.CostEstimate(
            flops=2 * length * features * inner, bytes_accessed=16 * 2**20, transcendentals=0
        ),
        name="finish",
    )(
        info, rows, *near(y, gate, c_rows, reach, reach, local), mine, other, partner,
        gain, spread, far(weight), *earlier,
    )


def split_state(packed):
    state = packed.shape[0] - HALO
    values = packed[:state].astype(F32)
    tail = packed[state:].astype(F32)
    return values, tail[0:1] + tail[1:2]


def joined_state(values, through):
    high = through.astype(BF16)
    low = (through - high.astype(F32)).astype(BF16)
    rest = jnp.zeros((HALO - 2, through.shape[1]), F32)
    tail = jnp.concatenate([high.astype(F32), low.astype(F32), rest], axis=0)
    return values.astype(BF16), tail.astype(BF16)


def after(earlier, later):
    return later[1] * earlier[0] + later[0], earlier[1] * later[1]


def chosen(condition, first, second):
    return tuple(jnp.where(condition, a, b) for a, b in zip(first, second))


def pair_kernel(info, mine, partner, out):
    half = out.shape[1]
    first = info[FIRST] == 1
    state = out.shape[0] - HALO
    for start in range(0, half, 256):
        place = pl.multiple_of(info[UPPER] * half + start, 256)
        one = split_state(mine[:, pl.ds(place, 256)])
        two = split_state(partner[:, pl.ds(place, 256)])
        total = after(chosen(first, one, two), chosen(first, two, one))
        out[:state, start : start + 256], out[state:, start : start + 256] = joined_state(*total)


def merge_kernel(group, slot, has_entering, last, info, *refs):
    members = refs[: 2**group]
    entering_out = refs[2**group + has_entering]
    rank = info[slot]
    state, half = entering_out.shape
    for start in range(0, half, 256):
        lanes = slice(start, start + 256)
        values = [split_state(member[:, lanes]) for member in members]
        before = (jnp.zeros((state, 256), F32), jnp.ones((1, 256), F32))
        whole = before
        for place in range(2**group):
            value = values[0]
            for code in range(1, 2**group):
                value = chosen((rank ^ code) == place, values[code], value)
            if place < 2**group - 1:
                before = chosen(place < rank, after(before, value), before)
            if not last:
                whole = after(whole, value)
        if has_entering:
            inside = refs[2**group][:, lanes].astype(F32)
            through = jnp.ones((1, 256), F32)
            before = after(before, (inside, through))
        entering_out[:, lanes] = before[0].astype(BF16)
        if not last:
            out = refs[-1]
            out[:state, lanes], out[state:, lanes] = joined_state(*whole)


def small_call(kernel, name, out_shape, info, *operands):
    return pl.pallas_call(
        kernel,
        in_specs=[pl.BlockSpec(memory_space=pltpu.SMEM)] + [whole_block(v.shape) for v in operands],
        out_specs=[whole_block(v.shape) for v in out_shape],
        out_shape=out_shape,
        compiler_params=pltpu.CompilerParams(vmem_limit_bytes=SMALL),
        cost_estimate=pl.CostEstimate(flops=10**6, bytes_accessed=10**6, transcendentals=0),
        name=name,
    )(info, *operands)


def settle_kernel(place, info, base, sent, other, *rest):
    section = info[place]
    rows = (base[...] + other[...].astype(F32)).astype(BF16)
    rows = jnp.where(section == 1, sent[...], rows)
    rest[-1][...] = jnp.where(section == 0, other[...], rows)


def settle(index, place, info, base, sent, other, finished):
    length, features = base.shape
    block = pl.BlockSpec((CHUNK, features), lambda j: (index, 0))
    out_block = pl.BlockSpec((None, CHUNK, features), lambda j: (0, index, 0))
    passed = [] if finished is None else [finished]
    return pl.pallas_call(
        functools.partial(settle_kernel, place),
        grid=(1,),
        in_specs=[pl.BlockSpec(memory_space=pltpu.SMEM), block]
        + [whole_block((CHUNK, features))] * 2
        + [pl.BlockSpec(memory_space=pl.ANY)] * len(passed),
        out_specs=out_block,
        out_shape=jax.ShapeDtypeStruct((1, length, features), BF16),
        input_output_aliases={4: 0} if passed else {},
        compiler_params=pltpu.CompilerParams(vmem_limit_bytes=SMALL),
        cost_estimate=pl.CostEstimate(flops=10**6, bytes_accessed=10**6, transcendentals=0),
        name="settle",
    )(info, base, sent, other, *passed)


def stages_of(seq_count):
    bits = seq_count.bit_length() - 1
    found = []
    bit = 1
    while bit < bits:
        group = min(2, bits - bit)
        found.append((bit, group))
        bit += group
    return found


def entering_state(packed, info, sections, seq_count, meanwhile):
    section_count = lax.axis_size("section")
    stages = stages_of(seq_count)

    def swap(value, mask):
        pairs = [
            (i * section_count + s, (i ^ mask) * section_count + s)
            for s in sections
            for i in range(seq_count)
        ]
        return lax.ppermute(value, ("seq", "section"), pairs)

    def forward(value, mask, low_bit):
        pairs = []
        for s in sections:
            for i in range(seq_count):
                later = (i ^ mask) >> low_bit > i >> low_bit
                if later == (s % 2 == 0):
                    pairs.append((i * section_count + s, (i ^ mask) * section_count + s))
        return lax.ppermute(value, ("seq", "section"), pairs)

    depth, inner = packed.shape
    half = jax.ShapeDtypeStruct((depth, inner // 2), BF16)
    states = jax.ShapeDtypeStruct((depth - HALO, inner // 2), BF16)
    partner = swap(packed, 1)
    (total,) = small_call(pair_kernel, "pair", [half], info, packed, partner)
    done = meanwhile(total)
    info, _ = lax.optimization_barrier((info, done[0]))
    entering = []
    for index, (bit, group) in enumerate(stages):
        last = index + 1 == len(stages)
        members = [total]
        for code in range(1, 2**group):
            mask = code << bit
            members.append(forward(total, mask, bit) if last else swap(total, mask))
        kernel = functools.partial(merge_kernel, group, RANKS + index, len(entering), last)
        shapes = [states] if last else [states, half]
        results = small_call(kernel, "merge", shapes, info, *members, *entering)
        entering = [results[0]]
        total = results[-1]
    return (entering[0], swap(entering[0], 1), partner), done


def per_device(
    tokens,
    input_gain,
    main_weight,
    side_weight,
    conv_kernel,
    step_bias,
    decay_rate,
    skip_gain,
    output_gain,
    output_weight,
):
    length, features = tokens.shape
    inner = main_weight.shape[2] // 2
    heads = decay_rate.shape[1]
    state = (side_weight.shape[2] - heads) // 2
    head_dim = inner // heads
    chunks = length // CHUNK
    seq_count = lax.axis_size("seq")
    section_count = lax.axis_size("section")
    section_index = lax.axis_index("section")
    seq_index = lax.axis_index("seq")
    reverse = section_index % 2
    weight = lax.all_gather(output_weight[0], "seq", axis=0, tiled=True)
    expand = np.repeat(np.eye(heads, dtype=np.float32), head_dim, axis=1)
    spread = jnp.asarray(np.concatenate([expand, expand], axis=0), BF16)
    skip_row = jnp.repeat(skip_gain, head_dim, axis=1)
    upper = seq_index % 2
    facts = [reverse, upper, (upper == reverse).astype(jnp.int32)]
    for bit, group in stages_of(seq_count):
        position = (seq_index >> bit) % 2**group
        facts.append(jnp.where(reverse == 1, 2**group - 1 - position, position))
    places = len(facts)
    rounds = section_count // 2
    for round_index in range(rounds):
        facts.append(section_index - 2 * round_index)
    info = jnp.stack([fact.astype(jnp.int32) for fact in facts])
    info, skip_row = lax.optimization_barrier((info, skip_row))
    order = [chunks - 1, 0] + list(range(1, chunks - 1))

    def edges(first_rows, last_rows, sections):
        pairs = []
        for s in sections:
            for i in range(seq_count):
                target = i + 1 if s % 2 == 0 else i - 1
                if 0 <= target < seq_count:
                    pairs.append((i * section_count + s, target * section_count + s))
        value = jnp.where(reverse == 1, first_rows, last_rows)
        return lax.ppermute(value, ("seq", "section"), pairs)

    current = tokens
    halo = edges(tokens[:HALO], tokens[length - HALO :], (0, 1))
    previous = None
    for round_index in range(rounds):
        active = (2 * round_index, 2 * round_index + 1)
        normed, x, b, c_rows, cumulative, shifted, reach, local, packed = prep(
            info,
            current,
            halo,
            input_gain,
            main_weight,
            side_weight,
            conv_kernel,
            step_bias,
            decay_rate,
            spread,
            inner,
            state,
        )
        def meanwhile(total):
            ready, _ = lax.optimization_barrier((normed, total))
            return mid(ready, main_weight, x, b, c_rows, cumulative, shifted, skip_row, inner)

        state_parts, (y, gate) = entering_state(packed, info, active, seq_count, meanwhile)
        last_round = round_index + 1 == rounds
        low, high = active
        place = section_index - low
        mode = ("exchange", places) if last_round else (tuple(order), SKEW, places + round_index)
        outs = finish(
            mode, info, current, y, gate, c_rows, reach, local, state_parts,
            output_gain, spread, weight, previous if last_round else [],
        )
        if last_round:
            *sent, base = outs
            break
        hops = 3
        received = []
        values = []
        for step in range(chunks + (hops - 1) * SKEW):
            pairs = [
                (low + hop, low + hop + 1) for hop in range(hops) if 0 <= step - hop * SKEW < chunks
            ]
            if step < SKEW:
                value = outs[step]
            elif step < len(outs):
                value = (outs[step] + received[step - SKEW].astype(F32)).astype(BF16)
            else:
                value = received[step - SKEW]
            values.append(value)
            received.append(lax.ppermute(value, "section", pairs))
        layer_rows = [None] * chunks
        next_rows = [None] * chunks
        for step, index in enumerate(order):
            layer_rows[index] = values[step + SKEW]
            next_rows[index] = jnp.where(place == 3, received[step + 2 * SKEW], received[step + SKEW])
        previous = layer_rows
        halo = edges(
            next_rows[0][:HALO], next_rows[chunks - 1][CHUNK - HALO :], (low + 2, high + 2)
        )
        current = jnp.concatenate(next_rows, axis=0)
    finished = None
    for index in range(chunks):
        other = lax.ppermute(sent[index], "section", [(low, high), (high, low), (1, 0)])
        finished = settle(index, places, info, base, sent[index], other, finished)
    return finished


def solution(mesh):
    placed = (
        P("seq", None),
        P("section", None),
        P("section", None, None),
        P("section", None, None),
        P("section", None, None),
        P("section", None),
        P("section", None),
        P("section", None),
        P("section", None),
        P("section", "seq", None),
    )
    return jax.shard_map(
        per_device, mesh=mesh, in_specs=placed, out_specs=P("section", "seq", None), check_vma=False
    )
```

```python
import functools

import jax
import jax.numpy as jnp
import numpy as np
from jax import lax
from jax.experimental import pallas as pl
from jax.experimental.pallas import tpu as pltpu
from jax.sharding import PartitionSpec as P

EPSILON = 1e-05
CHUNK = 128
WIDTH = 512
HALO = 16
LIMIT = 36 * 2**20
SMALL = 8 * 2**20
SKEW = 2
REVERSE, UPPER, FIRST, SEQ, RANKS = 0, 1, 2, 3, 4
LOG2E = 1.4426950408889634
F32 = jnp.float32
BF16 = jnp.bfloat16


def silu(value):
    half = 0.5 * value
    return half + half * jnp.tanh(half)


def dot(left, right):
    return jnp.dot(left, right, preferred_element_type=F32)


def order_matrix(size, reverse):
    row = lax.broadcasted_iota(jnp.int32, (size, size), 0)
    column = lax.broadcasted_iota(jnp.int32, (size, size), 1)
    target = jnp.where(reverse == 1, size - 1 - row, row)
    return jnp.where(column == target, 1.0, 0.0).astype(BF16)


def high_low(value):
    high = value.astype(BF16)
    low = (value - high.astype(F32)).astype(BF16)
    return jnp.concatenate([high, low], axis=1)


def norm_block(values, gain_row):
    widened = values.astype(F32)
    inverse_rms = lax.rsqrt(jnp.mean(widened * widened, axis=-1, keepdims=True) + EPSILON)
    return (widened * inverse_rms * gain_row).astype(BF16)


def prep_kernel(
    info,
    rows,
    halo,
    gain,
    wide,
    side_weight,
    taps,
    side_taps,
    bias,
    decay,
    spread,
    normed_out,
    x_out,
    b_out,
    c_out,
    cum_out,
    shifted_out,
    reach_out,
    local_out,
    state_out,
    extended,
    buffer,
    turned,
    shares,
    wide_shares,
    running,
):
    step_index = pl.program_id(0)
    reverse = info[REVERSE]
    length = rows.shape[0]
    heads = bias.shape[1]
    state = b_out.shape[1]
    chunks = length // CHUNK
    margin = taps.shape[0] - 1
    width = wide.shape[1]

    def filtered(kernel, start, size, lanes):
        total = None
        for k in range(margin + 1):
            part = buffer[HALO - margin + k + start : HALO - margin + k + start + size, lanes]
            term = kernel[k : k + 1, lanes] * part
            total = term if total is None else total + term
        return silu(total).astype(BF16)

    @pl.when(step_index == 0)
    def _():
        turn = order_matrix(2 * CHUNK, reverse)
        small_turn = order_matrix(HALO, reverse)
        edge = norm_block(halo[...], gain[...])
        extended[0:HALO] = dot(small_turn, edge).astype(BF16)
        pairs = length // (2 * CHUNK)
        for pair in range(pairs):
            source = jnp.where(reverse == 1, pairs - 1 - pair, pair) * (2 * CHUNK)
            source = pl.multiple_of(source, 2 * CHUNK)
            piece = norm_block(rows[pl.ds(source, 2 * CHUNK), :], gain[...])
            start = HALO + pair * 2 * CHUNK
            extended[start : start + 2 * CHUNK] = dot(turn, piece).astype(BF16)
        normed_out[...] = extended[HALO:]
        side = lax.dot_general(
            extended[...], side_weight[...], (((1,), (1,)), ((), ())), preferred_element_type=F32
        )
        side = side.astype(BF16).astype(F32)
        buffer[:, 0 : 2 * state] = side[:, 0 : 2 * state]
        raw = side[HALO:, 2 * state :] + bias[...]
        step = jnp.maximum(raw, 0.0) + jnp.log1p(jnp.exp(-jnp.abs(raw)))
        change = step * (decay[...] * (-LOG2E))
        row = lax.broadcasted_iota(jnp.int32, (CHUNK, CHUNK), 0)
        column = lax.broadcasted_iota(jnp.int32, (CHUNK, CHUNK), 1)
        triangle = jnp.where(row >= column, 1.0, 0.0).astype(F32)
        before = jnp.zeros((1, heads), F32)
        totals = []
        befores = []
        for c in range(chunks):
            here = slice(c * CHUNK, (c + 1) * CHUNK)
            cumulative = jnp.dot(
                triangle, change[here], preferred_element_type=F32, precision=lax.Precision.HIGHEST
            )
            last = cumulative[CHUNK - 1 :, :]
            befores.append(before)
            totals.append(last)
            before = before + last
            moved = cumulative - jnp.log2(step[here])
            blank = jnp.zeros((CHUNK, 128 - 2 * heads), F32)
            flipped = jnp.concatenate([cumulative, moved, blank], axis=1).T
            cum_out[:, here] = flipped[0:heads]
            shifted_out[:, here] = flipped[heads : 2 * heads]
            shares[here, :] = high_low(jnp.exp2(last - cumulative) * step[here])
            reach_out[here, :] = high_low(jnp.exp2(cumulative))
        befores.append(before)
        zero_rows = jnp.zeros((HALO - chunks, heads), F32)
        shares[length:, :] = high_low(jnp.exp2(jnp.concatenate(totals + [zero_rows], axis=0)))
        zero_rows = jnp.zeros((HALO - chunks - 1, heads), F32)
        reach_out[length:, :] = high_low(jnp.exp2(jnp.concatenate(befores + [zero_rows], axis=0)))
        for c in range(chunks):
            start = c * CHUNK
            here = slice(start, start + CHUNK)
            in_part = filtered(side_taps, start, CHUNK, slice(0, state))
            b_out[here] = in_part
            turned[:, here] = in_part.astype(F32).T.astype(BF16)
            c_out[here] = filtered(side_taps, start, CHUNK, slice(state, 2 * state))

    buffer[...] = dot(extended[...], wide[...]).astype(BF16).astype(F32)
    wide_shares[...] = dot(shares[...], spread[...])
    sub = 64
    running[...] = jnp.zeros_like(running)
    for c in range(chunks):
        here = slice(c * CHUNK, (c + 1) * CHUNK)
        for lane in range(0, width, 256):
            lanes = slice(lane, lane + 256)
            weighted = []
            for start in range(c * CHUNK, (c + 1) * CHUNK, sub):
                piece = filtered(taps, start, sub, lanes)
                x_out[start : start + sub, lanes] = piece
                weighted.append(
                    (piece.astype(F32) * wide_shares[start : start + sub, lanes]).astype(BF16)
                )
            states = dot(turned[:, here], jnp.concatenate(weighted, axis=0))
            entering = running[:, lanes]
            local_out[c, :, lanes] = entering.astype(BF16)
            total = wide_shares[length + c : length + c + 1, lanes]
            running[:, lanes] = total * entering + states
    state_out[0:state, :] = running[...].astype(BF16)
    through = wide_shares[length : length + 1, :]
    for c in range(1, chunks):
        through = through * wide_shares[length + c : length + c + 1, :]
    high = through.astype(BF16)
    low = (through - high.astype(F32)).astype(BF16)
    tail = jnp.concatenate(
        [high.astype(F32), low.astype(F32), jnp.zeros((HALO - 2, width), F32)], axis=0
    )
    state_out[state:, :] = tail.astype(BF16)


def mid_kernel(
    normed, gate_weight, x, b, c_rows, cumulative, shifted, skip, spread, y_out, gate_out, scores
):
    step_index = pl.program_id(0)
    length = x.shape[0]
    chunks = length // CHUNK
    heads_here = cumulative.shape[0]
    head_dim = x.shape[1] // heads_here
    row = lax.broadcasted_iota(jnp.int32, (CHUNK, CHUNK), 0)
    column = lax.broadcasted_iota(jnp.int32, (CHUNK, CHUNK), 1)
    causal = row >= column
    lane = lax.broadcasted_iota(jnp.int32, (CHUNK, 2 * head_dim), 1)

    @pl.when(step_index == 0)
    def _():
        for c in range(chunks):
            here = slice(c * CHUNK, (c + 1) * CHUNK)
            scores[here, :] = lax.dot_general(
                c_rows[here, :], b[here, :], (((1,), (1,)), ((), ())), preferred_element_type=F32
            )

    gate_out[...] = dot(normed[...], gate_weight[...]).astype(BF16)
    skip_rows = jnp.broadcast_to(skip[...], (HALO, skip.shape[1]))
    skips = dot(high_low(skip_rows), spread[...])[0:1]
    for c in range(chunks):
        here = slice(c * CHUNK, (c + 1) * CHUNK)
        score = scores[here, :]
        blank = jnp.zeros((128 - heads_here, CHUNK), F32)
        columns = jnp.concatenate([cumulative[:, here], blank], axis=0).T
        for pair in range(heads_here // 2):
            lanes = slice(2 * pair * head_dim, (2 * pair + 2) * head_dim)
            parts = []
            for h in (2 * pair, 2 * pair + 1):
                gap = columns[:, h : h + 1] - shifted[h : h + 1, here]
                parts.append((score * jnp.exp2(jnp.where(causal, gap, -jnp.inf))).astype(BF16))
            values = x[here, lanes]
            zero = jnp.zeros_like(values)
            stacked = jnp.concatenate(
                [jnp.where(lane < head_dim, values, zero), jnp.where(lane < head_dim, zero, values)],
                axis=0,
            )
            within = dot(jnp.concatenate(parts, axis=1), stacked)
            y_out[here, lanes] = within + skips[:, lanes] * values.astype(F32)


def finish_kernel(
    count,
    plan,
    shard_rows,
    mode,
    info,
    rows,
    y,
    gate,
    c_rows,
    reach,
    reach_tail,
    local,
    mine,
    other,
    partner,
    gain,
    spread,
    *rest,
):
    far_pieces = rest[: len(plan)]
    outs = rest[len(plan) : -4]
    normed, entering, weight, arrived = rest[-4:]
    step_index = pl.program_id(0)
    steps = pl.num_programs(0)
    reverse = info[REVERSE]
    size, inner = y.shape
    parts = size // CHUNK
    state = mine.shape[0]
    fetches = []
    for piece, ranges in zip(far_pieces, plan):
        for mask, source, offset, extent in ranges:
            place = 0
            if mask is not None:
                place = pl.multiple_of((info[SEQ] ^ mask) * shard_rows + offset, 16)
            fetches.append(
                pltpu.make_async_copy(
                    piece.at[source : source + extent],
                    weight.at[pl.ds(place, extent)],
                    arrived.at[len(fetches)],
                )
            )

    @pl.when(step_index == 0)
    def _():
        for fetch in fetches:
            fetch.start()
        half = inner // 2
        upper = info[UPPER] == 1
        first = info[FIRST] == 1
        for start in range(0, inner, 256):
            lanes = slice(start, start + 256)
            inside = slice(start % half, start % half + 256)
            pair = (other, mine) if start < half else (mine, other)
            full = jnp.where(upper, pair[0][:, inside], pair[1][:, inside])
            tail = partner[state:, lanes].astype(F32)
            through = tail[0:1] + tail[1:2]
            moved = (through * full.astype(F32) + partner[:state, lanes].astype(F32)).astype(BF16)
            entering[:, lanes] = jnp.where(first, full, moved)

    position = jnp.where(reverse == 1, steps - 1 - step_index, step_index)
    tail = dot(reach_tail[...], spread[...])
    index_row = lax.broadcasted_iota(jnp.int32, (HALO, 1), 0)
    turn = order_matrix(size, reverse)
    block = 256
    befores = [
        jnp.sum(jnp.where(index_row == position * parts + p, tail, 0.0), axis=0, keepdims=True)
        for p in range(parts)
    ]
    squares = [jnp.zeros((CHUNK, 1), F32) for _ in range(parts)]
    gated = {}
    for start in range(0, inner, block):
        lanes = slice(start, start + block)
        for p in range(parts):
            here = slice(p * CHUNK, (p + 1) * CHUNK)
            full = local[p, :, lanes].astype(F32) + befores[p][:, lanes] * entering[:, lanes].astype(F32)
            carried = dot(c_rows[here, :], full.astype(BF16)) * dot(reach[here, :], spread[:, lanes])
            part = (y[here, lanes] + carried) * silu(gate[here, lanes].astype(F32))
            squares[p] = squares[p] + jnp.sum(part * part, axis=-1, keepdims=True)
            gated[p, start] = part
    inverse_rms = [lax.rsqrt(total * (1.0 / inner) + EPSILON) for total in squares]
    for start in range(0, inner, block):
        lanes = slice(start, start + block)
        piece = jnp.concatenate(
            [(gated[p, start] * inverse_rms[p] * gain[:, lanes]).astype(BF16) for p in range(parts)],
            axis=0,
        )
        piece = dot(turn, piece).astype(BF16)
        normed[:, lanes] = piece

    @pl.when(step_index == 0)
    def _():
        for fetch in fetches:
            fetch.wait()

    total = dot(normed[...], weight[...])
    base = rows[...].astype(F32) + total
    if mode[0] == "exchange":
        earlier = outs[:count]
        sent = outs[count : 2 * count]
        outs[2 * count][...] = base
        for k in range(count):

            @pl.when(step_index == k // parts)
            def _(k=k):
                start = k % parts * CHUNK
                mine_now = total[start : start + CHUNK].astype(BF16)
                sent[k][...] = jnp.where(info[mode[1]] == 1, earlier[k][...], mine_now)

        return
    order, skew, place_slot = mode
    place = info[place_slot]

    @pl.when(step_index == 0)
    def _():
        for out in outs:
            out[...] = jnp.zeros_like(out)

    for k, index in enumerate(order):
        start = index % parts * CHUNK
        here = slice(start, start + CHUNK)

        @pl.when((step_index == index // parts) & (place == 0))
        def _(k=k, here=here):
            outs[k][...] = total[here].astype(outs[k].dtype)

        @pl.when((step_index == index // parts) & (place == 1))
        def _(k=k, here=here):
            outs[k + skew][...] = base[here]


def kept(shape, dtype):
    return pltpu.VMEM(shape, dtype)


def near(*values):
    return tuple(pltpu.with_memory_space_constraint(v, pltpu.VMEM) for v in values)


def far(value):
    return pltpu.with_memory_space_constraint(value, pltpu.HBM)


def whole_block(shape):
    return pl.BlockSpec(shape, lambda *_: (0,) * len(shape))


def prep(info, rows, halo, gain, main, side, conv, bias, decay, spread, inner, state):
    length, features = rows.shape
    heads = bias.shape[1]
    steps = inner // WIDTH
    chunks = length // CHUNK
    margin = conv.shape[1]
    side_width = 2 * state
    grid_spec = pltpu.PrefetchScalarGridSpec(
        num_scalar_prefetch=1,
        grid=(steps,),
        in_specs=[
            whole_block((length, features)),
            whole_block((HALO, features)),
            whole_block((1, features)),
            pl.BlockSpec((None, features, WIDTH), lambda j, _: (0, 0, steps + j)),
            pl.BlockSpec((None, side.shape[1], features), lambda j, _: (0, 0, 0)),
            pl.BlockSpec((None, margin, WIDTH), lambda j, _: (0, 0, j)),
            pl.BlockSpec((None, margin, side_width), lambda j, _: (0, 0, inner // side_width)),
            whole_block((1, heads)),
            whole_block((1, heads)),
            pl.BlockSpec((2 * heads, WIDTH), lambda j, _: (0, j)),
        ],
        out_specs=[
            whole_block((length, features)),
            pl.BlockSpec((length, WIDTH), lambda j, _: (0, j)),
            whole_block((length, state)),
            whole_block((length, state)),
            whole_block((heads, length)),
            whole_block((heads, length)),
            whole_block((length + HALO, 2 * heads)),
            pl.BlockSpec((chunks, state, WIDTH), lambda j, _: (0, 0, j)),
            pl.BlockSpec((state + HALO, WIDTH), lambda j, _: (0, j)),
        ],
        scratch_shapes=[
            pltpu.VMEM((length + HALO, features), BF16),
            pltpu.VMEM((length + HALO, WIDTH), F32),
            pltpu.VMEM((state, length), BF16),
            pltpu.VMEM((length + HALO, 2 * heads), BF16),
            pltpu.VMEM((length + HALO, WIDTH), F32),
            pltpu.VMEM((state, WIDTH), F32),
        ],
    )
    shape = jax.ShapeDtypeStruct
    return pl.pallas_call(
        prep_kernel,
        grid_spec=grid_spec,
        out_shape=[
            kept((length, features), BF16),
            kept((length, inner), BF16),
            kept((length, state), BF16),
            kept((length, state), BF16),
            kept((heads, length), F32),
            kept((heads, length), F32),
            kept((length + HALO, 2 * heads), BF16),
            kept((chunks, state, inner), BF16),
            shape((state + HALO, inner), BF16),
        ],
        compiler_params=pltpu.CompilerParams(
            vmem_limit_bytes=LIMIT, dimension_semantics=("arbitrary",)
        ),
        cost_estimate=pl.CostEstimate(
            flops=2 * length * features * inner, bytes_accessed=12 * 2**20, transcendentals=0
        ),
        name="prep",
    )(info, rows, halo, far(gain), far(main), far(side), far(conv), far(conv), far(bias), far(decay), far(spread))


def mid(normed, main, x, b, c_rows, cumulative, shifted, skip, spread, inner):
    length, features = normed.shape
    state = b.shape[1]
    steps = inner // WIDTH
    heads_here = cumulative.shape[0] // steps
    return pl.pallas_call(
        mid_kernel,
        grid=(steps,),
        in_specs=[
            whole_block((length, features)),
            pl.BlockSpec((None, features, WIDTH), lambda j: (0, 0, j)),
            pl.BlockSpec((length, WIDTH), lambda j: (0, j)),
            whole_block((length, state)),
            whole_block((length, state)),
            pl.BlockSpec((heads_here, length), lambda j: (j, 0)),
            pl.BlockSpec((heads_here, length), lambda j: (j, 0)),
            whole_block(skip.shape),
            pl.BlockSpec((spread.shape[0], WIDTH), lambda j: (0, j)),
        ],
        out_specs=[
            pl.BlockSpec((length, WIDTH), lambda j: (0, j)),
            pl.BlockSpec((length, WIDTH), lambda j: (0, j)),
        ],
        out_shape=[
            kept((length, inner), F32),
            kept((length, inner), BF16),
        ],
        scratch_shapes=[pltpu.VMEM((length, CHUNK), F32)],
        compiler_params=pltpu.CompilerParams(
            vmem_limit_bytes=LIMIT, dimension_semantics=("arbitrary",)
        ),
        cost_estimate=pl.CostEstimate(
            flops=2 * length * features * inner, bytes_accessed=12 * 2**20, transcendentals=0
        ),
        name="mid",
    )(*near(normed), far(main), *near(x, b, c_rows, cumulative, shifted), far(skip), far(spread))


def finish(mode, info, rows, y, gate, c_rows, reach, local, state_parts, gain, spread, pieces, earlier):
    features = rows.shape[1]
    length, inner = y.shape
    state = c_rows.shape[1]
    mine, other, partner = state_parts
    plan = [ranges for _, ranges in pieces]
    shard_rows = inner // lax.axis_size("seq")
    reach_width = reach.shape[1]
    tail = length // HALO
    size = 2 * CHUNK
    steps = length // size
    chunks = length // CHUNK

    if mode[0] == "exchange":
        out_specs = [whole_block((CHUNK, features))] * chunks
        out_specs = out_specs + [pl.BlockSpec((size, features), lambda j, s: (j, 0))]
        out_shape = [jax.ShapeDtypeStruct((CHUNK, features), BF16)] * chunks
        out_shape = out_shape + [kept((length, features), F32)]
    else:
        skew = mode[1]
        out_specs = [whole_block((CHUNK, features))] * (chunks + skew)
        out_shape = [jax.ShapeDtypeStruct((CHUNK, features), BF16)] * skew
        out_shape = out_shape + [kept((CHUNK, features), F32)] * chunks

    def turned_block(shape):
        def place(j, s):
            return (jnp.where(s[0] == 1, steps - 1 - j, j),) + (0,) * (len(shape) - 1)

        return pl.BlockSpec(shape, place)

    grid_spec = pltpu.PrefetchScalarGridSpec(
        num_scalar_prefetch=1,
        grid=(steps,),
        in_specs=[
            pl.BlockSpec((size, features), lambda j, s: (j, 0)),
            turned_block((size, inner)),
            turned_block((size, inner)),
            turned_block((size, state)),
            turned_block((size, reach_width)),
            pl.BlockSpec((HALO, reach_width), lambda j, s: (tail, 0)),
            turned_block((size // CHUNK, state, inner)),
            whole_block(mine.shape),
            whole_block(other.shape),
            whole_block(partner.shape),
            whole_block((1, inner)),
            whole_block(spread.shape),
        ]
        + [pl.BlockSpec(memory_space=pl.ANY)] * len(pieces)
        + [whole_block(value.shape) for value in earlier],
        out_specs=out_specs,
        scratch_shapes=[
            pltpu.VMEM((size, inner), BF16),
            pltpu.VMEM((state, inner), BF16),
            pltpu.VMEM((inner, features), BF16),
            pltpu.SemaphoreType.DMA((sum(len(ranges) for ranges in plan),)),
        ],
    )
    return pl.pallas_call(
        functools.partial(finish_kernel, chunks, plan, shard_rows, mode),
        grid_spec=grid_spec,
        out_shape=out_shape,
        compiler_params=pltpu.CompilerParams(
            vmem_limit_bytes=LIMIT, dimension_semantics=("arbitrary",)
        ),
        cost_estimate=pl.CostEstimate(
            flops=2 * length * features * inner, bytes_accessed=16 * 2**20, transcendentals=0
        ),
        name="finish",
    )(
        info, rows, *near(y, gate, c_rows, reach, reach, local), mine, other, partner,
        far(gain), far(spread), *[far(piece) for piece, _ in pieces], *earlier,
    )


def stack_kernel(counts, *refs):
    sources, outs = refs[: -len(counts)], refs[-len(counts) :]
    position = 0
    for out, count in zip(outs, counts):
        start = 0
        for source in sources[position : position + count]:
            out[start : start + source.shape[0]] = source[...]
            start += source.shape[0]
        position += count


def stacked(groups):
    operands = []
    specs = []
    out_shape = []
    for group in groups:
        total = 0
        for value, index, rows in group:
            operands.append(value)
            specs.append(pl.BlockSpec((rows, value.shape[1]), lambda j, index=index: (index, 0)))
            total += rows
        out_shape.append(pltpu.HBM((total, group[0][0].shape[1]), BF16))
    return pl.pallas_call(
        functools.partial(stack_kernel, [len(group) for group in groups]),
        grid=(1,),
        in_specs=specs,
        out_specs=[whole_block(shape.shape) for shape in out_shape],
        out_shape=out_shape,
        compiler_params=pltpu.CompilerParams(vmem_limit_bytes=16 * 2**20),
        cost_estimate=pl.CostEstimate(flops=10**6, bytes_accessed=10**6, transcendentals=0),
        name="stack",
    )(*[far(value) for value in operands])


def seq_swap(value, mask):
    count = lax.axis_size("seq")
    return lax.ppermute(value, "seq", [(i, i ^ mask) for i in range(count)])


def split_state(packed):
    state = packed.shape[0] - HALO
    values = packed[:state].astype(F32)
    tail = packed[state:].astype(F32)
    return values, tail[0:1] + tail[1:2]


def joined_state(values, through):
    high = through.astype(BF16)
    low = (through - high.astype(F32)).astype(BF16)
    rest = jnp.zeros((HALO - 2, through.shape[1]), F32)
    tail = jnp.concatenate([high.astype(F32), low.astype(F32), rest], axis=0)
    return values.astype(BF16), tail.astype(BF16)


def after(earlier, later):
    return later[1] * earlier[0] + later[0], earlier[1] * later[1]


def chosen(condition, first, second):
    return tuple(jnp.where(condition, a, b) for a, b in zip(first, second))


def pair_kernel(info, mine, partner, out):
    half = out.shape[1]
    first = info[FIRST] == 1
    state = out.shape[0] - HALO
    for start in range(0, half, 256):
        place = pl.multiple_of(info[UPPER] * half + start, 256)
        one = split_state(mine[:, pl.ds(place, 256)])
        two = split_state(partner[:, pl.ds(place, 256)])
        total = after(chosen(first, one, two), chosen(first, two, one))
        out[:state, start : start + 256], out[state:, start : start + 256] = joined_state(*total)


def merge_kernel(group, slot, has_entering, last, info, *refs):
    members = refs[: 2**group]
    entering_out = refs[2**group + has_entering]
    rank = info[slot]
    state, half = entering_out.shape
    for start in range(0, half, 256):
        lanes = slice(start, start + 256)
        values = [split_state(member[:, lanes]) for member in members]
        before = (jnp.zeros((state, 256), F32), jnp.ones((1, 256), F32))
        whole = before
        for place in range(2**group):
            value = values[0]
            for code in range(1, 2**group):
                value = chosen((rank ^ code) == place, values[code], value)
            if place < 2**group - 1:
                before = chosen(place < rank, after(before, value), before)
            if not last:
                whole = after(whole, value)
        if has_entering:
            inside = refs[2**group][:, lanes].astype(F32)
            through = jnp.ones((1, 256), F32)
            before = after(before, (inside, through))
        entering_out[:, lanes] = before[0].astype(BF16)
        if not last:
            out = refs[-1]
            out[:state, lanes], out[state:, lanes] = joined_state(*whole)


def small_call(kernel, name, out_shape, info, *operands):
    return pl.pallas_call(
        kernel,
        in_specs=[pl.BlockSpec(memory_space=pltpu.SMEM)] + [whole_block(v.shape) for v in operands],
        out_specs=[whole_block(v.shape) for v in out_shape],
        out_shape=out_shape,
        compiler_params=pltpu.CompilerParams(vmem_limit_bytes=SMALL),
        cost_estimate=pl.CostEstimate(flops=10**6, bytes_accessed=10**6, transcendentals=0),
        name=name,
    )(info, *operands)


def settle_kernel(place, info, base, sent, other, *rest):
    section = info[place]
    rows = (base[...] + other[...].astype(F32)).astype(BF16)
    rows = jnp.where(section == 1, sent[...], rows)
    rest[-1][...] = jnp.where(section == 0, other[...], rows)


def settle(index, place, info, base, sent, other, finished):
    length, features = base.shape
    block = pl.BlockSpec((CHUNK, features), lambda j: (index, 0))
    out_block = pl.BlockSpec((None, CHUNK, features), lambda j: (0, index, 0))
    passed = [] if finished is None else [finished]
    return pl.pallas_call(
        functools.partial(settle_kernel, place),
        grid=(1,),
        in_specs=[pl.BlockSpec(memory_space=pltpu.SMEM), block]
        + [whole_block((CHUNK, features))] * 2
        + [pl.BlockSpec(memory_space=pl.ANY)] * len(passed),
        out_specs=out_block,
        out_shape=jax.ShapeDtypeStruct((1, length, features), BF16),
        input_output_aliases={4: 0} if passed else {},
        compiler_params=pltpu.CompilerParams(vmem_limit_bytes=SMALL),
        cost_estimate=pl.CostEstimate(flops=10**6, bytes_accessed=10**6, transcendentals=0),
        name="settle",
    )(info, base, sent, other, *passed)


def stages_of(seq_count):
    bits = seq_count.bit_length() - 1
    found = []
    bit = 1
    while bit < bits:
        group = min(2, bits - bit)
        found.append((bit, group))
        bit += group
    return found


def entering_state(packed, info, sections, seq_count, meanwhile):
    section_count = lax.axis_size("section")
    stages = stages_of(seq_count)

    def swap(value, mask):
        pairs = [
            (i * section_count + s, (i ^ mask) * section_count + s)
            for s in sections
            for i in range(seq_count)
        ]
        return lax.ppermute(value, ("seq", "section"), pairs)

    def forward(value, mask, low_bit):
        pairs = []
        for s in sections:
            for i in range(seq_count):
                later = (i ^ mask) >> low_bit > i >> low_bit
                if later == (s % 2 == 0):
                    pairs.append((i * section_count + s, (i ^ mask) * section_count + s))
        return lax.ppermute(value, ("seq", "section"), pairs)

    depth, inner = packed.shape
    half = jax.ShapeDtypeStruct((depth, inner // 2), BF16)
    states = jax.ShapeDtypeStruct((depth - HALO, inner // 2), BF16)
    partner = swap(packed, 1)
    (total,) = small_call(pair_kernel, "pair", [half], info, packed, partner)
    done = meanwhile(total)
    info, _ = lax.optimization_barrier((info, done[0]))
    entering = []
    for index, (bit, group) in enumerate(stages):
        last = index + 1 == len(stages)
        members = [total]
        for code in range(1, 2**group):
            mask = code << bit
            members.append(forward(total, mask, bit) if last else swap(total, mask))
        kernel = functools.partial(merge_kernel, group, RANKS + index, len(entering), last)
        shapes = [states] if last else [states, half]
        results = small_call(kernel, "merge", shapes, info, *members, *entering)
        entering = [results[0]]
        total = results[-1]
    return (entering[0], swap(entering[0], 1), partner), done


def per_device(
    tokens,
    input_gain,
    main_weight,
    side_weight,
    conv_kernel,
    step_bias,
    decay_rate,
    skip_gain,
    output_gain,
    output_weight,
):
    length, features = tokens.shape
    inner = main_weight.shape[2] // 2
    heads = decay_rate.shape[1]
    state = (side_weight.shape[2] - heads) // 2
    head_dim = inner // heads
    chunks = length // CHUNK
    seq_count = lax.axis_size("seq")
    section_count = lax.axis_size("section")
    section_index = lax.axis_index("section")
    seq_index = lax.axis_index("seq")
    reverse = section_index % 2
    shard = output_weight[0]
    expand = np.repeat(np.eye(heads, dtype=np.float32), head_dim, axis=1)
    spread = jnp.asarray(np.concatenate([expand, expand], axis=0), BF16)
    upper = seq_index % 2
    facts = [reverse, upper, (upper == reverse).astype(jnp.int32), seq_index]
    for bit, group in stages_of(seq_count):
        position = (seq_index >> bit) % 2**group
        facts.append(jnp.where(reverse == 1, 2**group - 1 - position, position))
    places = len(facts)
    rounds = section_count // 2
    for round_index in range(rounds):
        facts.append(section_index - 2 * round_index)
    info = jnp.stack([fact.astype(jnp.int32) for fact in facts])
    order = [chunks - 1, 0] + list(range(1, chunks - 1))

    def edges(first_rows, last_rows, sections):
        pairs = []
        for s in sections:
            for i in range(seq_count):
                target = i + 1 if s % 2 == 0 else i - 1
                if 0 <= target < seq_count:
                    pairs.append((i * section_count + s, target * section_count + s))
        value = jnp.where(reverse == 1, first_rows, last_rows)
        return lax.ppermute(value, ("seq", "section"), pairs)

    current = tokens
    halo = edges(tokens[:HALO], tokens[length - HALO :], (0, 1))
    previous = None
    shards = None
    if seq_count == 8:
        halo, shard = lax.optimization_barrier((halo, shard))
        shards = [shard, seq_swap(shard, 2), seq_swap(shard, 4)]
        pieces = None
    else:
        whole = lax.all_gather(shard, "seq", axis=0, tiled=True)
        pieces = [(whole, [(None, 0, 0, inner)])]
    for round_index in range(rounds):
        active = (2 * round_index, 2 * round_index + 1)
        normed, x, b, c_rows, cumulative, shifted, reach, local, packed = prep(
            info,
            current,
            halo,
            input_gain,
            main_weight,
            jnp.swapaxes(side_weight, 1, 2),
            conv_kernel,
            step_bias,
            decay_rate,
            spread,
            inner,
            state,
        )
        early = round_index == 0 and shards
        if early:
            packed, *shards[1:] = lax.optimization_barrier((packed, *shards[1:]))

        def meanwhile(total, normed=normed):
            nonlocal pieces
            if early:
                *parts, _ = lax.optimization_barrier((*shards, total))
                rows = parts[0].shape[0] // 2
                up, down, three = stacked(
                    [
                        [(parts[2], 0, rows)],
                        [(parts[1], 1, rows)],
                        [(part, 0, 2 * rows) for part in parts],
                    ]
                )
                halves = [seq_swap(up, 2), seq_swap(down, 4)]
                swapped = seq_swap(three, 1)
            ready, _ = lax.optimization_barrier((normed, total))
            y, gate = mid(ready, main_weight, x, b, c_rows, cumulative, shifted, skip_gain, spread, inner)
            if early:
                *halves, _ = lax.optimization_barrier((*halves, y))
                rows = halves[0].shape[0]
                (joined,) = stacked([[(half, 0, rows) for half in halves]])
                diagonal = seq_swap(joined, 1)
                pieces = [(value, [(mask, 0, 0, 2 * rows)]) for value, mask in zip(shards, (0, 2, 4))]
                pieces += [(half, [(6, 0, i * rows, rows)]) for i, half in enumerate(halves)]
                pieces.append((swapped, [(m, i * 2 * rows, 0, 2 * rows) for i, m in enumerate((1, 3, 5))]))
                pieces.append((diagonal, [(7, 0, 0, 2 * rows)]))
            return y, gate

        state_parts, (y, gate) = entering_state(packed, info, active, seq_count, meanwhile)
        last_round = round_index + 1 == rounds
        low, high = active
        place = section_index - low
        mode = ("exchange", places) if last_round else (tuple(order), SKEW, places + round_index)
        outs = finish(
            mode, info, current, y, gate, c_rows, reach, local, state_parts,
            output_gain, spread, pieces, previous if last_round else [],
        )
        if last_round:
            *sent, base = outs
            break
        hops = 3
        received = []
        values = []
        for step in range(chunks + (hops - 1) * SKEW):
            pairs = [
                (low + hop, low + hop + 1) for hop in range(hops) if 0 <= step - hop * SKEW < chunks
            ]
            if step < SKEW:
                value = outs[step]
            elif step < len(outs):
                value = (outs[step] + received[step - SKEW].astype(F32)).astype(BF16)
            else:
                value = received[step - SKEW]
            values.append(value)
            received.append(lax.ppermute(value, "section", pairs))
        layer_rows = [None] * chunks
        next_rows = [None] * chunks
        for step, index in enumerate(order):
            layer_rows[index] = values[step + SKEW]
            next_rows[index] = jnp.where(place == 3, received[step + 2 * SKEW], received[step + SKEW])
        previous = layer_rows
        halo = edges(
            next_rows[0][:HALO], next_rows[chunks - 1][CHUNK - HALO :], (low + 2, high + 2)
        )
        current = jnp.concatenate(next_rows, axis=0)
    finished = None
    for index in range(chunks):
        other = lax.ppermute(sent[index], "section", [(low, high), (high, low), (1, 0)])
        finished = settle(index, places, info, base, sent[index], other, finished)
    return finished


def solution(mesh):
    placed = (
        P("seq", None),
        P("section", None),
        P("section", None, None),
        P("section", None, None),
        P("section", None, None),
        P("section", None),
        P("section", None),
        P("section", None),
        P("section", None),
        P("section", "seq", None),
    )
    return jax.shard_map(
        per_device, mesh=mesh, in_specs=placed, out_specs=P("section", "seq", None), check_vma=False
    )
```

```python
import functools

import jax
import jax.numpy as jnp
import numpy as np
from jax import lax
from jax.experimental import pallas as pl
from jax.experimental.pallas import tpu as pltpu
from jax.sharding import PartitionSpec as P

EPSILON = 1e-05
CHUNK = 128
WIDTH = 512
HALO = 16
LIMIT = 28 * 2**20
SMALL = 8 * 2**20
SKEW = 2
REVERSE, UPPER, FIRST, SEQ, RANKS = 0, 1, 2, 3, 4
LOG2E = 1.4426950408889634
F32 = jnp.float32
BF16 = jnp.bfloat16


def silu(value):
    half = 0.5 * value
    return half + half * jnp.tanh(half)


def dot(left, right):
    return jnp.dot(left, right, preferred_element_type=F32)


def order_matrix(size, reverse):
    row = lax.broadcasted_iota(jnp.int32, (size, size), 0)
    column = lax.broadcasted_iota(jnp.int32, (size, size), 1)
    target = jnp.where(reverse == 1, size - 1 - row, row)
    return jnp.where(column == target, 1.0, 0.0).astype(BF16)


def high_low(value):
    high = value.astype(BF16)
    low = (value - high.astype(F32)).astype(BF16)
    return jnp.concatenate([high, low], axis=1)


def norm_block(values, gain_row):
    widened = values.astype(F32)
    inverse_rms = lax.rsqrt(jnp.mean(widened * widened, axis=-1, keepdims=True) + EPSILON)
    return (widened * inverse_rms * gain_row).astype(BF16)


def prep_kernel(
    info,
    rows,
    halo,
    gain,
    wide,
    side_weight,
    taps,
    side_taps,
    bias,
    decay,
    spread,
    normed_out,
    x_out,
    b_out,
    c_out,
    cum_out,
    shifted_out,
    reach_out,
    local_out,
    state_out,
    extended,
    buffer,
    turned,
    shares,
    wide_shares,
    running,
):
    step_index = pl.program_id(0)
    reverse = info[REVERSE]
    length = rows.shape[0]
    heads = bias.shape[1]
    state = b_out.shape[1]
    chunks = length // CHUNK
    margin = taps.shape[0] - 1
    width = wide.shape[1]

    def filtered(kernel, start, size, lanes):
        total = None
        for k in range(margin + 1):
            part = buffer[HALO - margin + k + start : HALO - margin + k + start + size, lanes]
            term = kernel[k : k + 1, lanes] * part
            total = term if total is None else total + term
        return silu(total).astype(BF16)

    @pl.when(step_index == 0)
    def _():
        turn = order_matrix(2 * CHUNK, reverse)
        small_turn = order_matrix(HALO, reverse)
        edge = norm_block(halo[...], gain[...])
        extended[0:HALO] = dot(small_turn, edge).astype(BF16)
        pairs = length // (2 * CHUNK)
        for pair in range(pairs):
            source = jnp.where(reverse == 1, pairs - 1 - pair, pair) * (2 * CHUNK)
            source = pl.multiple_of(source, 2 * CHUNK)
            piece = norm_block(rows[pl.ds(source, 2 * CHUNK), :], gain[...])
            start = HALO + pair * 2 * CHUNK
            extended[start : start + 2 * CHUNK] = dot(turn, piece).astype(BF16)
        normed_out[...] = extended[HALO:]
        side = lax.dot_general(
            extended[...], side_weight[...], (((1,), (1,)), ((), ())), preferred_element_type=F32
        )
        side = side.astype(BF16).astype(F32)
        buffer[:, 0 : 2 * state] = side[:, 0 : 2 * state]
        raw = side[HALO:, 2 * state :] + bias[...]
        step = jnp.maximum(raw, 0.0) + jnp.log1p(jnp.exp(-jnp.abs(raw)))
        change = step * (decay[...] * (-LOG2E))
        row = lax.broadcasted_iota(jnp.int32, (CHUNK, CHUNK), 0)
        column = lax.broadcasted_iota(jnp.int32, (CHUNK, CHUNK), 1)
        triangle = jnp.where(row >= column, 1.0, 0.0).astype(F32)
        before = jnp.zeros((1, heads), F32)
        totals = []
        befores = []
        for c in range(chunks):
            here = slice(c * CHUNK, (c + 1) * CHUNK)
            cumulative = jnp.dot(
                triangle, change[here], preferred_element_type=F32, precision=lax.Precision.HIGHEST
            )
            last = cumulative[CHUNK - 1 :, :]
            befores.append(before)
            totals.append(last)
            before = before + last
            moved = cumulative - jnp.log2(step[here])
            blank = jnp.zeros((CHUNK, 128 - 2 * heads), F32)
            flipped = jnp.concatenate([cumulative, moved, blank], axis=1).T
            cum_out[:, here] = flipped[0:heads]
            shifted_out[:, here] = flipped[heads : 2 * heads]
            shares[here, :] = high_low(jnp.exp2(last - cumulative) * step[here])
            reach_out[here, :] = high_low(jnp.exp2(cumulative))
        befores.append(before)
        zero_rows = jnp.zeros((HALO - chunks, heads), F32)
        shares[length:, :] = high_low(jnp.exp2(jnp.concatenate(totals + [zero_rows], axis=0)))
        zero_rows = jnp.zeros((HALO - chunks - 1, heads), F32)
        reach_out[length:, :] = high_low(jnp.exp2(jnp.concatenate(befores + [zero_rows], axis=0)))
        for c in range(chunks):
            start = c * CHUNK
            here = slice(start, start + CHUNK)
            in_part = filtered(side_taps, start, CHUNK, slice(0, state))
            b_out[here] = in_part
            turned[:, here] = in_part.astype(F32).T.astype(BF16)
            c_out[here] = filtered(side_taps, start, CHUNK, slice(state, 2 * state))

    buffer[...] = dot(extended[...], wide[...]).astype(BF16).astype(F32)
    wide_shares[...] = dot(shares[...], spread[...])
    sub = 64
    running[...] = jnp.zeros_like(running)
    for c in range(chunks):
        here = slice(c * CHUNK, (c + 1) * CHUNK)
        for lane in range(0, width, 256):
            lanes = slice(lane, lane + 256)
            weighted = []
            for start in range(c * CHUNK, (c + 1) * CHUNK, sub):
                piece = filtered(taps, start, sub, lanes)
                x_out[start : start + sub, lanes] = piece
                weighted.append(
                    (piece.astype(F32) * wide_shares[start : start + sub, lanes]).astype(BF16)
                )
            states = dot(turned[:, here], jnp.concatenate(weighted, axis=0))
            entering = running[:, lanes]
            local_out[c, :, lanes] = entering.astype(BF16)
            total = wide_shares[length + c : length + c + 1, lanes]
            running[:, lanes] = total * entering + states
    state_out[0:state, :] = running[...].astype(BF16)
    through = wide_shares[length : length + 1, :]
    for c in range(1, chunks):
        through = through * wide_shares[length + c : length + c + 1, :]
    high = through.astype(BF16)
    low = (through - high.astype(F32)).astype(BF16)
    tail = jnp.concatenate(
        [high.astype(F32), low.astype(F32), jnp.zeros((HALO - 2, width), F32)], axis=0
    )
    state_out[state:, :] = tail.astype(BF16)


def mid_kernel(
    normed, gate_weight, x, b, c_rows, cumulative, shifted, skip, spread, y_out, gate_out, scores
):
    step_index = pl.program_id(0)
    length = x.shape[0]
    chunks = length // CHUNK
    heads_here = cumulative.shape[0]
    head_dim = x.shape[1] // heads_here
    row = lax.broadcasted_iota(jnp.int32, (CHUNK, CHUNK), 0)
    column = lax.broadcasted_iota(jnp.int32, (CHUNK, CHUNK), 1)
    causal = row >= column
    lane = lax.broadcasted_iota(jnp.int32, (CHUNK, 2 * head_dim), 1)

    @pl.when(step_index == 0)
    def _():
        for c in range(chunks):
            here = slice(c * CHUNK, (c + 1) * CHUNK)
            scores[here, :] = lax.dot_general(
                c_rows[here, :], b[here, :], (((1,), (1,)), ((), ())), preferred_element_type=F32
            )

    gate_out[...] = dot(normed[...], gate_weight[...]).astype(BF16)
    skip_rows = jnp.broadcast_to(skip[...], (HALO, skip.shape[1]))
    skips = dot(high_low(skip_rows), spread[...])[0:1]
    for c in range(chunks):
        here = slice(c * CHUNK, (c + 1) * CHUNK)
        score = scores[here, :]
        blank = jnp.zeros((128 - heads_here, CHUNK), F32)
        columns = jnp.concatenate([cumulative[:, here], blank], axis=0).T
        for pair in range(heads_here // 2):
            lanes = slice(2 * pair * head_dim, (2 * pair + 2) * head_dim)
            parts = []
            for h in (2 * pair, 2 * pair + 1):
                gap = columns[:, h : h + 1] - shifted[h : h + 1, here]
                parts.append((score * jnp.exp2(jnp.where(causal, gap, -jnp.inf))).astype(BF16))
            values = x[here, lanes]
            zero = jnp.zeros_like(values)
            stacked = jnp.concatenate(
                [jnp.where(lane < head_dim, values, zero), jnp.where(lane < head_dim, zero, values)],
                axis=0,
            )
            within = dot(jnp.concatenate(parts, axis=1), stacked)
            y_out[here, lanes] = within + skips[:, lanes] * values.astype(F32)


def finish_kernel(plan, shard_rows, members, place_slot, last, info, *refs):
    count = len(members)
    rows, y_all, gate_all, c_all, reach_all, local_all = refs[:6]
    mine, other, partner, gain, spread = refs[6:11]
    rest = refs[11:]
    if plan:
        far_pieces = rest[: len(plan)]
        outs = rest[len(plan) : -4]
        normed, entering, weight, arrived = rest[-4:]
    else:
        weight = rest[0]
        outs = rest[1:-2]
        normed, entering = rest[-2:]
    reverse = info[REVERSE]
    inner = weight.shape[0]
    length = y_all.shape[0]
    state = mine.shape[0]
    block = 256
    fetches = []
    if plan:
        fetches = piece_copies(plan, shard_rows, info, far_pieces, weight, arrived, 0)
    for fetch in fetches:
        fetch.start()
    half = inner // 2
    upper = info[UPPER] == 1
    first = info[FIRST] == 1
    for start in range(0, inner, block):
        lanes = slice(start, start + block)
        inside = slice(start % half, start % half + block)
        pair = (other, mine) if start < half else (mine, other)
        full = jnp.where(upper, pair[0][:, inside], pair[1][:, inside])
        tail = partner[state:, lanes].astype(F32)
        through = tail[0:1] + tail[1:2]
        moved = (through * full.astype(F32) + partner[:state, lanes].astype(F32)).astype(BF16)
        entering[:, lanes] = jnp.where(first, full, moved)
    tail = dot(reach_all[length:, :], spread[...])
    index_row = lax.broadcasted_iota(jnp.int32, (HALO, 1), 0)
    turn = order_matrix(CHUNK, reverse)
    for i, member in enumerate(members):
        position = jnp.where(reverse == 1, length // CHUNK - 1 - member, member)
        here = pl.ds(pl.multiple_of(position * CHUNK, CHUNK), CHUNK)
        c_rows, reach, local = c_all[here, :], reach_all[here, :], local_all.at[position]
        before = jnp.sum(jnp.where(index_row == position, tail, 0.0), axis=0, keepdims=True)
        squares = jnp.zeros((CHUNK, 1), F32)
        gated = []
        for start in range(0, inner, block):
            lanes = slice(start, start + block)
            full = local[:, lanes].astype(F32) + before[:, lanes] * entering[:, lanes].astype(F32)
            carried = dot(c_rows, full.astype(BF16)) * dot(reach, spread[:, lanes])
            part = (y_all[here, lanes] + carried) * silu(gate_all[here, lanes].astype(F32))
            squares = squares + jnp.sum(part * part, axis=-1, keepdims=True)
            gated.append(part)
        inverse_rms = lax.rsqrt(squares * (1.0 / inner) + EPSILON)
        for index, start in enumerate(range(0, inner, block)):
            lanes = slice(start, start + block)
            piece = (gated[index] * inverse_rms * gain[:, lanes]).astype(BF16)
            normed[i * CHUNK : (i + 1) * CHUNK, lanes] = dot(turn, piece).astype(BF16)
    for fetch in fetches:
        fetch.wait()
    total = dot(normed[...], weight[...])
    place = info[place_slot]
    for i in range(count):
        term = total[i * CHUNK : (i + 1) * CHUNK]
        base = rows[members[i] * CHUNK : (members[i] + 1) * CHUNK].astype(F32) + term
        if last:
            earlier, sent, base_out = outs[i], outs[count + i], outs[2 * count + i]
            sent[...] = jnp.where(place == 1, earlier[...], term.astype(BF16))
            base_out[...] = base
        else:
            outs[i][...] = jnp.where(place == 0, term, 0.0).astype(BF16)
            outs[count + i][...] = jnp.where(place == 1, base, 0.0)


def kept(shape, dtype):
    return pltpu.VMEM(shape, dtype)


def near(*values):
    return tuple(pltpu.with_memory_space_constraint(v, pltpu.VMEM) for v in values)


def near_one(value):
    return near(value)[0]


def far(value):
    return pltpu.with_memory_space_constraint(value, pltpu.HBM)


def whole_block(shape):
    return pl.BlockSpec(shape, lambda *_: (0,) * len(shape))


def prep(info, rows, halo, gain, main, side, conv, bias, decay, spread, inner, state, resident=False):
    length, features = rows.shape
    heads = bias.shape[1]
    steps = inner // WIDTH
    chunks = length // CHUNK
    margin = conv.shape[1]
    side_width = 2 * state
    grid_spec = pltpu.PrefetchScalarGridSpec(
        num_scalar_prefetch=1,
        grid=(steps,),
        in_specs=[
            whole_block((length, features)),
            whole_block((HALO, features)),
            whole_block((1, features)),
            pl.BlockSpec((None, features, WIDTH), lambda j, _: (0, 0, steps + j)),
            pl.BlockSpec((None, side.shape[1], features), lambda j, _: (0, 0, 0)),
            pl.BlockSpec((None, margin, WIDTH), lambda j, _: (0, 0, j)),
            pl.BlockSpec((None, margin, side_width), lambda j, _: (0, 0, inner // side_width)),
            whole_block((1, heads)),
            whole_block((1, heads)),
            pl.BlockSpec((2 * heads, WIDTH), lambda j, _: (0, j)),
        ],
        out_specs=[
            whole_block((length, features)),
            pl.BlockSpec((length, WIDTH), lambda j, _: (0, j)),
            whole_block((length, state)),
            whole_block((length, state)),
            whole_block((heads, length)),
            whole_block((heads, length)),
            whole_block((length + HALO, 2 * heads)),
            pl.BlockSpec((chunks, state, WIDTH), lambda j, _: (0, 0, j)),
            pl.BlockSpec((state + HALO, WIDTH), lambda j, _: (0, j)),
        ],
        scratch_shapes=[
            pltpu.VMEM((length + HALO, features), BF16),
            pltpu.VMEM((length + HALO, WIDTH), F32),
            pltpu.VMEM((state, length), BF16),
            pltpu.VMEM((length + HALO, 2 * heads), BF16),
            pltpu.VMEM((length + HALO, WIDTH), F32),
            pltpu.VMEM((state, WIDTH), F32),
        ],
    )
    shape = jax.ShapeDtypeStruct
    return pl.pallas_call(
        prep_kernel,
        grid_spec=grid_spec,
        out_shape=[
            kept((length, features), BF16),
            kept((length, inner), BF16),
            kept((length, state), BF16),
            kept((length, state), BF16),
            kept((heads, length), F32),
            kept((heads, length), F32),
            kept((length + HALO, 2 * heads), BF16),
            kept((chunks, state, inner), BF16),
            shape((state + HALO, inner), BF16),
        ],
        compiler_params=pltpu.CompilerParams(
            vmem_limit_bytes=LIMIT, dimension_semantics=("arbitrary",)
        ),
        cost_estimate=pl.CostEstimate(
            flops=2 * length * features * inner, bytes_accessed=12 * 2**20, transcendentals=0
        ),
        name="prep",
    )(info, far(rows), halo, far(gain), (far, near_one)[resident](main), far(side), far(conv), far(conv), far(bias), far(decay), far(spread))


def mid(normed, main, x, b, c_rows, cumulative, shifted, skip, spread, inner, resident=False):
    length, features = normed.shape
    state = b.shape[1]
    steps = inner // WIDTH
    heads_here = cumulative.shape[0] // steps
    return pl.pallas_call(
        mid_kernel,
        grid=(steps,),
        in_specs=[
            whole_block((length, features)),
            pl.BlockSpec((None, features, WIDTH), lambda j: (0, 0, j)),
            pl.BlockSpec((length, WIDTH), lambda j: (0, j)),
            whole_block((length, state)),
            whole_block((length, state)),
            pl.BlockSpec((heads_here, length), lambda j: (j, 0)),
            pl.BlockSpec((heads_here, length), lambda j: (j, 0)),
            whole_block(skip.shape),
            pl.BlockSpec((spread.shape[0], WIDTH), lambda j: (0, j)),
        ],
        out_specs=[
            pl.BlockSpec((length, WIDTH), lambda j: (0, j)),
            pl.BlockSpec((length, WIDTH), lambda j: (0, j)),
        ],
        out_shape=[
            kept((length, inner), F32),
            kept((length, inner), BF16),
        ],
        scratch_shapes=[pltpu.VMEM((length, CHUNK), F32)],
        compiler_params=pltpu.CompilerParams(
            vmem_limit_bytes=LIMIT, dimension_semantics=("arbitrary",)
        ),
        cost_estimate=pl.CostEstimate(
            flops=2 * length * features * inner, bytes_accessed=12 * 2**20, transcendentals=0
        ),
        name="mid",
    )(*near(normed), (far, near_one)[resident](main), *near(x, b, c_rows, cumulative, shifted), far(skip), far(spread))


def finish(
    members, place_slot, last, info, rows, y, gate, c_rows, reach, local, state_parts,
    gain, spread, pieces, earlier,
):
    features = rows.shape[1]
    length, inner = y.shape
    state = c_rows.shape[1]
    mine, other, partner = state_parts
    resident = not isinstance(pieces, list)
    plan = [] if resident else [ranges for _, ranges in pieces]
    shard_rows = inner // lax.axis_size("seq")
    count = len(members)
    whole = pl.BlockSpec(memory_space=pltpu.VMEM)
    in_specs = [pl.BlockSpec(memory_space=pltpu.SMEM)]
    in_specs += [whole] * 11
    operands = [rows, *near(y, gate, c_rows, reach, local)]
    in_specs += [whole] if resident else [pl.BlockSpec(memory_space=pl.ANY)] * len(pieces)
    in_specs += [whole] * len(earlier)
    operands += [mine, other, partner, far(gain), far(spread)]
    operands += [*near(pieces)] if resident else [far(piece) for piece, _ in pieces]
    operands += list(earlier)
    scratch = [pltpu.VMEM((count * CHUNK, inner), BF16), pltpu.VMEM((state, inner), BF16)]
    if not resident:
        scratch.append(pltpu.VMEM((inner, features), BF16))
        scratch.append(pltpu.SemaphoreType.DMA((sum(len(ranges) for ranges in plan),)))
    shape = (CHUNK, features)
    return pl.pallas_call(
        functools.partial(finish_kernel, plan, shard_rows, members, place_slot, last),
        in_specs=in_specs,
        out_specs=[whole] * (2 * count),
        scratch_shapes=scratch,
        out_shape=[jax.ShapeDtypeStruct(shape, BF16)] * count + [kept(shape, F32)] * count,
        compiler_params=pltpu.CompilerParams(
            vmem_limit_bytes=LIMIT
        ),
        cost_estimate=pl.CostEstimate(
            flops=2 * count * CHUNK * features * inner, bytes_accessed=8 * 2**20, transcendentals=0
        ),
        name="finish",
    )(info, *operands)


def hold_kernel(plan, shard_rows, info, *refs):
    main = refs[1]
    far_pieces = refs[2 : 2 + len(plan)]
    main_out, weight_out, arrived = refs[2 + len(plan) :]
    parts = 4
    rows = main.shape[1] // parts
    copies = []
    for i in range(parts):
        here = pl.ds(i * rows, rows)
        copies.append(
            pltpu.make_async_copy(main.at[0, here], main_out.at[0, here], arrived.at[len(copies)])
        )
    copies += piece_copies(plan, shard_rows, info, far_pieces, weight_out, arrived, len(copies))
    for copy in copies:
        copy.start()
    for copy in copies:
        copy.wait()


def hold(info, trigger, main, pieces, inner):
    plan = [ranges for _, ranges in pieces]
    features = main.shape[1]
    anywhere = pl.BlockSpec(memory_space=pl.ANY)
    whole = pl.BlockSpec(memory_space=pltpu.VMEM)
    count = 4 + sum(len(ranges) for ranges in plan)
    return pl.pallas_call(
        functools.partial(hold_kernel, plan, inner // lax.axis_size("seq")),
        in_specs=[pl.BlockSpec(memory_space=pltpu.SMEM)] + [anywhere] * (2 + len(pieces)),
        out_specs=[whole, whole],
        out_shape=[kept(main.shape, BF16), kept((inner, features), BF16)],
        scratch_shapes=[pltpu.SemaphoreType.DMA((count,))],
        compiler_params=pltpu.CompilerParams(vmem_limit_bytes=SMALL),
        cost_estimate=pl.CostEstimate(flops=10**6, bytes_accessed=24 * 2**20, transcendentals=0),
        name="hold",
    )(info, far(trigger), far(main), *[far(piece) for piece, _ in pieces])


def piece_copies(plan, shard_rows, info, far_pieces, weight, arrived, base):
    copies = []
    for piece, ranges in zip(far_pieces, plan):
        for mask, source, offset, extent in ranges:
            place = 0
            if mask is not None:
                place = pl.multiple_of((info[SEQ] ^ mask) * shard_rows + offset, 16)
            copies.append(
                pltpu.make_async_copy(
                    piece.at[source : source + extent],
                    weight.at[pl.ds(place, extent)],
                    arrived.at[base + len(copies)],
                )
            )
    return copies


def stack_kernel(counts, *refs):
    sources, outs = refs[: -len(counts)], refs[-len(counts) :]
    position = 0
    for out, count in zip(outs, counts):
        start = 0
        for source in sources[position : position + count]:
            out[start : start + source.shape[0]] = source[...]
            start += source.shape[0]
        position += count


def stacked(groups):
    operands = []
    specs = []
    out_shape = []
    for group in groups:
        total = 0
        for value, index, rows in group:
            operands.append(value)
            specs.append(pl.BlockSpec((rows, value.shape[1]), lambda j, index=index: (index, 0)))
            total += rows
        out_shape.append(pltpu.HBM((total, group[0][0].shape[1]), BF16))
    return pl.pallas_call(
        functools.partial(stack_kernel, [len(group) for group in groups]),
        grid=(1,),
        in_specs=specs,
        out_specs=[whole_block(shape.shape) for shape in out_shape],
        out_shape=out_shape,
        compiler_params=pltpu.CompilerParams(vmem_limit_bytes=16 * 2**20),
        cost_estimate=pl.CostEstimate(flops=10**6, bytes_accessed=10**6, transcendentals=0),
        name="stack",
    )(*[far(value) for value in operands])


def seq_swap(value, mask):
    count = lax.axis_size("seq")
    return lax.ppermute(value, "seq", [(i, i ^ mask) for i in range(count)])


def split_state(packed):
    state = packed.shape[0] - HALO
    values = packed[:state].astype(F32)
    tail = packed[state:].astype(F32)
    return values, tail[0:1] + tail[1:2]


def joined_state(values, through):
    high = through.astype(BF16)
    low = (through - high.astype(F32)).astype(BF16)
    rest = jnp.zeros((HALO - 2, through.shape[1]), F32)
    tail = jnp.concatenate([high.astype(F32), low.astype(F32), rest], axis=0)
    return values.astype(BF16), tail.astype(BF16)


def after(earlier, later):
    return later[1] * earlier[0] + later[0], earlier[1] * later[1]


def chosen(condition, first, second):
    return tuple(jnp.where(condition, a, b) for a, b in zip(first, second))


def pair_kernel(info, mine, partner, out):
    half = out.shape[1]
    first = info[FIRST] == 1
    state = out.shape[0] - HALO
    for start in range(0, half, 256):
        place = pl.multiple_of(info[UPPER] * half + start, 256)
        one = split_state(mine[:, pl.ds(place, 256)])
        two = split_state(partner[:, pl.ds(place, 256)])
        total = after(chosen(first, one, two), chosen(first, two, one))
        out[:state, start : start + 256], out[state:, start : start + 256] = joined_state(*total)


def merge_kernel(group, slot, has_entering, last, info, *refs):
    members = refs[: 2**group]
    entering_out = refs[2**group + has_entering]
    rank = info[slot]
    state, half = entering_out.shape
    for start in range(0, half, 256):
        lanes = slice(start, start + 256)
        values = [split_state(member[:, lanes]) for member in members]
        before = (jnp.zeros((state, 256), F32), jnp.ones((1, 256), F32))
        whole = before
        for place in range(2**group):
            value = values[0]
            for code in range(1, 2**group):
                value = chosen((rank ^ code) == place, values[code], value)
            if place < 2**group - 1:
                before = chosen(place < rank, after(before, value), before)
            if not last:
                whole = after(whole, value)
        if has_entering:
            inside = refs[2**group][:, lanes].astype(F32)
            through = jnp.ones((1, 256), F32)
            before = after(before, (inside, through))
        entering_out[:, lanes] = before[0].astype(BF16)
        if not last:
            out = refs[-1]
            out[:state, lanes], out[state:, lanes] = joined_state(*whole)


def small_call(kernel, name, out_shape, info, *operands):
    return pl.pallas_call(
        kernel,
        in_specs=[pl.BlockSpec(memory_space=pltpu.SMEM)] + [whole_block(v.shape) for v in operands],
        out_specs=[whole_block(v.shape) for v in out_shape],
        out_shape=out_shape,
        compiler_params=pltpu.CompilerParams(vmem_limit_bytes=SMALL),
        cost_estimate=pl.CostEstimate(flops=10**6, bytes_accessed=10**6, transcendentals=0),
        name=name,
    )(info, *operands)


def settle_kernel(place, info, base, sent, other, *rest):
    section = info[place]
    rows = (base[...] + other[...].astype(F32)).astype(BF16)
    rows = jnp.where(section == 1, sent[...], rows)
    rest[-1][...] = jnp.where(section == 0, other[...], rows)


def settle(index, chunks, place, info, base, sent, other, finished):
    features = base.shape[1]
    length = chunks * CHUNK
    out_block = pl.BlockSpec((None, CHUNK, features), lambda j: (0, index, 0))
    passed = [] if finished is None else [finished]
    return pl.pallas_call(
        functools.partial(settle_kernel, place),
        grid=(1,),
        in_specs=[pl.BlockSpec(memory_space=pltpu.SMEM)]
        + [whole_block((CHUNK, features))] * 3
        + [pl.BlockSpec(memory_space=pl.ANY)] * len(passed),
        out_specs=out_block,
        out_shape=jax.ShapeDtypeStruct((1, length, features), BF16),
        input_output_aliases={4: 0} if passed else {},
        compiler_params=pltpu.CompilerParams(vmem_limit_bytes=SMALL),
        cost_estimate=pl.CostEstimate(flops=10**6, bytes_accessed=10**6, transcendentals=0),
        name="settle",
    )(info, base, sent, other, *passed)


def stages_of(seq_count):
    bits = seq_count.bit_length() - 1
    found = []
    bit = 1
    while bit < bits:
        group = min(2, bits - bit)
        found.append((bit, group))
        bit += group
    return found


def entering_state(packed, info, sections, seq_count, meanwhile):
    section_count = lax.axis_size("section")
    stages = stages_of(seq_count)

    def swap(value, mask):
        pairs = [
            (i * section_count + s, (i ^ mask) * section_count + s)
            for s in sections
            for i in range(seq_count)
        ]
        return lax.ppermute(value, ("seq", "section"), pairs)

    def forward(value, mask, low_bit):
        pairs = []
        for s in sections:
            for i in range(seq_count):
                later = (i ^ mask) >> low_bit > i >> low_bit
                if later == (s % 2 == 0):
                    pairs.append((i * section_count + s, (i ^ mask) * section_count + s))
        return lax.ppermute(value, ("seq", "section"), pairs)

    depth, inner = packed.shape
    half = jax.ShapeDtypeStruct((depth, inner // 2), BF16)
    states = jax.ShapeDtypeStruct((depth - HALO, inner // 2), BF16)
    partner = swap(packed, 1)
    (total,) = small_call(pair_kernel, "pair", [half], info, packed, partner)
    done = meanwhile(total)
    info, _ = lax.optimization_barrier((info, done[0]))
    entering = []
    for index, (bit, group) in enumerate(stages):
        last = index + 1 == len(stages)
        members = [total]
        for code in range(1, 2**group):
            mask = code << bit
            members.append(forward(total, mask, bit) if last else swap(total, mask))
        kernel = functools.partial(merge_kernel, group, RANKS + index, len(entering), last)
        shapes = [states] if last else [states, half]
        results = small_call(kernel, "merge", shapes, info, *members, *entering)
        entering = [results[0]]
        total = results[-1]
    return (entering[0], swap(entering[0], 1), partner), done


def per_device(
    tokens,
    input_gain,
    main_weight,
    side_weight,
    conv_kernel,
    step_bias,
    decay_rate,
    skip_gain,
    output_gain,
    output_weight,
):
    length, features = tokens.shape
    inner = main_weight.shape[2] // 2
    heads = decay_rate.shape[1]
    state = (side_weight.shape[2] - heads) // 2
    head_dim = inner // heads
    chunks = length // CHUNK
    seq_count = lax.axis_size("seq")
    section_count = lax.axis_size("section")
    section_index = lax.axis_index("section")
    seq_index = lax.axis_index("seq")
    reverse = section_index % 2
    shard = output_weight[0]
    expand = np.repeat(np.eye(heads, dtype=np.float32), head_dim, axis=1)
    spread = jnp.asarray(np.concatenate([expand, expand], axis=0), BF16)
    upper = seq_index % 2
    facts = [reverse, upper, (upper == reverse).astype(jnp.int32), seq_index]
    for bit, group in stages_of(seq_count):
        position = (seq_index >> bit) % 2**group
        facts.append(jnp.where(reverse == 1, 2**group - 1 - position, position))
    places = len(facts)
    rounds = section_count // 2
    for round_index in range(rounds):
        facts.append(section_index - 2 * round_index)
    info = jnp.stack([fact.astype(jnp.int32) for fact in facts])
    order = [chunks - 1, 0] + list(range(1, chunks - 1))

    def edges(first_rows, last_rows, first_wanted, sources, targets):
        pairs = []
        for source, target in zip(sources, targets):
            for i in range(seq_count):
                beside = i + 1 if target % 2 == 0 else i - 1
                if 0 <= beside < seq_count:
                    pairs.append((i * section_count + source, beside * section_count + target))
        value = jnp.where(first_wanted, first_rows, last_rows)
        return lax.ppermute(value, ("seq", "section"), pairs)

    current = tokens
    halo = edges(tokens[:HALO], tokens[length - HALO :], reverse == 1, (0, 1), (0, 1))
    previous = None
    shards = None
    if seq_count == 8:
        halo, shard = lax.optimization_barrier((halo, shard))
        shards = [shard, seq_swap(shard, 2), seq_swap(shard, 4)]
        pieces = None
    else:
        whole = lax.all_gather(shard, "seq", axis=0, tiled=True)
        pieces = [(whole, [(None, 0, 0, inner)])]
    main = main_weight
    for round_index in range(rounds):
        active = (2 * round_index, 2 * round_index + 1)
        normed, x, b, c_rows, cumulative, shifted, reach, local, packed = prep(
            info,
            current,
            halo,
            input_gain,
            main,
            jnp.swapaxes(side_weight, 1, 2),
            conv_kernel,
            step_bias,
            decay_rate,
            spread,
            inner,
            state,
            round_index > 0,
        )
        early = round_index == 0 and shards
        if early:
            packed, *shards[1:] = lax.optimization_barrier((packed, *shards[1:]))

        def meanwhile(total, normed=normed):
            nonlocal pieces
            if early:
                *parts, _ = lax.optimization_barrier((*shards, total))
                rows = parts[0].shape[0] // 2
                up, down, three = stacked(
                    [
                        [(parts[2], 0, rows)],
                        [(parts[1], 1, rows)],
                        [(part, 0, 2 * rows) for part in parts],
                    ]
                )
                halves = [seq_swap(up, 2), seq_swap(down, 4)]
                swapped = seq_swap(three, 1)
            ready, _ = lax.optimization_barrier((normed, total))
            y, gate = mid(
                ready, main, x, b, c_rows, cumulative, shifted, skip_gain, spread, inner,
                round_index > 0,
            )
            if early:
                *halves, _ = lax.optimization_barrier((*halves, y))
                rows = halves[0].shape[0]
                (joined,) = stacked([[(half, 0, rows) for half in halves]])
                diagonal = seq_swap(joined, 1)
                pieces = [(value, [(mask, 0, 0, 2 * rows)]) for value, mask in zip(shards, (0, 2, 4))]
                pieces += [(half, [(6, 0, i * rows, rows)]) for i, half in enumerate(halves)]
                pieces.append((swapped, [(m, i * 2 * rows, 0, 2 * rows) for i, m in enumerate((1, 3, 5))]))
                pieces.append((diagonal, [(7, 0, 0, 2 * rows)]))
            return y, gate

        state_parts, (y, gate) = entering_state(packed, info, active, seq_count, meanwhile)
        last_round = round_index + 1 == rounds
        low, high = active
        place = section_index - low
        terms = {}
        bases = {}
        for members in (order[: chunks // 2], order[chunks // 2 :]):
            outs = finish(
                tuple(members), places if last_round else places + round_index, last_round, info,
                current, y, gate, c_rows, reach, local, state_parts, output_gain, spread, pieces,
                [previous[member] for member in members] if last_round else [],
            )
            for i, member in enumerate(members):
                terms[member] = outs[i]
                bases[member] = outs[len(members) + i]
        if last_round:
            break
        received = []
        values = []
        direct = None
        for step in range(chunks + 2 * SKEW - 1):
            pairs = [(low + hop, low + hop + 1) for hop in range(3) if 0 <= step - hop * SKEW < chunks]
            value = terms[order[step]] if step < chunks else None
            if step >= SKEW:
                passed = received[step - SKEW]
                if step - SKEW < chunks:
                    total = bases[order[step - SKEW]] + passed.astype(F32)
                    total = total if value is None else total + value.astype(F32)
                    passed = total.astype(BF16)
                value = passed
            values.append(value)
            received.append(lax.ppermute(value, "section", pairs))
            if step == chunks + SKEW - 1:
                direct = lax.ppermute(value, "section", [(low + 1, low + 3)])
        received.append(direct)
        trigger, _ = lax.optimization_barrier((values[chunks + SKEW - 1], received[2 * SKEW]))
        main, pieces = hold(info, trigger, main_weight, pieces, inner)
        last_rows = jnp.where(place == 3, received[2 * SKEW], received[SKEW])[CHUNK - HALO :]
        first_rows = jnp.where(place == 3, received[2 * SKEW + 1], received[SKEW + 1])[:HALO]
        halo = edges(first_rows, last_rows, reverse == 1, (low + 2, high + 2), (low + 2, high + 2))
        received[-1], received[-2], halo = lax.optimization_barrier((received[-1], received[-2], halo))
        layer_rows = [None] * chunks
        next_rows = [None] * chunks
        for step, index in enumerate(order):
            layer_rows[index] = values[step + SKEW]
            next_rows[index] = jnp.where(place == 3, received[step + 2 * SKEW], received[step + SKEW])
        previous = layer_rows
        current = jnp.concatenate(next_rows, axis=0)
    finished = None
    for index in order:
        other = lax.ppermute(terms[index], "section", [(low, high), (high, low), (1, 0)])
        finished = settle(index, chunks, places, info, bases[index], terms[index], other, finished)
    return finished


def solution(mesh):
    placed = (
        P("seq", None),
        P("section", None),
        P("section", None, None),
        P("section", None, None),
        P("section", None, None),
        P("section", None),
        P("section", None),
        P("section", None),
        P("section", None),
        P("section", "seq", None),
    )
    return jax.shard_map(
        per_device, mesh=mesh, in_specs=placed, out_specs=P("section", "seq", None), check_vma=False
    )
```

```python
import functools

import jax
import jax.numpy as jnp
import numpy as np
from jax import lax
from jax.experimental import pallas as pl
from jax.experimental.pallas import tpu as pltpu
from jax.sharding import PartitionSpec as P

EPSILON = 1e-05
CHUNK = 128
WIDTH = 2048
HALO = 16
EDGE = 32
LIMIT = 28 * 2**20
SMALL = 8 * 2**20
SKEW = 2
REVERSE, UPPER, FIRST, SEQ, RANKS = 0, 1, 2, 3, 4
LOG2E = 1.4426950408889634
F32 = jnp.float32
BF16 = jnp.bfloat16


def silu(value):
    half = 0.5 * value
    return half + half * jnp.tanh(half)


def dot(left, right):
    return jnp.dot(left, right, preferred_element_type=F32)


def time_of(index):
    row = index & (CHUNK - 1)
    return (index - row) + ((row & 7) << 4) + (row >> 3)


def order_matrix(size, reverse, back=False):
    place = lax.broadcasted_iota(jnp.int32, (size, size), 1 if back else 0)
    token = lax.broadcasted_iota(jnp.int32, (size, size), 0 if back else 1)
    time = time_of(place)
    target = jnp.where(reverse == 1, size - 1 - time, time)
    return jnp.where(token == target, 1.0, 0.0).astype(BF16)


def edge_matrix(margin, reverse):
    row = lax.broadcasted_iota(jnp.int32, (EDGE, HALO), 0)
    column = lax.broadcasted_iota(jnp.int32, (EDGE, HALO), 1)
    step = (row >> 3) - (EDGE // 8 - margin)
    source = jnp.where(reverse == 1, margin - 1 - step, HALO - margin + step)
    wanted = (step >= 0) & ((row & 7) == 7) & (column == source)
    return jnp.where(wanted, 1.0, 0.0).astype(BF16)


def high_low(value):
    high = value.astype(BF16)
    low = (value - high.astype(F32)).astype(BF16)
    return jnp.concatenate([high, low], axis=1)


def norm_block(values, gain_row):
    widened = values.astype(F32)
    inverse_rms = lax.rsqrt(jnp.mean(widened * widened, axis=-1, keepdims=True) + EPSILON)
    return (widened * inverse_rms * gain_row).astype(BF16)


def prep_kernel(
    info,
    rows,
    halo,
    gain,
    wide,
    side_weight,
    taps,
    side_taps,
    bias,
    decay,
    spread,
    normed_out,
    x_out,
    b_out,
    c_out,
    cum_out,
    shifted_out,
    reach_out,
    local_out,
    state_out,
    extended,
    buffer,
    turned,
    shares,
    wide_shares,
    running,
):
    step_index = pl.program_id(0)
    reverse = info[REVERSE]
    length = rows.shape[0]
    heads = bias.shape[1]
    state = b_out.shape[1]
    chunks = length // CHUNK
    margin = taps.shape[0] - 1
    width = wide.shape[1]

    def filtered(kernel, c, lanes):
        start = EDGE + c * CHUNK
        tail = 8 * margin
        ending = buffer[start + CHUNK - tail : start + CHUNK, lanes]
        previous = buffer[start - tail : start, lanes]
        leading = lax.broadcasted_iota(jnp.int32, ending.shape, 0) & 7 == 0
        entry = jnp.where(
            leading, pltpu.roll(previous, tail - 7, axis=0), pltpu.roll(ending, 1, axis=0)
        )
        region = jnp.concatenate([entry, buffer[start : start + CHUNK, lanes]], axis=0)
        total = None
        for k in range(margin + 1):
            term = kernel[k : k + 1, lanes] * region[8 * k : 8 * k + CHUNK]
            total = term if total is None else total + term
        return silu(total).astype(BF16)

    @pl.when(step_index == 0)
    def _():
        turn = order_matrix(2 * CHUNK, reverse)
        edge = norm_block(halo[...], gain[...])
        extended[0:EDGE] = dot(edge_matrix(margin, reverse), edge).astype(BF16)
        pairs = length // (2 * CHUNK)
        for pair in range(pairs):
            source = jnp.where(reverse == 1, pairs - 1 - pair, pair) * (2 * CHUNK)
            source = pl.multiple_of(source, 2 * CHUNK)
            piece = norm_block(rows[pl.ds(source, 2 * CHUNK), :], gain[...])
            start = EDGE + pair * 2 * CHUNK
            extended[start : start + 2 * CHUNK] = dot(turn, piece).astype(BF16)
        normed_out[...] = extended[EDGE:]
        side = lax.dot_general(
            extended[...], side_weight[...], (((1,), (1,)), ((), ())), preferred_element_type=F32
        )
        side = side.astype(BF16).astype(F32)
        buffer[:, 0 : 2 * state] = side[:, 0 : 2 * state]
        raw = side[EDGE:, 2 * state :] + bias[...]
        step = jnp.maximum(raw, 0.0) + jnp.log1p(jnp.exp(-jnp.abs(raw)))
        change = step * (decay[...] * (-LOG2E))
        row = lax.broadcasted_iota(jnp.int32, (CHUNK, CHUNK), 0)
        column = lax.broadcasted_iota(jnp.int32, (CHUNK, CHUNK), 1)
        triangle = jnp.where(time_of(row) >= time_of(column), 1.0, 0.0).astype(F32)
        before = jnp.zeros((1, heads), F32)
        totals = []
        befores = []
        for c in range(chunks):
            here = slice(c * CHUNK, (c + 1) * CHUNK)
            cumulative = jnp.dot(
                triangle, change[here], preferred_element_type=F32, precision=lax.Precision.HIGHEST
            )
            last = cumulative[CHUNK - 1 :, :]
            befores.append(before)
            totals.append(last)
            before = before + last
            moved = cumulative - jnp.log2(step[here])
            blank = jnp.zeros((CHUNK, 128 - 2 * heads), F32)
            flipped = jnp.concatenate([cumulative, moved, blank], axis=1).T
            cum_out[:, here] = flipped[0:heads]
            shifted_out[:, here] = flipped[heads : 2 * heads]
            shares[here, :] = high_low(jnp.exp2(last - cumulative) * step[here])
            reach_out[here, :] = high_low(jnp.exp2(cumulative))
        befores.append(before)
        zero_rows = jnp.zeros((HALO - chunks, heads), F32)
        shares[length:, :] = high_low(jnp.exp2(jnp.concatenate(totals + [zero_rows], axis=0)))
        zero_rows = jnp.zeros((HALO - chunks - 1, heads), F32)
        reach_out[length:, :] = high_low(jnp.exp2(jnp.concatenate(befores + [zero_rows], axis=0)))
        for c in range(chunks):
            start = c * CHUNK
            here = slice(start, start + CHUNK)
            in_part = filtered(side_taps, c, slice(0, state))
            b_out[here] = in_part
            flipped = in_part.astype(F32).T.astype(BF16)
            blank = jnp.zeros_like(flipped)
            turned[0:state, here] = flipped if c % 2 == 0 else blank
            turned[state:, here] = blank if c % 2 == 0 else flipped
            c_out[here] = filtered(side_taps, c, slice(state, 2 * state))

    buffer[...] = dot(extended[...], wide[...]).astype(BF16).astype(F32)
    wide_shares[...] = dot(shares[...], spread[...])
    running[...] = jnp.zeros_like(running)
    for pair in range(chunks // 2):
        both = slice(2 * pair * CHUNK, (2 * pair + 2) * CHUNK)
        for lane in range(0, width, 256):
            lanes = slice(lane, lane + 256)
            columns = []
            for inside in (slice(lane, lane + 128), slice(lane + 128, lane + 256)):
                weighted = []
                for c in (2 * pair, 2 * pair + 1):
                    here = slice(c * CHUNK, (c + 1) * CHUNK)
                    piece = filtered(taps, c, inside)
                    x_out[here, inside] = piece
                    weighted.append((piece.astype(F32) * wide_shares[here, inside]).astype(BF16))
                columns.append(jnp.concatenate(weighted, axis=0))
            states = dot(turned[:, both], jnp.concatenate(columns, axis=1))
            entering = running[:, lanes]
            for i, c in enumerate((2 * pair, 2 * pair + 1)):
                local_out[c, :, lanes] = entering.astype(BF16)
                total = wide_shares[length + c : length + c + 1, lanes]
                entering = total * entering + states[i * state : (i + 1) * state]
            running[:, lanes] = entering
    state_out[0:state, :] = running[...].astype(BF16)
    through = wide_shares[length : length + 1, :]
    for c in range(1, chunks):
        through = through * wide_shares[length + c : length + c + 1, :]
    high = through.astype(BF16)
    low = (through - high.astype(F32)).astype(BF16)
    tail = jnp.concatenate(
        [high.astype(F32), low.astype(F32), jnp.zeros((HALO - 2, width), F32)], axis=0
    )
    state_out[state:, :] = tail.astype(BF16)


def mid_kernel(
    normed, gate_weight, x, b, c_rows, cumulative, shifted, skip, spread, y_out, gate_out, scores
):
    step_index = pl.program_id(0)
    length = x.shape[0]
    chunks = length // CHUNK
    heads_here = cumulative.shape[0]
    head_dim = x.shape[1] // heads_here
    row = lax.broadcasted_iota(jnp.int32, (CHUNK, CHUNK), 0)
    column = lax.broadcasted_iota(jnp.int32, (CHUNK, CHUNK), 1)
    causal = time_of(row) >= time_of(column)
    lane = lax.broadcasted_iota(jnp.int32, (CHUNK, 2 * head_dim), 1)

    @pl.when(step_index == 0)
    def _():
        for c in range(chunks):
            here = slice(c * CHUNK, (c + 1) * CHUNK)
            scores[here, :] = lax.dot_general(
                c_rows[here, :], b[here, :], (((1,), (1,)), ((), ())), preferred_element_type=F32
            )

    gate_out[...] = dot(normed[...], gate_weight[...]).astype(BF16)
    skip_rows = jnp.broadcast_to(skip[...], (HALO, skip.shape[1]))
    skips = dot(high_low(skip_rows), spread[...])[0:1]
    for c in range(chunks):
        here = slice(c * CHUNK, (c + 1) * CHUNK)
        score = scores[here, :]
        blank = jnp.zeros((128 - heads_here, CHUNK), F32)
        columns = jnp.concatenate([cumulative[:, here], blank], axis=0).T
        for pair in range(heads_here // 2):
            lanes = slice(2 * pair * head_dim, (2 * pair + 2) * head_dim)
            parts = []
            for h in (2 * pair, 2 * pair + 1):
                gap = columns[:, h : h + 1] - shifted[h : h + 1, here]
                parts.append((score * jnp.exp2(jnp.where(causal, gap, -jnp.inf))).astype(BF16))
            values = x[here, lanes]
            zero = jnp.zeros_like(values)
            stacked = jnp.concatenate(
                [jnp.where(lane < head_dim, values, zero), jnp.where(lane < head_dim, zero, values)],
                axis=0,
            )
            within = dot(jnp.concatenate(parts, axis=1), stacked)
            y_out[here, lanes] = within + skips[:, lanes] * values.astype(F32)


def finish_kernel(plan, shard_rows, members, place_slot, last, info, *refs):
    count = len(members)
    rows, y_all, gate_all, c_all, reach_all, local_all = refs[:6]
    mine, other, partner, gain, spread = refs[6:11]
    rest = refs[11:]
    if plan:
        far_pieces = rest[: len(plan)]
        outs = rest[len(plan) : -4]
        normed, entering, weight, arrived = rest[-4:]
    else:
        weight = rest[0]
        outs = rest[1:-2]
        normed, entering = rest[-2:]
    reverse = info[REVERSE]
    inner = weight.shape[0]
    length = y_all.shape[0]
    state = mine.shape[0]
    block = 256
    fetches = []
    if plan:
        fetches = piece_copies(plan, shard_rows, info, far_pieces, weight, arrived, 0)
    for fetch in fetches:
        fetch.start()
    half = inner // 2
    upper = info[UPPER] == 1
    first = info[FIRST] == 1
    for start in range(0, inner, block):
        lanes = slice(start, start + block)
        inside = slice(start % half, start % half + block)
        pair = (other, mine) if start < half else (mine, other)
        full = jnp.where(upper, pair[0][:, inside], pair[1][:, inside])
        tail = partner[state:, lanes].astype(F32)
        through = tail[0:1] + tail[1:2]
        moved = (through * full.astype(F32) + partner[:state, lanes].astype(F32)).astype(BF16)
        entering[:, lanes] = jnp.where(first, full, moved)
    tail = dot(reach_all[length:, :], spread[...])
    index_row = lax.broadcasted_iota(jnp.int32, (HALO, 1), 0)
    turn = order_matrix(CHUNK, reverse, back=True)
    for i, member in enumerate(members):
        position = jnp.where(reverse == 1, length // CHUNK - 1 - member, member)
        here = pl.ds(pl.multiple_of(position * CHUNK, CHUNK), CHUNK)
        c_rows, reach, local = c_all[here, :], reach_all[here, :], local_all.at[position]
        before = jnp.sum(jnp.where(index_row == position, tail, 0.0), axis=0, keepdims=True)
        squares = jnp.zeros((CHUNK, 1), F32)
        gated = []
        for start in range(0, inner, block):
            lanes = slice(start, start + block)
            full = local[:, lanes].astype(F32) + before[:, lanes] * entering[:, lanes].astype(F32)
            carried = dot(c_rows, full.astype(BF16)) * dot(reach, spread[:, lanes])
            part = (y_all[here, lanes] + carried) * silu(gate_all[here, lanes].astype(F32))
            squares = squares + jnp.sum(part * part, axis=-1, keepdims=True)
            gated.append(part)
        inverse_rms = lax.rsqrt(squares * (1.0 / inner) + EPSILON)
        for index, start in enumerate(range(0, inner, block)):
            lanes = slice(start, start + block)
            piece = (gated[index] * inverse_rms * gain[:, lanes]).astype(BF16)
            normed[i * CHUNK : (i + 1) * CHUNK, lanes] = dot(turn, piece).astype(BF16)
    for fetch in fetches:
        fetch.wait()
    total = dot(normed[...], weight[...])
    place = info[place_slot]
    for i in range(count):
        term = total[i * CHUNK : (i + 1) * CHUNK]
        base = rows[members[i] * CHUNK : (members[i] + 1) * CHUNK].astype(F32) + term
        if last:
            earlier, sent, base_out = outs[i], outs[count + i], outs[2 * count + i]
            sent[...] = jnp.where(place == 1, earlier[...], term.astype(BF16))
            base_out[...] = base
        else:
            outs[i][...] = jnp.where(place == 0, term, 0.0).astype(BF16)
            outs[count + i][...] = jnp.where(place == 1, base, 0.0)


def kept(shape, dtype):
    return pltpu.VMEM(shape, dtype)


def near(*values):
    return tuple(pltpu.with_memory_space_constraint(v, pltpu.VMEM) for v in values)


def near_one(value):
    return near(value)[0]


def far(value):
    return pltpu.with_memory_space_constraint(value, pltpu.HBM)


def whole_block(shape):
    return pl.BlockSpec(shape, lambda *_: (0,) * len(shape))


def prep(info, rows, halo, gain, main, side, conv, bias, decay, spread, inner, state, resident=False):
    length, features = rows.shape
    heads = bias.shape[1]
    steps = inner // WIDTH
    chunks = length // CHUNK
    margin = conv.shape[1]
    side_width = 2 * state
    grid_spec = pltpu.PrefetchScalarGridSpec(
        num_scalar_prefetch=1,
        grid=(steps,),
        in_specs=[
            whole_block((length, features)),
            whole_block((HALO, features)),
            whole_block((1, features)),
            pl.BlockSpec((None, features, WIDTH), lambda j, _: (0, 0, steps + j)),
            pl.BlockSpec((None, side.shape[1], features), lambda j, _: (0, 0, 0)),
            pl.BlockSpec((None, margin, WIDTH), lambda j, _: (0, 0, j)),
            pl.BlockSpec((None, margin, side_width), lambda j, _: (0, 0, inner // side_width)),
            whole_block((1, heads)),
            whole_block((1, heads)),
            pl.BlockSpec((2 * heads, WIDTH), lambda j, _: (0, j)),
        ],
        out_specs=[
            whole_block((length, features)),
            pl.BlockSpec((length, WIDTH), lambda j, _: (0, j)),
            whole_block((length, state)),
            whole_block((length, state)),
            whole_block((heads, length)),
            whole_block((heads, length)),
            whole_block((length + HALO, 2 * heads)),
            pl.BlockSpec((chunks, state, WIDTH), lambda j, _: (0, 0, j)),
            pl.BlockSpec((state + HALO, WIDTH), lambda j, _: (0, j)),
        ],
        scratch_shapes=[
            pltpu.VMEM((length + EDGE, features), BF16),
            pltpu.VMEM((length + EDGE, WIDTH), F32),
            pltpu.VMEM((2 * state, length), BF16),
            pltpu.VMEM((length + HALO, 2 * heads), BF16),
            pltpu.VMEM((length + HALO, WIDTH), F32),
            pltpu.VMEM((state, WIDTH), F32),
        ],
    )
    shape = jax.ShapeDtypeStruct
    return pl.pallas_call(
        prep_kernel,
        grid_spec=grid_spec,
        out_shape=[
            kept((length, features), BF16),
            kept((length, inner), BF16),
            kept((length, state), BF16),
            kept((length, state), BF16),
            kept((heads, length), F32),
            kept((heads, length), F32),
            kept((length + HALO, 2 * heads), BF16),
            kept((chunks, state, inner), BF16),
            shape((state + HALO, inner), BF16),
        ],
        compiler_params=pltpu.CompilerParams(
            vmem_limit_bytes=LIMIT, dimension_semantics=("arbitrary",)
        ),
        cost_estimate=pl.CostEstimate(
            flops=2 * length * features * inner, bytes_accessed=12 * 2**20, transcendentals=0
        ),
        name="prep",
    )(info, far(rows), halo, far(gain), (far, near_one)[resident](main), far(side), far(conv), far(conv), far(bias), far(decay), far(spread))


def mid(normed, main, x, b, c_rows, cumulative, shifted, skip, spread, inner, resident=False):
    length, features = normed.shape
    state = b.shape[1]
    steps = inner // WIDTH
    heads_here = cumulative.shape[0] // steps
    return pl.pallas_call(
        mid_kernel,
        grid=(steps,),
        in_specs=[
            whole_block((length, features)),
            pl.BlockSpec((None, features, WIDTH), lambda j: (0, 0, j)),
            pl.BlockSpec((length, WIDTH), lambda j: (0, j)),
            whole_block((length, state)),
            whole_block((length, state)),
            pl.BlockSpec((heads_here, length), lambda j: (j, 0)),
            pl.BlockSpec((heads_here, length), lambda j: (j, 0)),
            whole_block(skip.shape),
            pl.BlockSpec((spread.shape[0], WIDTH), lambda j: (0, j)),
        ],
        out_specs=[
            pl.BlockSpec((length, WIDTH), lambda j: (0, j)),
            pl.BlockSpec((length, WIDTH), lambda j: (0, j)),
        ],
        out_shape=[
            kept((length, inner), F32),
            kept((length, inner), BF16),
        ],
        scratch_shapes=[pltpu.VMEM((length, CHUNK), F32)],
        compiler_params=pltpu.CompilerParams(
            vmem_limit_bytes=LIMIT, dimension_semantics=("arbitrary",)
        ),
        cost_estimate=pl.CostEstimate(
            flops=2 * length * features * inner, bytes_accessed=12 * 2**20, transcendentals=0
        ),
        name="mid",
    )(*near(normed), (far, near_one)[resident](main), *near(x, b, c_rows, cumulative, shifted), far(skip), far(spread))


def finish(
    members, place_slot, last, info, rows, y, gate, c_rows, reach, local, state_parts,
    gain, spread, pieces, earlier,
):
    features = rows.shape[1]
    length, inner = y.shape
    state = c_rows.shape[1]
    mine, other, partner = state_parts
    resident = not isinstance(pieces, list)
    plan = [] if resident else [ranges for _, ranges in pieces]
    shard_rows = inner // lax.axis_size("seq")
    count = len(members)
    whole = pl.BlockSpec(memory_space=pltpu.VMEM)
    in_specs = [pl.BlockSpec(memory_space=pltpu.SMEM)]
    in_specs += [whole] * 11
    operands = [rows, *near(y, gate, c_rows, reach, local)]
    in_specs += [whole] if resident else [pl.BlockSpec(memory_space=pl.ANY)] * len(pieces)
    in_specs += [whole] * len(earlier)
    operands += [mine, other, partner, far(gain), far(spread)]
    operands += [*near(pieces)] if resident else [far(piece) for piece, _ in pieces]
    operands += list(earlier)
    scratch = [pltpu.VMEM((count * CHUNK, inner), BF16), pltpu.VMEM((state, inner), BF16)]
    if not resident:
        scratch.append(pltpu.VMEM((inner, features), BF16))
        scratch.append(pltpu.SemaphoreType.DMA((sum(len(ranges) for ranges in plan),)))
    shape = (CHUNK, features)
    return pl.pallas_call(
        functools.partial(finish_kernel, plan, shard_rows, members, place_slot, last),
        in_specs=in_specs,
        out_specs=[whole] * (2 * count),
        scratch_shapes=scratch,
        out_shape=[jax.ShapeDtypeStruct(shape, BF16)] * count + [kept(shape, F32)] * count,
        compiler_params=pltpu.CompilerParams(
            vmem_limit_bytes=LIMIT
        ),
        cost_estimate=pl.CostEstimate(
            flops=2 * count * CHUNK * features * inner, bytes_accessed=8 * 2**20, transcendentals=0
        ),
        name="finish",
    )(info, *operands)


def hold_kernel(plan, shard_rows, info, *refs):
    main = refs[1]
    far_pieces = refs[2 : 2 + len(plan)]
    main_out, weight_out, arrived = refs[2 + len(plan) :]
    parts = 4
    rows = main.shape[1] // parts
    copies = []
    for i in range(parts):
        here = pl.ds(i * rows, rows)
        copies.append(
            pltpu.make_async_copy(main.at[0, here], main_out.at[0, here], arrived.at[len(copies)])
        )
    copies += piece_copies(plan, shard_rows, info, far_pieces, weight_out, arrived, len(copies))
    for copy in copies:
        copy.start()
    for copy in copies:
        copy.wait()


def hold(info, trigger, main, pieces, inner):
    plan = [ranges for _, ranges in pieces]
    features = main.shape[1]
    anywhere = pl.BlockSpec(memory_space=pl.ANY)
    whole = pl.BlockSpec(memory_space=pltpu.VMEM)
    count = 4 + sum(len(ranges) for ranges in plan)
    return pl.pallas_call(
        functools.partial(hold_kernel, plan, inner // lax.axis_size("seq")),
        in_specs=[pl.BlockSpec(memory_space=pltpu.SMEM)] + [anywhere] * (2 + len(pieces)),
        out_specs=[whole, whole],
        out_shape=[kept(main.shape, BF16), kept((inner, features), BF16)],
        scratch_shapes=[pltpu.SemaphoreType.DMA((count,))],
        compiler_params=pltpu.CompilerParams(vmem_limit_bytes=SMALL),
        cost_estimate=pl.CostEstimate(flops=10**6, bytes_accessed=24 * 2**20, transcendentals=0),
        name="hold",
    )(info, far(trigger), far(main), *[far(piece) for piece, _ in pieces])


def piece_copies(plan, shard_rows, info, far_pieces, weight, arrived, base):
    copies = []
    for piece, ranges in zip(far_pieces, plan):
        for mask, source, offset, extent in ranges:
            place = 0
            if mask is not None:
                place = pl.multiple_of((info[SEQ] ^ mask) * shard_rows + offset, 16)
            copies.append(
                pltpu.make_async_copy(
                    piece.at[source : source + extent],
                    weight.at[pl.ds(place, extent)],
                    arrived.at[base + len(copies)],
                )
            )
    return copies


def stack_kernel(counts, *refs):
    sources, outs = refs[: -len(counts)], refs[-len(counts) :]
    position = 0
    for out, count in zip(outs, counts):
        start = 0
        for source in sources[position : position + count]:
            out[start : start + source.shape[0]] = source[...]
            start += source.shape[0]
        position += count


def stacked(groups):
    operands = []
    specs = []
    out_shape = []
    for group in groups:
        total = 0
        for value, index, rows in group:
            operands.append(value)
            specs.append(pl.BlockSpec((rows, value.shape[1]), lambda j, index=index: (index, 0)))
            total += rows
        out_shape.append(pltpu.HBM((total, group[0][0].shape[1]), BF16))
    return pl.pallas_call(
        functools.partial(stack_kernel, [len(group) for group in groups]),
        grid=(1,),
        in_specs=specs,
        out_specs=[whole_block(shape.shape) for shape in out_shape],
        out_shape=out_shape,
        compiler_params=pltpu.CompilerParams(vmem_limit_bytes=16 * 2**20),
        cost_estimate=pl.CostEstimate(flops=10**6, bytes_accessed=10**6, transcendentals=0),
        name="stack",
    )(*[far(value) for value in operands])


def seq_swap(value, mask):
    count = lax.axis_size("seq")
    return lax.ppermute(value, "seq", [(i, i ^ mask) for i in range(count)])


def split_state(packed):
    state = packed.shape[0] - HALO
    values = packed[:state].astype(F32)
    tail = packed[state:].astype(F32)
    return values, tail[0:1] + tail[1:2]


def joined_state(values, through):
    high = through.astype(BF16)
    low = (through - high.astype(F32)).astype(BF16)
    rest = jnp.zeros((HALO - 2, through.shape[1]), F32)
    tail = jnp.concatenate([high.astype(F32), low.astype(F32), rest], axis=0)
    return values.astype(BF16), tail.astype(BF16)


def after(earlier, later):
    return later[1] * earlier[0] + later[0], earlier[1] * later[1]


def chosen(condition, first, second):
    return tuple(jnp.where(condition, a, b) for a, b in zip(first, second))


def pair_kernel(info, mine, partner, out):
    half = out.shape[1]
    first = info[FIRST] == 1
    state = out.shape[0] - HALO
    for start in range(0, half, 256):
        place = pl.multiple_of(info[UPPER] * half + start, 256)
        one = split_state(mine[:, pl.ds(place, 256)])
        two = split_state(partner[:, pl.ds(place, 256)])
        total = after(chosen(first, one, two), chosen(first, two, one))
        out[:state, start : start + 256], out[state:, start : start + 256] = joined_state(*total)


def merge_kernel(group, slot, has_entering, last, info, *refs):
    members = refs[: 2**group]
    entering_out = refs[2**group + has_entering]
    rank = info[slot]
    state, half = entering_out.shape
    for start in range(0, half, 256):
        lanes = slice(start, start + 256)
        values = [split_state(member[:, lanes]) for member in members]
        before = (jnp.zeros((state, 256), F32), jnp.ones((1, 256), F32))
        whole = before
        for place in range(2**group):
            value = values[0]
            for code in range(1, 2**group):
                value = chosen((rank ^ code) == place, values[code], value)
            if place < 2**group - 1:
                before = chosen(place < rank, after(before, value), before)
            if not last:
                whole = after(whole, value)
        if has_entering:
            inside = refs[2**group][:, lanes].astype(F32)
            through = jnp.ones((1, 256), F32)
            before = after(before, (inside, through))
        entering_out[:, lanes] = before[0].astype(BF16)
        if not last:
            out = refs[-1]
            out[:state, lanes], out[state:, lanes] = joined_state(*whole)


def small_call(kernel, name, out_shape, info, *operands):
    return pl.pallas_call(
        kernel,
        in_specs=[pl.BlockSpec(memory_space=pltpu.SMEM)] + [whole_block(v.shape) for v in operands],
        out_specs=[whole_block(v.shape) for v in out_shape],
        out_shape=out_shape,
        compiler_params=pltpu.CompilerParams(vmem_limit_bytes=SMALL),
        cost_estimate=pl.CostEstimate(flops=10**6, bytes_accessed=10**6, transcendentals=0),
        name=name,
    )(info, *operands)


def settle_kernel(place, info, base, sent, other, *rest):
    section = info[place]
    rows = (base[...] + other[...].astype(F32)).astype(BF16)
    rows = jnp.where(section == 1, sent[...], rows)
    rest[-1][...] = jnp.where(section == 0, other[...], rows)


def settle(index, chunks, place, info, base, sent, other, finished):
    features = base.shape[1]
    length = chunks * CHUNK
    out_block = pl.BlockSpec((None, CHUNK, features), lambda j: (0, index, 0))
    passed = [] if finished is None else [finished]
    return pl.pallas_call(
        functools.partial(settle_kernel, place),
        grid=(1,),
        in_specs=[pl.BlockSpec(memory_space=pltpu.SMEM)]
        + [whole_block((CHUNK, features))] * 3
        + [pl.BlockSpec(memory_space=pl.ANY)] * len(passed),
        out_specs=out_block,
        out_shape=jax.ShapeDtypeStruct((1, length, features), BF16),
        input_output_aliases={4: 0} if passed else {},
        compiler_params=pltpu.CompilerParams(vmem_limit_bytes=SMALL),
        cost_estimate=pl.CostEstimate(flops=10**6, bytes_accessed=10**6, transcendentals=0),
        name="settle",
    )(info, base, sent, other, *passed)


def stages_of(seq_count):
    bits = seq_count.bit_length() - 1
    found = []
    bit = 1
    while bit < bits:
        group = min(2, bits - bit)
        found.append((bit, group))
        bit += group
    return found


def entering_state(packed, info, sections, seq_count, meanwhile):
    section_count = lax.axis_size("section")
    stages = stages_of(seq_count)

    def swap(value, mask):
        pairs = [
            (i * section_count + s, (i ^ mask) * section_count + s)
            for s in sections
            for i in range(seq_count)
        ]
        return lax.ppermute(value, ("seq", "section"), pairs)

    def forward(value, mask, low_bit):
        pairs = []
        for s in sections:
            for i in range(seq_count):
                later = (i ^ mask) >> low_bit > i >> low_bit
                if later == (s % 2 == 0):
                    pairs.append((i * section_count + s, (i ^ mask) * section_count + s))
        return lax.ppermute(value, ("seq", "section"), pairs)

    depth, inner = packed.shape
    half = jax.ShapeDtypeStruct((depth, inner // 2), BF16)
    states = jax.ShapeDtypeStruct((depth - HALO, inner // 2), BF16)
    partner = swap(packed, 1)
    (total,) = small_call(pair_kernel, "pair", [half], info, packed, partner)
    done = meanwhile(total)
    info, _ = lax.optimization_barrier((info, done[0]))
    entering = []
    for index, (bit, group) in enumerate(stages):
        last = index + 1 == len(stages)
        members = [total]
        for code in range(1, 2**group):
            mask = code << bit
            members.append(forward(total, mask, bit) if last else swap(total, mask))
        kernel = functools.partial(merge_kernel, group, RANKS + index, len(entering), last)
        shapes = [states] if last else [states, half]
        results = small_call(kernel, "merge", shapes, info, *members, *entering)
        entering = [results[0]]
        total = results[-1]
    return (entering[0], swap(entering[0], 1), partner), done


def per_device(
    tokens,
    input_gain,
    main_weight,
    side_weight,
    conv_kernel,
    step_bias,
    decay_rate,
    skip_gain,
    output_gain,
    output_weight,
):
    length, features = tokens.shape
    inner = main_weight.shape[2] // 2
    heads = decay_rate.shape[1]
    state = (side_weight.shape[2] - heads) // 2
    head_dim = inner // heads
    chunks = length // CHUNK
    seq_count = lax.axis_size("seq")
    section_count = lax.axis_size("section")
    section_index = lax.axis_index("section")
    seq_index = lax.axis_index("seq")
    reverse = section_index % 2
    shard = output_weight[0]
    expand = np.repeat(np.eye(heads, dtype=np.float32), head_dim, axis=1)
    spread = jnp.asarray(np.concatenate([expand, expand], axis=0), BF16)
    upper = seq_index % 2
    facts = [reverse, upper, (upper == reverse).astype(jnp.int32), seq_index]
    for bit, group in stages_of(seq_count):
        position = (seq_index >> bit) % 2**group
        facts.append(jnp.where(reverse == 1, 2**group - 1 - position, position))
    places = len(facts)
    rounds = section_count // 2
    for round_index in range(rounds):
        facts.append(section_index - 2 * round_index)
    info = jnp.stack([fact.astype(jnp.int32) for fact in facts])
    order = [chunks - 1, 0] + list(range(1, chunks - 1))

    def edges(first_rows, last_rows, first_wanted, sources, targets):
        pairs = []
        for source, target in zip(sources, targets):
            for i in range(seq_count):
                beside = i + 1 if target % 2 == 0 else i - 1
                if 0 <= beside < seq_count:
                    pairs.append((i * section_count + source, beside * section_count + target))
        value = jnp.where(first_wanted, first_rows, last_rows)
        return lax.ppermute(value, ("seq", "section"), pairs)

    current = tokens
    halo = edges(tokens[:HALO], tokens[length - HALO :], reverse == 1, (0, 1), (0, 1))
    previous = None
    shards = None
    if seq_count == 8:
        halo, shard = lax.optimization_barrier((halo, shard))
        shards = [shard, seq_swap(shard, 2), seq_swap(shard, 4)]
        pieces = None
    else:
        whole = lax.all_gather(shard, "seq", axis=0, tiled=True)
        pieces = [(whole, [(None, 0, 0, inner)])]
    main = main_weight
    for round_index in range(rounds):
        active = (2 * round_index, 2 * round_index + 1)
        normed, x, b, c_rows, cumulative, shifted, reach, local, packed = prep(
            info,
            current,
            halo,
            input_gain,
            main,
            jnp.swapaxes(side_weight, 1, 2),
            conv_kernel,
            step_bias,
            decay_rate,
            spread,
            inner,
            state,
            round_index > 0,
        )
        early = round_index == 0 and shards
        if early:
            packed, *shards[1:] = lax.optimization_barrier((packed, *shards[1:]))

        def meanwhile(total, normed=normed):
            nonlocal pieces
            if early:
                *parts, _ = lax.optimization_barrier((*shards, total))
                rows = parts[0].shape[0] // 2
                up, down, three = stacked(
                    [
                        [(parts[2], 0, rows)],
                        [(parts[1], 1, rows)],
                        [(part, 0, 2 * rows) for part in parts],
                    ]
                )
                halves = [seq_swap(up, 2), seq_swap(down, 4)]
                swapped = seq_swap(three, 1)
            ready, _ = lax.optimization_barrier((normed, total))
            y, gate = mid(
                ready, main, x, b, c_rows, cumulative, shifted, skip_gain, spread, inner,
                round_index > 0,
            )
            if early:
                *halves, _ = lax.optimization_barrier((*halves, y))
                rows = halves[0].shape[0]
                (joined,) = stacked([[(half, 0, rows) for half in halves]])
                diagonal = seq_swap(joined, 1)
                pieces = [(value, [(mask, 0, 0, 2 * rows)]) for value, mask in zip(shards, (0, 2, 4))]
                pieces += [(half, [(6, 0, i * rows, rows)]) for i, half in enumerate(halves)]
                pieces.append((swapped, [(m, i * 2 * rows, 0, 2 * rows) for i, m in enumerate((1, 3, 5))]))
                pieces.append((diagonal, [(7, 0, 0, 2 * rows)]))
            return y, gate

        state_parts, (y, gate) = entering_state(packed, info, active, seq_count, meanwhile)
        last_round = round_index + 1 == rounds
        low, high = active
        place = section_index - low
        terms = {}
        bases = {}
        for members in (order[: chunks // 2], order[chunks // 2 :]):
            outs = finish(
                tuple(members), places if last_round else places + round_index, last_round, info,
                current, y, gate, c_rows, reach, local, state_parts, output_gain, spread, pieces,
                [previous[member] for member in members] if last_round else [],
            )
            for i, member in enumerate(members):
                terms[member] = outs[i]
                bases[member] = outs[len(members) + i]
        if last_round:
            break
        received = []
        values = []
        direct = None
        for step in range(chunks + 2 * SKEW - 1):
            pairs = [(low + hop, low + hop + 1) for hop in range(3) if 0 <= step - hop * SKEW < chunks]
            value = terms[order[step]] if step < chunks else None
            if step >= SKEW:
                passed = received[step - SKEW]
                if step - SKEW < chunks:
                    total = bases[order[step - SKEW]] + passed.astype(F32)
                    total = total if value is None else total + value.astype(F32)
                    passed = total.astype(BF16)
                value = passed
            values.append(value)
            received.append(lax.ppermute(value, "section", pairs))
            if step == chunks + SKEW - 1:
                direct = lax.ppermute(value, "section", [(low + 1, low + 3)])
        received.append(direct)
        trigger, _ = lax.optimization_barrier((values[chunks + SKEW - 1], received[2 * SKEW]))
        main, pieces = hold(info, trigger, main_weight, pieces, inner)
        last_rows = jnp.where(place == 3, received[2 * SKEW], received[SKEW])[CHUNK - HALO :]
        first_rows = jnp.where(place == 3, received[2 * SKEW + 1], received[SKEW + 1])[:HALO]
        halo = edges(first_rows, last_rows, reverse == 1, (low + 2, high + 2), (low + 2, high + 2))
        received[-1], received[-2], halo = lax.optimization_barrier((received[-1], received[-2], halo))
        layer_rows = [None] * chunks
        next_rows = [None] * chunks
        for step, index in enumerate(order):
            layer_rows[index] = values[step + SKEW]
            next_rows[index] = jnp.where(place == 3, received[step + 2 * SKEW], received[step + SKEW])
        previous = layer_rows
        current = jnp.concatenate(next_rows, axis=0)
    finished = None
    for index in order:
        other = lax.ppermute(terms[index], "section", [(low, high), (high, low), (1, 0)])
        finished = settle(index, chunks, places, info, bases[index], terms[index], other, finished)
    return finished


def solution(mesh):
    placed = (
        P("seq", None),
        P("section", None),
        P("section", None, None),
        P("section", None, None),
        P("section", None, None),
        P("section", None),
        P("section", None),
        P("section", None),
        P("section", None),
        P("section", "seq", None),
    )
    return jax.shard_map(
        per_device, mesh=mesh, in_specs=placed, out_specs=P("section", "seq", None), check_vma=False
    )
```

```python
import functools

import jax
import jax.numpy as jnp
import numpy as np
from jax import lax
from jax.experimental import pallas as pl
from jax.experimental.pallas import tpu as pltpu
from jax.sharding import PartitionSpec as P

EPSILON = 1e-05
CHUNK = 128
WIDTH = (512, 2048)
HALO = 16
EDGE = 32
LIMIT = 28 * 2**20
SMALL = 8 * 2**20
SKEW = 2
REVERSE, UPPER, FIRST, SEQ, RANKS = 0, 1, 2, 3, 4
LOG2E = 1.4426950408889634
F32 = jnp.float32
BF16 = jnp.bfloat16


def silu(value):
    half = 0.5 * value
    return half + half * jnp.tanh(half)


def dot(left, right):
    return jnp.dot(left, right, preferred_element_type=F32)


def time_of(index):
    row = index & (CHUNK - 1)
    return (index - row) + ((row & 7) << 4) + (row >> 3)


def order_matrix(size, reverse, back=False):
    place = lax.broadcasted_iota(jnp.int32, (size, size), 1 if back else 0)
    token = lax.broadcasted_iota(jnp.int32, (size, size), 0 if back else 1)
    time = time_of(place)
    target = jnp.where(reverse == 1, size - 1 - time, time)
    return jnp.where(token == target, 1.0, 0.0).astype(BF16)


def edge_matrix(margin, reverse):
    row = lax.broadcasted_iota(jnp.int32, (EDGE, HALO), 0)
    column = lax.broadcasted_iota(jnp.int32, (EDGE, HALO), 1)
    step = (row >> 3) - (EDGE // 8 - margin)
    source = jnp.where(reverse == 1, margin - 1 - step, HALO - margin + step)
    wanted = (step >= 0) & ((row & 7) == 7) & (column == source)
    return jnp.where(wanted, 1.0, 0.0).astype(BF16)


def high_low(value):
    high = value.astype(BF16)
    low = (value - high.astype(F32)).astype(BF16)
    return jnp.concatenate([high, low], axis=1)


def norm_block(values, gain_row):
    widened = values.astype(F32)
    inverse_rms = lax.rsqrt(jnp.mean(widened * widened, axis=-1, keepdims=True) + EPSILON)
    return (widened * inverse_rms * gain_row).astype(BF16)


def prep_kernel(
    info,
    rows,
    halo,
    gain,
    wide,
    side_weight,
    taps,
    side_taps,
    bias,
    decay,
    spread,
    normed_out,
    x_out,
    b_out,
    c_out,
    cum_out,
    shifted_out,
    reach_out,
    local_out,
    state_out,
    extended,
    buffer,
    turned,
    shares,
    wide_shares,
    running,
):
    step_index = pl.program_id(0)
    reverse = info[REVERSE]
    length = rows.shape[0]
    heads = bias.shape[1]
    state = b_out.shape[1]
    chunks = length // CHUNK
    margin = taps.shape[0] - 1
    width = wide.shape[1]

    def filtered(kernel, c, lanes):
        start = EDGE + c * CHUNK
        tail = 8 * margin
        ending = buffer[start + CHUNK - tail : start + CHUNK, lanes]
        previous = buffer[start - tail : start, lanes]
        leading = lax.broadcasted_iota(jnp.int32, ending.shape, 0) & 7 == 0
        entry = jnp.where(
            leading, pltpu.roll(previous, tail - 7, axis=0), pltpu.roll(ending, 1, axis=0)
        )
        region = jnp.concatenate([entry, buffer[start : start + CHUNK, lanes]], axis=0)
        total = None
        for k in range(margin + 1):
            term = kernel[k : k + 1, lanes] * region[8 * k : 8 * k + CHUNK]
            total = term if total is None else total + term
        return silu(total).astype(BF16)

    @pl.when(step_index == 0)
    def _():
        turn = order_matrix(2 * CHUNK, reverse)
        edge = norm_block(halo[...], gain[...])
        extended[0:EDGE] = dot(edge_matrix(margin, reverse), edge).astype(BF16)
        pairs = length // (2 * CHUNK)
        for pair in range(pairs):
            source = jnp.where(reverse == 1, pairs - 1 - pair, pair) * (2 * CHUNK)
            source = pl.multiple_of(source, 2 * CHUNK)
            piece = norm_block(rows[pl.ds(source, 2 * CHUNK), :], gain[...])
            start = EDGE + pair * 2 * CHUNK
            extended[start : start + 2 * CHUNK] = dot(turn, piece).astype(BF16)
        normed_out[...] = extended[EDGE:]
        side = lax.dot_general(
            extended[...], side_weight[...], (((1,), (1,)), ((), ())), preferred_element_type=F32
        )
        side = side.astype(BF16).astype(F32)
        buffer[:, 0 : 2 * state] = side[:, 0 : 2 * state]
        raw = side[EDGE:, 2 * state :] + bias[...]
        step = jnp.maximum(raw, 0.0) + jnp.log1p(jnp.exp(-jnp.abs(raw)))
        change = step * (decay[...] * (-LOG2E))
        row = lax.broadcasted_iota(jnp.int32, (CHUNK, CHUNK), 0)
        column = lax.broadcasted_iota(jnp.int32, (CHUNK, CHUNK), 1)
        triangle = jnp.where(time_of(row) >= time_of(column), 1.0, 0.0).astype(F32)
        before = jnp.zeros((1, heads), F32)
        totals = []
        befores = []
        for c in range(chunks):
            here = slice(c * CHUNK, (c + 1) * CHUNK)
            cumulative = jnp.dot(
                triangle, change[here], preferred_element_type=F32, precision=lax.Precision.HIGHEST
            )
            last = cumulative[CHUNK - 1 :, :]
            befores.append(before)
            totals.append(last)
            before = before + last
            moved = cumulative - jnp.log2(step[here])
            blank = jnp.zeros((CHUNK, 128 - 2 * heads), F32)
            flipped = jnp.concatenate([cumulative, moved, blank], axis=1).T
            cum_out[:, here] = flipped[0:heads]
            shifted_out[:, here] = flipped[heads : 2 * heads]
            shares[here, :] = high_low(jnp.exp2(last - cumulative) * step[here])
            reach_out[here, :] = high_low(jnp.exp2(cumulative))
        befores.append(before)
        zero_rows = jnp.zeros((HALO - chunks, heads), F32)
        shares[length:, :] = high_low(jnp.exp2(jnp.concatenate(totals + [zero_rows], axis=0)))
        zero_rows = jnp.zeros((HALO - chunks - 1, heads), F32)
        reach_out[length:, :] = high_low(jnp.exp2(jnp.concatenate(befores + [zero_rows], axis=0)))
        for c in range(chunks):
            start = c * CHUNK
            here = slice(start, start + CHUNK)
            in_part = filtered(side_taps, c, slice(0, state))
            b_out[here] = in_part
            flipped = in_part.astype(F32).T.astype(BF16)
            blank = jnp.zeros_like(flipped)
            turned[0:state, here] = flipped if c % 2 == 0 else blank
            turned[state:, here] = blank if c % 2 == 0 else flipped
            c_out[here] = filtered(side_taps, c, slice(state, 2 * state))

    buffer[...] = dot(extended[...], wide[...]).astype(BF16).astype(F32)
    wide_shares[...] = dot(shares[...], spread[...])
    running[...] = jnp.zeros_like(running)
    for pair in range(chunks // 2):
        both = slice(2 * pair * CHUNK, (2 * pair + 2) * CHUNK)
        for lane in range(0, width, 256):
            lanes = slice(lane, lane + 256)
            columns = []
            for inside in (slice(lane, lane + 128), slice(lane + 128, lane + 256)):
                weighted = []
                for c in (2 * pair, 2 * pair + 1):
                    here = slice(c * CHUNK, (c + 1) * CHUNK)
                    piece = filtered(taps, c, inside)
                    x_out[here, inside] = piece
                    weighted.append((piece.astype(F32) * wide_shares[here, inside]).astype(BF16))
                columns.append(jnp.concatenate(weighted, axis=0))
            states = dot(turned[:, both], jnp.concatenate(columns, axis=1))
            entering = running[:, lanes]
            for i, c in enumerate((2 * pair, 2 * pair + 1)):
                local_out[c, :, lanes] = entering.astype(BF16)
                total = wide_shares[length + c : length + c + 1, lanes]
                entering = total * entering + states[i * state : (i + 1) * state]
            running[:, lanes] = entering
    state_out[0:state, :] = running[...].astype(BF16)
    through = wide_shares[length : length + 1, :]
    for c in range(1, chunks):
        through = through * wide_shares[length + c : length + c + 1, :]
    high = through.astype(BF16)
    low = (through - high.astype(F32)).astype(BF16)
    tail = jnp.concatenate(
        [high.astype(F32), low.astype(F32), jnp.zeros((HALO - 2, width), F32)], axis=0
    )
    state_out[state:, :] = tail.astype(BF16)


def mid_kernel(
    normed, gate_weight, x, b, c_rows, cumulative, shifted, skip, spread, y_out, gate_out, scores
):
    step_index = pl.program_id(0)
    length = x.shape[0]
    chunks = length // CHUNK
    heads_here = cumulative.shape[0]
    head_dim = x.shape[1] // heads_here
    row = lax.broadcasted_iota(jnp.int32, (CHUNK, CHUNK), 0)
    column = lax.broadcasted_iota(jnp.int32, (CHUNK, CHUNK), 1)
    causal = time_of(row) >= time_of(column)
    lane = lax.broadcasted_iota(jnp.int32, (CHUNK, 2 * head_dim), 1)

    @pl.when(step_index == 0)
    def _():
        for c in range(chunks):
            here = slice(c * CHUNK, (c + 1) * CHUNK)
            scores[here, :] = lax.dot_general(
                c_rows[here, :], b[here, :], (((1,), (1,)), ((), ())), preferred_element_type=F32
            )

    gate_out[...] = dot(normed[...], gate_weight[...]).astype(BF16)
    skip_rows = jnp.broadcast_to(skip[...], (HALO, skip.shape[1]))
    skips = dot(high_low(skip_rows), spread[...])[0:1]
    for c in range(chunks):
        here = slice(c * CHUNK, (c + 1) * CHUNK)
        score = scores[here, :]
        blank = jnp.zeros((128 - heads_here, CHUNK), F32)
        columns = jnp.concatenate([cumulative[:, here], blank], axis=0).T
        for pair in range(heads_here // 2):
            lanes = slice(2 * pair * head_dim, (2 * pair + 2) * head_dim)
            parts = []
            for h in (2 * pair, 2 * pair + 1):
                gap = columns[:, h : h + 1] - shifted[h : h + 1, here]
                parts.append((score * jnp.exp2(jnp.where(causal, gap, -jnp.inf))).astype(BF16))
            values = x[here, lanes]
            zero = jnp.zeros_like(values)
            stacked = jnp.concatenate(
                [jnp.where(lane < head_dim, values, zero), jnp.where(lane < head_dim, zero, values)],
                axis=0,
            )
            within = dot(jnp.concatenate(parts, axis=1), stacked)
            y_out[here, lanes] = within + skips[:, lanes] * values.astype(F32)


def finish_kernel(plan, shard_rows, members, leading, place_slot, last, info, *refs):
    count = len(members)
    rows, y_all, gate_all, c_all, reach_all, local_all = refs[:6]
    mine, other, partner, gain, spread = refs[6:11]
    rest = refs[11:]
    if plan:
        far_pieces = rest[: len(plan)]
        outs = rest[len(plan) : -4]
        normed, entering, weight, arrived = rest[-4:]
    else:
        weight = rest[0]
        outs = rest[1:-2]
        normed, entering = rest[-2:]
    reverse = info[REVERSE]
    inner = weight.shape[0]
    length = y_all.shape[0]
    state = mine.shape[0]
    block = 256
    fetches = []
    if plan:
        fetches = piece_copies(plan, shard_rows, info, far_pieces, weight, arrived, 0)
    for fetch in fetches:
        fetch.start()
    half = inner // 2
    upper = info[UPPER] == 1
    first = info[FIRST] == 1
    for start in range(0, inner, block):
        lanes = slice(start, start + block)
        inside = slice(start % half, start % half + block)
        pair = (other, mine) if start < half else (mine, other)
        full = jnp.where(upper, pair[0][:, inside], pair[1][:, inside])
        tail = partner[state:, lanes].astype(F32)
        through = tail[0:1] + tail[1:2]
        moved = (through * full.astype(F32) + partner[:state, lanes].astype(F32)).astype(BF16)
        entering[:, lanes] = jnp.where(first, full, moved)
    tail = dot(reach_all[length:, :], spread[...])
    index_row = lax.broadcasted_iota(jnp.int32, (HALO, 1), 0)
    turn = order_matrix(CHUNK, reverse, back=True)
    for i, member in enumerate(members):
        position = jnp.where(reverse == 1, length // CHUNK - 1 - member, member)
        here = pl.ds(pl.multiple_of(position * CHUNK, CHUNK), CHUNK)
        c_rows, reach, local = c_all[here, :], reach_all[here, :], local_all.at[position]
        before = jnp.sum(jnp.where(index_row == position, tail, 0.0), axis=0, keepdims=True)
        squares = jnp.zeros((CHUNK, 1), F32)
        gated = []
        for start in range(0, inner, block):
            lanes = slice(start, start + block)
            full = local[:, lanes].astype(F32) + before[:, lanes] * entering[:, lanes].astype(F32)
            carried = dot(c_rows, full.astype(BF16)) * dot(reach, spread[:, lanes])
            part = (y_all[here, lanes] + carried) * silu(gate_all[here, lanes].astype(F32))
            squares = squares + jnp.sum(part * part, axis=-1, keepdims=True)
            gated.append(part)
        inverse_rms = lax.rsqrt(squares * (1.0 / inner) + EPSILON)
        for index, start in enumerate(range(0, inner, block)):
            lanes = slice(start, start + block)
            piece = (gated[index] * inverse_rms * gain[:, lanes]).astype(BF16)
            normed[i * CHUNK : (i + 1) * CHUNK, lanes] = dot(turn, piece).astype(BF16)
    for fetch in fetches:
        fetch.wait()
    place = info[place_slot]

    def columns(j, carry):
        lanes = pl.ds(j * block if leading else pl.multiple_of(j * block, block), block)
        total = dot(normed[...], weight[:, lanes])
        for i in range(count):
            term = total[i * CHUNK : (i + 1) * CHUNK]
            own = rows[members[i] * CHUNK : (members[i] + 1) * CHUNK, lanes]
            base = own.astype(F32) + term
            if last:
                earlier, sent, base_out = outs[i], outs[count + i], outs[2 * count + i]
                sent[:, lanes] = jnp.where(place == 1, earlier[:, lanes], term.astype(BF16))
                base_out[:, lanes] = base
            else:
                outs[i][:, lanes] = jnp.where(place == 0, term, 0.0).astype(BF16)
                outs[count + i][:, lanes] = jnp.where(place == 1, base, 0.0)
        return carry

    if leading:
        for j in range(weight.shape[1] // block):
            columns(j, 0)
    else:
        lax.fori_loop(0, weight.shape[1] // block, columns, 0)


def kept(shape, dtype):
    return pltpu.VMEM(shape, dtype)


def near(*values):
    return tuple(pltpu.with_memory_space_constraint(v, pltpu.VMEM) for v in values)


def near_one(value):
    return near(value)[0]


def far(value):
    return pltpu.with_memory_space_constraint(value, pltpu.HBM)


def whole_block(shape):
    return pl.BlockSpec(shape, lambda *_: (0,) * len(shape))


def prep(info, rows, halo, params, main, inner, state, resident=False):
    place = near_one if resident else far
    width = min(WIDTH[int(resident)], inner)
    main = place(main)
    gain, side, conv, bias, decay, spread = [place(v) for v in params[:6]]
    length, features = rows.shape
    heads = bias.shape[1]
    steps = inner // width
    chunks = length // CHUNK
    margin = conv.shape[1]
    side_width = 2 * state
    grid_spec = pltpu.PrefetchScalarGridSpec(
        num_scalar_prefetch=1,
        grid=(steps,),
        in_specs=[
            whole_block((length, features)),
            whole_block((HALO, features)),
            whole_block((1, features)),
            pl.BlockSpec((None, features, width), lambda j, _: (0, 0, steps + j)),
            pl.BlockSpec((None, side.shape[1], features), lambda j, _: (0, 0, 0)),
            pl.BlockSpec((None, margin, width), lambda j, _: (0, 0, j)),
            pl.BlockSpec((None, margin, side_width), lambda j, _: (0, 0, inner // side_width)),
            whole_block((1, heads)),
            whole_block((1, heads)),
            pl.BlockSpec((2 * heads, width), lambda j, _: (0, j)),
        ],
        out_specs=[
            whole_block((length, features)),
            pl.BlockSpec((length, width), lambda j, _: (0, j)),
            whole_block((length, state)),
            whole_block((length, state)),
            whole_block((heads, length)),
            whole_block((heads, length)),
            whole_block((length + HALO, 2 * heads)),
            pl.BlockSpec((chunks, state, width), lambda j, _: (0, 0, j)),
            pl.BlockSpec((state + HALO, width), lambda j, _: (0, j)),
        ],
        scratch_shapes=[
            pltpu.VMEM((length + EDGE, features), BF16),
            pltpu.VMEM((length + EDGE, width), F32),
            pltpu.VMEM((2 * state, length), BF16),
            pltpu.VMEM((length + HALO, 2 * heads), BF16),
            pltpu.VMEM((length + HALO, width), F32),
            pltpu.VMEM((state, width), F32),
        ],
    )
    shape = jax.ShapeDtypeStruct
    return pl.pallas_call(
        prep_kernel,
        grid_spec=grid_spec,
        out_shape=[
            kept((length, features), BF16),
            kept((length, inner), BF16),
            kept((length, state), BF16),
            kept((length, state), BF16),
            kept((heads, length), F32),
            kept((heads, length), F32),
            kept((length + HALO, 2 * heads), BF16),
            kept((chunks, state, inner), BF16),
            shape((state + HALO, inner), BF16),
        ],
        compiler_params=pltpu.CompilerParams(
            vmem_limit_bytes=LIMIT, dimension_semantics=("arbitrary",)
        ),
        cost_estimate=pl.CostEstimate(
            flops=2 * length * features * inner, bytes_accessed=12 * 2**20, transcendentals=0
        ),
        name="prep",
    )(info, far(rows), halo, gain, main, side, conv, conv, bias, decay, spread)


def mid(normed, main, x, b, c_rows, cumulative, shifted, params, inner, resident=False):
    place = near_one if resident else far
    width = min(WIDTH[0], inner)
    main, spread, skip = place(main), place(params[5]), place(params[6])
    length, features = normed.shape
    state = b.shape[1]
    steps = inner // width
    heads_here = cumulative.shape[0] // steps
    return pl.pallas_call(
        mid_kernel,
        grid=(steps,),
        in_specs=[
            whole_block((length, features)),
            pl.BlockSpec((None, features, width), lambda j: (0, 0, j)),
            pl.BlockSpec((length, width), lambda j: (0, j)),
            whole_block((length, state)),
            whole_block((length, state)),
            pl.BlockSpec((heads_here, length), lambda j: (j, 0)),
            pl.BlockSpec((heads_here, length), lambda j: (j, 0)),
            whole_block(skip.shape),
            pl.BlockSpec((spread.shape[0], width), lambda j: (0, j)),
        ],
        out_specs=[
            pl.BlockSpec((length, width), lambda j: (0, j)),
            pl.BlockSpec((length, width), lambda j: (0, j)),
        ],
        out_shape=[
            kept((length, inner), F32),
            kept((length, inner), BF16),
        ],
        scratch_shapes=[pltpu.VMEM((length, CHUNK), F32)],
        compiler_params=pltpu.CompilerParams(
            vmem_limit_bytes=LIMIT, dimension_semantics=("arbitrary",)
        ),
        cost_estimate=pl.CostEstimate(
            flops=2 * length * features * inner, bytes_accessed=12 * 2**20, transcendentals=0
        ),
        name="mid",
    )(*near(normed), main, *near(x, b, c_rows, cumulative, shifted), skip, spread)


def finish(
    members, leading, place_slot, last, info, rows, y, gate, c_rows, reach, local, state_parts,
    params, pieces, earlier,
):
    features = rows.shape[1]
    length, inner = y.shape
    state = c_rows.shape[1]
    mine, other, partner = state_parts
    resident = not isinstance(pieces, list)
    place = near_one if resident else far
    spread, gain = place(params[5]), place(params[7])
    plan = [] if resident else [ranges for _, ranges in pieces]
    shard_rows = inner // lax.axis_size("seq")
    count = len(members)
    whole = pl.BlockSpec(memory_space=pltpu.VMEM)
    in_specs = [pl.BlockSpec(memory_space=pltpu.SMEM)]
    in_specs += [whole] * 11
    operands = [rows, *near(y, gate, c_rows, reach, local)]
    in_specs += [whole] if resident else [pl.BlockSpec(memory_space=pl.ANY)] * len(pieces)
    in_specs += [whole] * len(earlier)
    operands += [mine, other, partner, gain, spread]
    operands += [*near(pieces)] if resident else [far(piece) for piece, _ in pieces]
    operands += list(earlier)
    scratch = [pltpu.VMEM((count * CHUNK, inner), BF16), pltpu.VMEM((state, inner), BF16)]
    if not resident:
        scratch.append(pltpu.VMEM((inner, features), BF16))
        scratch.append(pltpu.SemaphoreType.DMA((sum(len(ranges) for ranges in plan),)))
    shape = (CHUNK, features)
    return pl.pallas_call(
        functools.partial(finish_kernel, plan, shard_rows, members, leading, place_slot, last),
        in_specs=in_specs,
        out_specs=[whole] * (2 * count),
        scratch_shapes=scratch,
        out_shape=[jax.ShapeDtypeStruct(shape, BF16)] * count + [kept(shape, F32)] * count,
        compiler_params=pltpu.CompilerParams(
            vmem_limit_bytes=LIMIT
        ),
        cost_estimate=pl.CostEstimate(
            flops=2 * count * CHUNK * features * inner, bytes_accessed=8 * 2**20, transcendentals=0
        ),
        name="finish",
    )(info, *operands)


def hold_kernel(plan, shard_rows, extras, info, *refs):
    main = refs[1]
    far_pieces = refs[2 : 2 + len(plan)]
    small = refs[2 + len(plan) : 2 + len(plan) + extras]
    main_out, weight_out, *small_out, arrived = refs[2 + len(plan) + extras :]
    parts = 4
    rows = main.shape[1] // parts
    copies = []
    for i in range(parts):
        here = pl.ds(i * rows, rows)
        copies.append(
            pltpu.make_async_copy(main.at[0, here], main_out.at[0, here], arrived.at[len(copies)])
        )
    for source, target in zip(small, small_out):
        copies.append(pltpu.make_async_copy(source, target, arrived.at[len(copies)]))
    copies += piece_copies(plan, shard_rows, info, far_pieces, weight_out, arrived, len(copies))
    for copy in copies:
        copy.start()
    for copy in copies:
        copy.wait()


def hold(info, trigger, main, pieces, extras, inner):
    plan = [ranges for _, ranges in pieces]
    features = main.shape[1]
    anywhere = pl.BlockSpec(memory_space=pl.ANY)
    whole = pl.BlockSpec(memory_space=pltpu.VMEM)
    count = 4 + len(extras) + sum(len(ranges) for ranges in plan)
    return pl.pallas_call(
        functools.partial(hold_kernel, plan, inner // lax.axis_size("seq"), len(extras)),
        in_specs=[pl.BlockSpec(memory_space=pltpu.SMEM)]
        + [anywhere] * (2 + len(pieces) + len(extras)),
        out_specs=[whole] * (2 + len(extras)),
        out_shape=[kept(main.shape, BF16), kept((inner, features), BF16)]
        + [kept(v.shape, v.dtype) for v in extras],
        scratch_shapes=[pltpu.SemaphoreType.DMA((count,))],
        compiler_params=pltpu.CompilerParams(vmem_limit_bytes=SMALL),
        cost_estimate=pl.CostEstimate(flops=10**6, bytes_accessed=24 * 2**20, transcendentals=0),
        name="hold",
    )(info, far(trigger), far(main), *[far(piece) for piece, _ in pieces], *[far(v) for v in extras])


def piece_copies(plan, shard_rows, info, far_pieces, weight, arrived, base):
    copies = []
    for piece, ranges in zip(far_pieces, plan):
        for mask, source, offset, extent in ranges:
            place = 0
            if mask is not None:
                place = pl.multiple_of((info[SEQ] ^ mask) * shard_rows + offset, 16)
            copies.append(
                pltpu.make_async_copy(
                    piece.at[source : source + extent],
                    weight.at[pl.ds(place, extent)],
                    arrived.at[base + len(copies)],
                )
            )
    return copies


def stack_kernel(counts, *refs):
    sources, outs = refs[: -len(counts)], refs[-len(counts) :]
    position = 0
    for out, count in zip(outs, counts):
        start = 0
        for source in sources[position : position + count]:
            out[start : start + source.shape[0]] = source[...]
            start += source.shape[0]
        position += count


def stacked(groups):
    operands = []
    specs = []
    out_shape = []
    for group in groups:
        total = 0
        for value, index, rows in group:
            operands.append(value)
            specs.append(pl.BlockSpec((rows, value.shape[1] // 2), lambda j, index=index: (index, j)))
            total += rows
        out_shape.append(pltpu.HBM((total, group[0][0].shape[1]), BF16))
    return pl.pallas_call(
        functools.partial(stack_kernel, [len(group) for group in groups]),
        grid=(2,),
        in_specs=specs,
        out_specs=[
            pl.BlockSpec((shape.shape[0], shape.shape[1] // 2), lambda j: (0, j)) for shape in out_shape
        ],
        out_shape=out_shape,
        compiler_params=pltpu.CompilerParams(vmem_limit_bytes=16 * 2**20),
        cost_estimate=pl.CostEstimate(flops=10**6, bytes_accessed=10**6, transcendentals=0),
        name="stack",
    )(*[far(value) for value in operands])


def seq_swap(value, mask):
    count = lax.axis_size("seq")
    return lax.ppermute(value, "seq", [(i, i ^ mask) for i in range(count)])


def split_state(packed):
    state = packed.shape[0] - HALO
    values = packed[:state].astype(F32)
    tail = packed[state:].astype(F32)
    return values, tail[0:1] + tail[1:2]


def joined_state(values, through):
    high = through.astype(BF16)
    low = (through - high.astype(F32)).astype(BF16)
    rest = jnp.zeros((HALO - 2, through.shape[1]), F32)
    tail = jnp.concatenate([high.astype(F32), low.astype(F32), rest], axis=0)
    return values.astype(BF16), tail.astype(BF16)


def after(earlier, later):
    return later[1] * earlier[0] + later[0], earlier[1] * later[1]


def chosen(condition, first, second):
    return tuple(jnp.where(condition, a, b) for a, b in zip(first, second))


def pair_kernel(info, mine, partner, out):
    half = out.shape[1]
    first = info[FIRST] == 1
    state = out.shape[0] - HALO
    for start in range(0, half, 256):
        place = pl.multiple_of(info[UPPER] * half + start, 256)
        one = split_state(mine[:, pl.ds(place, 256)])
        two = split_state(partner[:, pl.ds(place, 256)])
        total = after(chosen(first, one, two), chosen(first, two, one))
        out[:state, start : start + 256], out[state:, start : start + 256] = joined_state(*total)


def merge_kernel(group, slot, has_entering, last, info, *refs):
    members = refs[: 2**group]
    entering_out = refs[2**group + has_entering]
    rank = info[slot]
    state, half = entering_out.shape
    for start in range(0, half, 256):
        lanes = slice(start, start + 256)
        values = [split_state(member[:, lanes]) for member in members]
        before = (jnp.zeros((state, 256), F32), jnp.ones((1, 256), F32))
        whole = before
        for place in range(2**group):
            value = values[0]
            for code in range(1, 2**group):
                value = chosen((rank ^ code) == place, values[code], value)
            if place < 2**group - 1:
                before = chosen(place < rank, after(before, value), before)
            if not last:
                whole = after(whole, value)
        if has_entering:
            inside = refs[2**group][:, lanes].astype(F32)
            through = jnp.ones((1, 256), F32)
            before = after(before, (inside, through))
        entering_out[:, lanes] = before[0].astype(BF16)
        if not last:
            out = refs[-1]
            out[:state, lanes], out[state:, lanes] = joined_state(*whole)


def small_call(kernel, name, out_shape, info, *operands):
    return pl.pallas_call(
        kernel,
        in_specs=[pl.BlockSpec(memory_space=pltpu.SMEM)] + [whole_block(v.shape) for v in operands],
        out_specs=[whole_block(v.shape) for v in out_shape],
        out_shape=out_shape,
        compiler_params=pltpu.CompilerParams(vmem_limit_bytes=SMALL),
        cost_estimate=pl.CostEstimate(flops=10**6, bytes_accessed=10**6, transcendentals=0),
        name=name,
    )(info, *operands)


def settle_kernel(place, info, base, sent, other, *rest):
    section = info[place]
    rows = (base[...] + other[...].astype(F32)).astype(BF16)
    rows = jnp.where(section == 1, sent[...], rows)
    rest[-1][...] = jnp.where(section == 0, other[...], rows)


def settle(index, chunks, place, info, base, sent, other, finished):
    features = base.shape[1]
    length = chunks * CHUNK
    out_block = pl.BlockSpec((None, CHUNK, features), lambda j: (0, index, 0))
    passed = [] if finished is None else [finished]
    return pl.pallas_call(
        functools.partial(settle_kernel, place),
        grid=(1,),
        in_specs=[pl.BlockSpec(memory_space=pltpu.SMEM)]
        + [whole_block((CHUNK, features))] * 3
        + [pl.BlockSpec(memory_space=pl.ANY)] * len(passed),
        out_specs=out_block,
        out_shape=jax.ShapeDtypeStruct((1, length, features), BF16),
        input_output_aliases={4: 0} if passed else {},
        compiler_params=pltpu.CompilerParams(vmem_limit_bytes=SMALL),
        cost_estimate=pl.CostEstimate(flops=10**6, bytes_accessed=10**6, transcendentals=0),
        name="settle",
    )(info, base, sent, other, *passed)


def stages_of(seq_count):
    bits = seq_count.bit_length() - 1
    found = []
    bit = 1
    while bit < bits:
        group = min(2, bits - bit)
        found.append((bit, group))
        bit += group
    return found


def entering_state(packed, info, sections, seq_count, meanwhile):
    section_count = lax.axis_size("section")
    stages = stages_of(seq_count)

    def swap(value, mask):
        pairs = [
            (i * section_count + s, (i ^ mask) * section_count + s)
            for s in sections
            for i in range(seq_count)
        ]
        return lax.ppermute(value, ("seq", "section"), pairs)

    def forward(value, mask, low_bit):
        pairs = []
        for s in sections:
            for i in range(seq_count):
                later = (i ^ mask) >> low_bit > i >> low_bit
                if later == (s % 2 == 0):
                    pairs.append((i * section_count + s, (i ^ mask) * section_count + s))
        return lax.ppermute(value, ("seq", "section"), pairs)

    depth, inner = packed.shape
    half = jax.ShapeDtypeStruct((depth, inner // 2), BF16)
    states = jax.ShapeDtypeStruct((depth - HALO, inner // 2), BF16)
    partner = swap(packed, 1)
    (total,) = small_call(pair_kernel, "pair", [half], info, packed, partner)
    done = meanwhile(total)
    info, _ = lax.optimization_barrier((info, done[0]))
    entering = []
    for index, (bit, group) in enumerate(stages):
        last = index + 1 == len(stages)
        members = [total]
        for code in range(1, 2**group):
            mask = code << bit
            members.append(forward(total, mask, bit) if last else swap(total, mask))
        kernel = functools.partial(merge_kernel, group, RANKS + index, len(entering), last)
        shapes = [states] if last else [states, half]
        results = small_call(kernel, "merge", shapes, info, *members, *entering)
        entering = [results[0]]
        total = results[-1]
    return (entering[0], swap(entering[0], 1), partner), done


def per_device(
    tokens,
    input_gain,
    main_weight,
    side_weight,
    conv_kernel,
    step_bias,
    decay_rate,
    skip_gain,
    output_gain,
    output_weight,
):
    length, features = tokens.shape
    inner = main_weight.shape[2] // 2
    heads = decay_rate.shape[1]
    state = (side_weight.shape[2] - heads) // 2
    head_dim = inner // heads
    chunks = length // CHUNK
    seq_count = lax.axis_size("seq")
    section_count = lax.axis_size("section")
    section_index = lax.axis_index("section")
    seq_index = lax.axis_index("seq")
    reverse = section_index % 2
    shard = output_weight[0]
    expand = np.repeat(np.eye(heads, dtype=np.float32), head_dim, axis=1)
    spread = jnp.asarray(np.concatenate([expand, expand], axis=0), BF16)
    upper = seq_index % 2
    facts = [reverse, upper, (upper == reverse).astype(jnp.int32), seq_index]
    for bit, group in stages_of(seq_count):
        position = (seq_index >> bit) % 2**group
        facts.append(jnp.where(reverse == 1, 2**group - 1 - position, position))
    places = len(facts)
    rounds = section_count // 2
    for round_index in range(rounds):
        facts.append(section_index - 2 * round_index)
    info = jnp.stack([fact.astype(jnp.int32) for fact in facts])
    order = [chunks - 1, 0] + list(range(1, chunks - 1))

    def edges(first_rows, last_rows, first_wanted, sources, targets):
        pairs = []
        for source, target in zip(sources, targets):
            for i in range(seq_count):
                beside = i + 1 if target % 2 == 0 else i - 1
                if 0 <= beside < seq_count:
                    pairs.append((i * section_count + source, beside * section_count + target))
        value = jnp.where(first_wanted, first_rows, last_rows)
        return lax.ppermute(value, ("seq", "section"), pairs)

    current = tokens
    halo = edges(tokens[:HALO], tokens[length - HALO :], reverse == 1, (0, 1), (0, 1))
    previous = None
    shards = None
    if seq_count == 8:
        halo, shard = lax.optimization_barrier((halo, shard))
        shards = [shard, seq_swap(shard, 2), seq_swap(shard, 4)]
        pieces = None
    else:
        whole = lax.all_gather(shard, "seq", axis=0, tiled=True)
        pieces = [(whole, [(None, 0, 0, inner)])]
    main = main_weight
    params = [
        input_gain, jnp.swapaxes(side_weight, 1, 2), conv_kernel, step_bias, decay_rate, spread,
        skip_gain, output_gain,
    ]
    for round_index in range(rounds):
        active = (2 * round_index, 2 * round_index + 1)
        normed, x, b, c_rows, cumulative, shifted, reach, local, packed = prep(
            info,
            current,
            halo,
            params,
            main,
            inner,
            state,
            round_index > 0,
        )
        early = round_index == 0 and shards
        if early:
            packed, *shards[1:] = lax.optimization_barrier((packed, *shards[1:]))

        def meanwhile(total, normed=normed):
            nonlocal pieces
            if early:
                *parts, _ = lax.optimization_barrier((*shards, total))
                rows = parts[0].shape[0] // 2
                up, down, three = stacked(
                    [
                        [(parts[2], 0, rows)],
                        [(parts[1], 1, rows)],
                        [(part, 0, 2 * rows) for part in parts],
                    ]
                )
                halves = [seq_swap(up, 2), seq_swap(down, 4)]
                swapped = seq_swap(three, 1)
            ready, _ = lax.optimization_barrier((normed, total))
            y, gate = mid(
                ready, main, x, b, c_rows, cumulative, shifted, params, inner,
                round_index > 0,
            )
            if early:
                *halves, _ = lax.optimization_barrier((*halves, y))
                rows = halves[0].shape[0]
                (joined,) = stacked([[(half, 0, rows) for half in halves]])
                diagonal = seq_swap(joined, 1)
                pieces = [(value, [(mask, 0, 0, 2 * rows)]) for value, mask in zip(shards, (0, 2, 4))]
                pieces += [(half, [(6, 0, i * rows, rows)]) for i, half in enumerate(halves)]
                pieces.append((swapped, [(m, i * 2 * rows, 0, 2 * rows) for i, m in enumerate((1, 3, 5))]))
                pieces.append((diagonal, [(7, 0, 0, 2 * rows)]))
            return y, gate

        state_parts, (y, gate) = entering_state(packed, info, active, seq_count, meanwhile)
        last_round = round_index + 1 == rounds
        low, high = active
        place = section_index - low
        terms = {}
        bases = {}
        for members in (order[: chunks // 2], order[chunks // 2 :]):
            outs = finish(
                tuple(members), members[0] == order[0], places if last_round else places + round_index, last_round, info,
                current, y, gate, c_rows, reach, local, state_parts, params, pieces,
                [previous[member] for member in members] if last_round else [],
            )
            for i, member in enumerate(members):
                terms[member] = outs[i]
                bases[member] = outs[len(members) + i]
        if last_round:
            break
        received = []
        values = []
        direct = None
        for step in range(chunks + 2 * SKEW - 1):
            pairs = [(low + hop, low + hop + 1) for hop in range(3) if 0 <= step - hop * SKEW < chunks]
            value = terms[order[step]] if step < chunks else None
            if step >= SKEW:
                passed = received[step - SKEW]
                if step - SKEW < chunks:
                    total = bases[order[step - SKEW]] + passed.astype(F32)
                    total = total if value is None else total + value.astype(F32)
                    passed = total.astype(BF16)
                value = passed
            values.append(value)
            received.append(lax.ppermute(value, "section", pairs))
            if step == chunks + SKEW - 1:
                direct = lax.ppermute(value, "section", [(low + 1, low + 3)])
        received.append(direct)
        trigger, _ = lax.optimization_barrier((values[chunks + SKEW - 1], received[2 * SKEW]))
        main, pieces, *params = hold(info, trigger, main_weight, pieces, params, inner)
        last_rows = jnp.where(place == 3, received[2 * SKEW], received[SKEW])[CHUNK - HALO :]
        first_rows = jnp.where(place == 3, received[2 * SKEW + 1], received[SKEW + 1])[:HALO]
        halo = edges(first_rows, last_rows, reverse == 1, (low + 2, high + 2), (low + 2, high + 2))
        received[-1], received[-2], halo = lax.optimization_barrier((received[-1], received[-2], halo))
        layer_rows = [None] * chunks
        next_rows = [None] * chunks
        for step, index in enumerate(order):
            layer_rows[index] = values[step + SKEW]
            next_rows[index] = jnp.where(place == 3, received[step + 2 * SKEW], received[step + SKEW])
        previous = layer_rows
        current = jnp.concatenate(next_rows, axis=0)
    finished = None
    for index in order:
        other = lax.ppermute(terms[index], "section", [(low, high), (high, low), (1, 0)])
        finished = settle(index, chunks, places, info, bases[index], terms[index], other, finished)
    return finished


def solution(mesh):
    placed = (
        P("seq", None),
        P("section", None),
        P("section", None, None),
        P("section", None, None),
        P("section", None, None),
        P("section", None),
        P("section", None),
        P("section", None),
        P("section", None),
        P("section", "seq", None),
    )
    return jax.shard_map(
        per_device, mesh=mesh, in_specs=placed, out_specs=P("section", "seq", None), check_vma=False
    )
```

```python
import functools

import jax
import jax.numpy as jnp
import numpy as np
from jax import lax
from jax.experimental import pallas as pl
from jax.experimental.pallas import tpu as pltpu
from jax.sharding import PartitionSpec as P

EPSILON = 1e-05
CHUNK = 128
WIDTH = (512, 2048)
HALO = 16
EDGE = 32
LIMIT = 28 * 2**20
SMALL = 8 * 2**20
SKEW = 2
REVERSE, UPPER, FIRST, SEQ, RANKS = 0, 1, 2, 3, 4
LOG2E = 1.4426950408889634
F32 = jnp.float32
BF16 = jnp.bfloat16


def silu(value):
    half = 0.5 * value
    return half + half * jnp.tanh(half)


def dot(left, right):
    return jnp.dot(left, right, preferred_element_type=F32)


def time_of(index):
    row = index & (CHUNK - 1)
    return (index - row) + ((row & 7) << 4) + (row >> 3)


def order_matrix(size, reverse, back=False):
    place = lax.broadcasted_iota(jnp.int32, (size, size), 1 if back else 0)
    token = lax.broadcasted_iota(jnp.int32, (size, size), 0 if back else 1)
    time = time_of(place)
    target = jnp.where(reverse == 1, size - 1 - time, time)
    return jnp.where(token == target, 1.0, 0.0).astype(BF16)


def edge_matrix(margin, reverse):
    row = lax.broadcasted_iota(jnp.int32, (EDGE, HALO), 0)
    column = lax.broadcasted_iota(jnp.int32, (EDGE, HALO), 1)
    step = (row >> 3) - (EDGE // 8 - margin)
    source = jnp.where(reverse == 1, margin - 1 - step, HALO - margin + step)
    wanted = (step >= 0) & ((row & 7) == 7) & (column == source)
    return jnp.where(wanted, 1.0, 0.0).astype(BF16)


def high_low(value):
    high = value.astype(BF16)
    low = (value - high.astype(F32)).astype(BF16)
    return jnp.concatenate([high, low], axis=1)


def norm_block(values, gain_row):
    widened = values.astype(F32)
    inverse_rms = lax.rsqrt(jnp.mean(widened * widened, axis=-1, keepdims=True) + EPSILON)
    return (widened * inverse_rms * gain_row).astype(BF16)


def prep_kernel(
    info,
    rows,
    halo,
    gain,
    wide,
    side_weight,
    taps,
    side_taps,
    bias,
    decay,
    spread,
    normed_out,
    x_out,
    b_out,
    c_out,
    cum_out,
    shifted_out,
    reach_out,
    local_out,
    state_out,
    extended,
    buffer,
    turned,
    shares,
    wide_shares,
    running,
):
    step_index = pl.program_id(0)
    reverse = info[REVERSE]
    length = rows.shape[0]
    heads = bias.shape[1]
    state = b_out.shape[1]
    chunks = length // CHUNK
    margin = taps.shape[0] - 1
    width = wide.shape[1]

    def filtered(kernel, c, lanes):
        start = EDGE + c * CHUNK
        tail = 8 * margin
        ending = buffer[start + CHUNK - tail : start + CHUNK, lanes]
        previous = buffer[start - tail : start, lanes]
        leading = lax.broadcasted_iota(jnp.int32, ending.shape, 0) & 7 == 0
        entry = jnp.where(
            leading, pltpu.roll(previous, tail - 7, axis=0), pltpu.roll(ending, 1, axis=0)
        )
        region = jnp.concatenate([entry, buffer[start : start + CHUNK, lanes]], axis=0)
        total = None
        for k in range(margin + 1):
            term = kernel[k : k + 1, lanes] * region[8 * k : 8 * k + CHUNK]
            total = term if total is None else total + term
        return silu(total).astype(BF16)

    @pl.when(step_index == 0)
    def _():
        turn = order_matrix(2 * CHUNK, reverse)
        edge = norm_block(halo[...], gain[...])
        extended[0:EDGE] = dot(edge_matrix(margin, reverse), edge).astype(BF16)
        pairs = length // (2 * CHUNK)
        for pair in range(pairs):
            source = jnp.where(reverse == 1, pairs - 1 - pair, pair) * (2 * CHUNK)
            source = pl.multiple_of(source, 2 * CHUNK)
            piece = norm_block(rows[pl.ds(source, 2 * CHUNK), :], gain[...])
            start = EDGE + pair * 2 * CHUNK
            extended[start : start + 2 * CHUNK] = dot(turn, piece).astype(BF16)
        normed_out[...] = extended[EDGE:]
        side = lax.dot_general(
            extended[...], side_weight[...], (((1,), (1,)), ((), ())), preferred_element_type=F32
        )
        side = side.astype(BF16).astype(F32)
        buffer[:, 0 : 2 * state] = side[:, 0 : 2 * state]
        raw = side[EDGE:, 2 * state :] + bias[...]
        step = jnp.maximum(raw, 0.0) + jnp.log1p(jnp.exp(-jnp.abs(raw)))
        change = step * (decay[...] * (-LOG2E))
        row = lax.broadcasted_iota(jnp.int32, (CHUNK, CHUNK), 0)
        column = lax.broadcasted_iota(jnp.int32, (CHUNK, CHUNK), 1)
        triangle = jnp.where(time_of(row) >= time_of(column), 1.0, 0.0).astype(F32)
        before = jnp.zeros((1, heads), F32)
        totals = []
        befores = []
        for c in range(chunks):
            here = slice(c * CHUNK, (c + 1) * CHUNK)
            cumulative = jnp.dot(
                triangle, change[here], preferred_element_type=F32, precision=lax.Precision.HIGHEST
            )
            last = cumulative[CHUNK - 1 :, :]
            befores.append(before)
            totals.append(last)
            before = before + last
            moved = cumulative - jnp.log2(step[here])
            blank = jnp.zeros((CHUNK, 128 - 2 * heads), F32)
            flipped = jnp.concatenate([cumulative, moved, blank], axis=1).T
            cum_out[:, here] = flipped[0:heads]
            shifted_out[:, here] = flipped[heads : 2 * heads]
            shares[here, :] = high_low(jnp.exp2(last - cumulative) * step[here])
            reach_out[here, :] = high_low(jnp.exp2(cumulative))
        befores.append(before)
        zero_rows = jnp.zeros((HALO - chunks, heads), F32)
        shares[length:, :] = high_low(jnp.exp2(jnp.concatenate(totals + [zero_rows], axis=0)))
        zero_rows = jnp.zeros((HALO - chunks - 1, heads), F32)
        reach_out[length:, :] = high_low(jnp.exp2(jnp.concatenate(befores + [zero_rows], axis=0)))
        for c in range(chunks):
            start = c * CHUNK
            here = slice(start, start + CHUNK)
            in_part = filtered(side_taps, c, slice(0, state))
            b_out[here] = in_part
            flipped = in_part.astype(F32).T.astype(BF16)
            blank = jnp.zeros_like(flipped)
            turned[0:state, here] = flipped if c % 2 == 0 else blank
            turned[state:, here] = blank if c % 2 == 0 else flipped
            c_out[here] = filtered(side_taps, c, slice(state, 2 * state))

    buffer[...] = dot(extended[...], wide[...]).astype(BF16).astype(F32)
    wide_shares[...] = dot(shares[...], spread[...])
    running[...] = jnp.zeros_like(running)
    for pair in range(chunks // 2):
        both = slice(2 * pair * CHUNK, (2 * pair + 2) * CHUNK)
        for lane in range(0, width, 256):
            lanes = slice(lane, lane + 256)
            columns = []
            for inside in (slice(lane, lane + 128), slice(lane + 128, lane + 256)):
                weighted = []
                for c in (2 * pair, 2 * pair + 1):
                    here = slice(c * CHUNK, (c + 1) * CHUNK)
                    piece = filtered(taps, c, inside)
                    x_out[here, inside] = piece
                    weighted.append((piece.astype(F32) * wide_shares[here, inside]).astype(BF16))
                columns.append(jnp.concatenate(weighted, axis=0))
            states = dot(turned[:, both], jnp.concatenate(columns, axis=1))
            entering = running[:, lanes]
            for i, c in enumerate((2 * pair, 2 * pair + 1)):
                local_out[c, :, lanes] = entering.astype(BF16)
                total = wide_shares[length + c : length + c + 1, lanes]
                entering = total * entering + states[i * state : (i + 1) * state]
            running[:, lanes] = entering
    state_out[0:state, :] = running[...].astype(BF16)
    through = wide_shares[length : length + 1, :]
    for c in range(1, chunks):
        through = through * wide_shares[length + c : length + c + 1, :]
    high = through.astype(BF16)
    low = (through - high.astype(F32)).astype(BF16)
    tail = jnp.concatenate(
        [high.astype(F32), low.astype(F32), jnp.zeros((HALO - 2, width), F32)], axis=0
    )
    state_out[state:, :] = tail.astype(BF16)


def mid_kernel(
    normed, gate_weight, x, b, c_rows, cumulative, shifted, skip, spread, y_out, gate_out, scores
):
    step_index = pl.program_id(0)
    length = x.shape[0]
    chunks = length // CHUNK
    heads_here = cumulative.shape[0]
    head_dim = x.shape[1] // heads_here
    row = lax.broadcasted_iota(jnp.int32, (CHUNK, CHUNK), 0)
    column = lax.broadcasted_iota(jnp.int32, (CHUNK, CHUNK), 1)
    causal = time_of(row) >= time_of(column)
    lane = lax.broadcasted_iota(jnp.int32, (CHUNK, 2 * head_dim), 1)

    @pl.when(step_index == 0)
    def _():
        for c in range(chunks):
            here = slice(c * CHUNK, (c + 1) * CHUNK)
            scores[here, :] = lax.dot_general(
                c_rows[here, :], b[here, :], (((1,), (1,)), ((), ())), preferred_element_type=F32
            )

    gate_out[...] = dot(normed[...], gate_weight[...]).astype(BF16)
    skip_rows = jnp.broadcast_to(skip[...], (HALO, skip.shape[1]))
    skips = dot(high_low(skip_rows), spread[...])[0:1]
    for c in range(chunks):
        here = slice(c * CHUNK, (c + 1) * CHUNK)
        score = scores[here, :]
        blank = jnp.zeros((128 - heads_here, CHUNK), F32)
        columns = jnp.concatenate([cumulative[:, here], blank], axis=0).T
        for pair in range(heads_here // 2):
            lanes = slice(2 * pair * head_dim, (2 * pair + 2) * head_dim)
            parts = []
            for h in (2 * pair, 2 * pair + 1):
                gap = columns[:, h : h + 1] - shifted[h : h + 1, here]
                parts.append((score * jnp.exp2(jnp.where(causal, gap, -jnp.inf))).astype(BF16))
            values = x[here, lanes]
            zero = jnp.zeros_like(values)
            stacked = jnp.concatenate(
                [jnp.where(lane < head_dim, values, zero), jnp.where(lane < head_dim, zero, values)],
                axis=0,
            )
            within = dot(jnp.concatenate(parts, axis=1), stacked)
            y_out[here, lanes] = within + skips[:, lanes] * values.astype(F32)


def finish_kernel(plan, shard_rows, members, leading, place_slot, last, info, *refs):
    count = len(members)
    rows, y_all, gate_all, c_all, reach_all, local_all = refs[:6]
    mine, other, partner, gain, spread = refs[6:11]
    rest = refs[11:]
    if plan:
        far_pieces = rest[: len(plan)]
        outs = rest[len(plan) : -4]
        normed, entering, weight, arrived = rest[-4:]
    else:
        weight = rest[0]
        outs = rest[1:-2]
        normed, entering = rest[-2:]
    reverse = info[REVERSE]
    inner = weight.shape[0]
    length = y_all.shape[0]
    state = mine.shape[0]
    block = 256
    fetches = []
    if plan:
        fetches = piece_copies(plan, shard_rows, info, far_pieces, weight, arrived, 0)
    for fetch in fetches:
        fetch.start()
    half = inner // 2
    upper = info[UPPER] == 1
    first = info[FIRST] == 1
    for start in range(0, inner, block):
        lanes = slice(start, start + block)
        inside = slice(start % half, start % half + block)
        pair = (other, mine) if start < half else (mine, other)
        full = jnp.where(upper, pair[0][:, inside], pair[1][:, inside])
        tail = partner[state:, lanes].astype(F32)
        through = tail[0:1] + tail[1:2]
        moved = (through * full.astype(F32) + partner[:state, lanes].astype(F32)).astype(BF16)
        entering[:, lanes] = jnp.where(first, full, moved)
    tail = dot(reach_all[length:, :], spread[...])
    index_row = lax.broadcasted_iota(jnp.int32, (HALO, 1), 0)
    turn = order_matrix(CHUNK, reverse, back=True)
    for i, member in enumerate(members):
        position = jnp.where(reverse == 1, length // CHUNK - 1 - member, member)
        here = pl.ds(pl.multiple_of(position * CHUNK, CHUNK), CHUNK)
        c_rows, reach, local = c_all[here, :], reach_all[here, :], local_all.at[position]
        before = jnp.sum(jnp.where(index_row == position, tail, 0.0), axis=0, keepdims=True)
        squares = jnp.zeros((CHUNK, 1), F32)
        gated = []
        for start in range(0, inner, block):
            lanes = slice(start, start + block)
            full = local[:, lanes].astype(F32) + before[:, lanes] * entering[:, lanes].astype(F32)
            carried = dot(c_rows, full.astype(BF16)) * dot(reach, spread[:, lanes])
            part = (y_all[here, lanes] + carried) * silu(gate_all[here, lanes].astype(F32))
            squares = squares + jnp.sum(part * part, axis=-1, keepdims=True)
            gated.append(part)
        inverse_rms = lax.rsqrt(squares * (1.0 / inner) + EPSILON)
        for index, start in enumerate(range(0, inner, block)):
            lanes = slice(start, start + block)
            piece = (gated[index] * inverse_rms * gain[:, lanes]).astype(BF16)
            normed[i * CHUNK : (i + 1) * CHUNK, lanes] = dot(turn, piece).astype(BF16)
    for fetch in fetches:
        fetch.wait()
    place = info[place_slot]

    def columns(j, carry):
        lanes = pl.ds(j * block if leading else pl.multiple_of(j * block, block), block)
        total = dot(normed[...], weight[:, lanes])
        for i in range(count):
            term = total[i * CHUNK : (i + 1) * CHUNK]
            own = rows[members[i] * CHUNK : (members[i] + 1) * CHUNK, lanes]
            base = own.astype(F32) + term
            if last:
                earlier, sent, base_out = outs[i], outs[count + i], outs[2 * count + i]
                sent[:, lanes] = jnp.where(place == 1, earlier[:, lanes], term.astype(BF16))
                base_out[:, lanes] = base
            else:
                outs[i][:, lanes] = jnp.where(place == 0, term, 0.0).astype(BF16)
                outs[count + i][:, lanes] = jnp.where(place == 1, base, 0.0)
        return carry

    if leading:
        for j in range(weight.shape[1] // block):
            columns(j, 0)
    else:
        lax.fori_loop(0, weight.shape[1] // block, columns, 0)


def kept(shape, dtype):
    return pltpu.VMEM(shape, dtype)


def near(*values):
    return tuple(pltpu.with_memory_space_constraint(v, pltpu.VMEM) for v in values)


def near_one(value):
    return near(value)[0]


def far(value):
    return pltpu.with_memory_space_constraint(value, pltpu.HBM)


def whole_block(shape):
    return pl.BlockSpec(shape, lambda *_: (0,) * len(shape))


def prep(info, rows, halo, params, main, inner, state, resident=False):
    place = near_one if resident else far
    width = min(WIDTH[int(resident)], inner)
    main = place(main)
    gain, side, conv, bias, decay, spread = [place(v) for v in params[:6]]
    length, features = rows.shape
    heads = bias.shape[1]
    steps = inner // width
    chunks = length // CHUNK
    margin = conv.shape[1]
    side_width = 2 * state
    grid_spec = pltpu.PrefetchScalarGridSpec(
        num_scalar_prefetch=1,
        grid=(steps,),
        in_specs=[
            whole_block((length, features)),
            whole_block((HALO, features)),
            whole_block((1, features)),
            pl.BlockSpec((None, features, width), lambda j, _: (0, 0, steps + j)),
            pl.BlockSpec((None, side.shape[1], features), lambda j, _: (0, 0, 0)),
            pl.BlockSpec((None, margin, width), lambda j, _: (0, 0, j)),
            pl.BlockSpec((None, margin, side_width), lambda j, _: (0, 0, inner // side_width)),
            whole_block((1, heads)),
            whole_block((1, heads)),
            pl.BlockSpec((2 * heads, width), lambda j, _: (0, j)),
        ],
        out_specs=[
            whole_block((length, features)),
            pl.BlockSpec((length, width), lambda j, _: (0, j)),
            whole_block((length, state)),
            whole_block((length, state)),
            whole_block((heads, length)),
            whole_block((heads, length)),
            whole_block((length + HALO, 2 * heads)),
            pl.BlockSpec((chunks, state, width), lambda j, _: (0, 0, j)),
            pl.BlockSpec((state + HALO, width), lambda j, _: (0, j)),
        ],
        scratch_shapes=[
            pltpu.VMEM((length + EDGE, features), BF16),
            pltpu.VMEM((length + EDGE, width), F32),
            pltpu.VMEM((2 * state, length), BF16),
            pltpu.VMEM((length + HALO, 2 * heads), BF16),
            pltpu.VMEM((length + HALO, width), F32),
            pltpu.VMEM((state, width), F32),
        ],
    )
    shape = jax.ShapeDtypeStruct
    return pl.pallas_call(
        prep_kernel,
        grid_spec=grid_spec,
        out_shape=[
            kept((length, features), BF16),
            kept((length, inner), BF16),
            kept((length, state), BF16),
            kept((length, state), BF16),
            kept((heads, length), F32),
            kept((heads, length), F32),
            kept((length + HALO, 2 * heads), BF16),
            kept((chunks, state, inner), BF16),
            shape((state + HALO, inner), BF16),
        ],
        compiler_params=pltpu.CompilerParams(
            vmem_limit_bytes=LIMIT, dimension_semantics=("arbitrary",)
        ),
        cost_estimate=pl.CostEstimate(
            flops=2 * length * features * inner, bytes_accessed=12 * 2**20, transcendentals=0
        ),
        name="prep",
    )(info, place(rows), halo, gain, main, side, conv, conv, bias, decay, spread)


def mid(normed, main, x, b, c_rows, cumulative, shifted, params, inner, resident=False):
    place = near_one if resident else far
    width = min(WIDTH[0], inner)
    main, spread, skip = place(main), place(params[5]), place(params[6])
    length, features = normed.shape
    state = b.shape[1]
    steps = inner // width
    heads_here = cumulative.shape[0] // steps
    return pl.pallas_call(
        mid_kernel,
        grid=(steps,),
        in_specs=[
            whole_block((length, features)),
            pl.BlockSpec((None, features, width), lambda j: (0, 0, j)),
            pl.BlockSpec((length, width), lambda j: (0, j)),
            whole_block((length, state)),
            whole_block((length, state)),
            pl.BlockSpec((heads_here, length), lambda j: (j, 0)),
            pl.BlockSpec((heads_here, length), lambda j: (j, 0)),
            whole_block(skip.shape),
            pl.BlockSpec((spread.shape[0], width), lambda j: (0, j)),
        ],
        out_specs=[
            pl.BlockSpec((length, width), lambda j: (0, j)),
            pl.BlockSpec((length, width), lambda j: (0, j)),
        ],
        out_shape=[
            kept((length, inner), F32),
            kept((length, inner), BF16),
        ],
        scratch_shapes=[pltpu.VMEM((length, CHUNK), F32)],
        compiler_params=pltpu.CompilerParams(
            vmem_limit_bytes=LIMIT, dimension_semantics=("arbitrary",)
        ),
        cost_estimate=pl.CostEstimate(
            flops=2 * length * features * inner, bytes_accessed=12 * 2**20, transcendentals=0
        ),
        name="mid",
    )(*near(normed), main, *near(x, b, c_rows, cumulative, shifted), skip, spread)


def finish(
    members, leading, place_slot, last, info, rows, y, gate, c_rows, reach, local, state_parts,
    params, pieces, earlier,
):
    features = rows.shape[1]
    length, inner = y.shape
    state = c_rows.shape[1]
    mine, other, partner = state_parts
    resident = not isinstance(pieces, list)
    place = near_one if resident else far
    spread, gain = place(params[5]), place(params[7])
    plan = [] if resident else [ranges for _, ranges in pieces]
    shard_rows = inner // lax.axis_size("seq")
    count = len(members)
    whole = pl.BlockSpec(memory_space=pltpu.VMEM)
    in_specs = [pl.BlockSpec(memory_space=pltpu.SMEM)]
    in_specs += [whole] * 11
    operands = [rows, *near(y, gate, c_rows, reach, local)]
    in_specs += [whole] if resident else [pl.BlockSpec(memory_space=pl.ANY)] * len(pieces)
    in_specs += [whole] * len(earlier)
    operands += [mine, other, partner, gain, spread]
    operands += [*near(pieces)] if resident else [far(piece) for piece, _ in pieces]
    operands += list(earlier)
    scratch = [pltpu.VMEM((count * CHUNK, inner), BF16), pltpu.VMEM((state, inner), BF16)]
    if not resident:
        scratch.append(pltpu.VMEM((inner, features), BF16))
        scratch.append(pltpu.SemaphoreType.DMA((sum(len(ranges) for ranges in plan),)))
    shape = (CHUNK, features)
    return pl.pallas_call(
        functools.partial(finish_kernel, plan, shard_rows, members, leading, place_slot, last),
        in_specs=in_specs,
        out_specs=[whole] * (2 * count),
        scratch_shapes=scratch,
        out_shape=[jax.ShapeDtypeStruct(shape, BF16)] * count + [kept(shape, F32)] * count,
        compiler_params=pltpu.CompilerParams(
            vmem_limit_bytes=LIMIT
        ),
        cost_estimate=pl.CostEstimate(
            flops=2 * count * CHUNK * features * inner, bytes_accessed=8 * 2**20, transcendentals=0
        ),
        name="finish",
    )(info, *operands)


def hold_kernel(plan, shard_rows, extras, info, *refs):
    main = refs[1]
    far_pieces = refs[2 : 2 + len(plan)]
    small = refs[2 + len(plan) : 2 + len(plan) + extras]
    main_out, weight_out, *small_out, arrived = refs[2 + len(plan) + extras :]
    parts = 4
    rows = main.shape[1] // parts
    copies = []
    for i in range(parts):
        here = pl.ds(i * rows, rows)
        copies.append(
            pltpu.make_async_copy(main.at[0, here], main_out.at[0, here], arrived.at[len(copies)])
        )
    for source, target in zip(small, small_out):
        copies.append(pltpu.make_async_copy(source, target, arrived.at[len(copies)]))
    copies += piece_copies(plan, shard_rows, info, far_pieces, weight_out, arrived, len(copies))
    for copy in copies:
        copy.start()
    for copy in copies:
        copy.wait()


def hold(info, trigger, main, pieces, extras, inner):
    plan = [ranges for _, ranges in pieces]
    features = main.shape[1]
    anywhere = pl.BlockSpec(memory_space=pl.ANY)
    whole = pl.BlockSpec(memory_space=pltpu.VMEM)
    count = 4 + len(extras) + sum(len(ranges) for ranges in plan)
    return pl.pallas_call(
        functools.partial(hold_kernel, plan, inner // lax.axis_size("seq"), len(extras)),
        in_specs=[pl.BlockSpec(memory_space=pltpu.SMEM)]
        + [anywhere] * (2 + len(pieces) + len(extras)),
        out_specs=[whole] * (2 + len(extras)),
        out_shape=[kept(main.shape, BF16), kept((inner, features), BF16)]
        + [kept(v.shape, v.dtype) for v in extras],
        scratch_shapes=[pltpu.SemaphoreType.DMA((count,))],
        compiler_params=pltpu.CompilerParams(vmem_limit_bytes=SMALL),
        cost_estimate=pl.CostEstimate(flops=10**6, bytes_accessed=24 * 2**20, transcendentals=0),
        name="hold",
    )(info, far(trigger), far(main), *[far(piece) for piece, _ in pieces], *[far(v) for v in extras])


def piece_copies(plan, shard_rows, info, far_pieces, weight, arrived, base):
    copies = []
    for piece, ranges in zip(far_pieces, plan):
        for mask, source, offset, extent in ranges:
            place = 0
            if mask is not None:
                place = pl.multiple_of((info[SEQ] ^ mask) * shard_rows + offset, 16)
            copies.append(
                pltpu.make_async_copy(
                    piece.at[source : source + extent],
                    weight.at[pl.ds(place, extent)],
                    arrived.at[base + len(copies)],
                )
            )
    return copies


def stack_kernel(counts, *refs):
    sources, outs = refs[: -len(counts)], refs[-len(counts) :]
    position = 0
    for out, count in zip(outs, counts):
        start = 0
        for source in sources[position : position + count]:
            out[start : start + source.shape[0]] = source[...]
            start += source.shape[0]
        position += count


def stacked(groups):
    operands = []
    specs = []
    out_shape = []
    for group in groups:
        total = 0
        for value, index, rows in group:
            operands.append(value)
            specs.append(pl.BlockSpec((rows, value.shape[1] // 2), lambda j, index=index: (index, j)))
            total += rows
        out_shape.append(pltpu.HBM((total, group[0][0].shape[1]), BF16))
    return pl.pallas_call(
        functools.partial(stack_kernel, [len(group) for group in groups]),
        grid=(2,),
        in_specs=specs,
        out_specs=[
            pl.BlockSpec((shape.shape[0], shape.shape[1] // 2), lambda j: (0, j)) for shape in out_shape
        ],
        out_shape=out_shape,
        compiler_params=pltpu.CompilerParams(vmem_limit_bytes=16 * 2**20),
        cost_estimate=pl.CostEstimate(flops=10**6, bytes_accessed=10**6, transcendentals=0),
        name="stack",
    )(*[far(value) for value in operands])


def seq_swap(value, mask):
    count = lax.axis_size("seq")
    return lax.ppermute(value, "seq", [(i, i ^ mask) for i in range(count)])


def split_state(packed):
    state = packed.shape[0] - HALO
    values = packed[:state].astype(F32)
    tail = packed[state:].astype(F32)
    return values, tail[0:1] + tail[1:2]


def joined_state(values, through):
    high = through.astype(BF16)
    low = (through - high.astype(F32)).astype(BF16)
    rest = jnp.zeros((HALO - 2, through.shape[1]), F32)
    tail = jnp.concatenate([high.astype(F32), low.astype(F32), rest], axis=0)
    return values.astype(BF16), tail.astype(BF16)


def after(earlier, later):
    return later[1] * earlier[0] + later[0], earlier[1] * later[1]


def chosen(condition, first, second):
    return tuple(jnp.where(condition, a, b) for a, b in zip(first, second))


def pair_kernel(info, mine, partner, out):
    half = out.shape[1]
    first = info[FIRST] == 1
    state = out.shape[0] - HALO
    for start in range(0, half, 256):
        place = pl.multiple_of(info[UPPER] * half + start, 256)
        one = split_state(mine[:, pl.ds(place, 256)])
        two = split_state(partner[:, pl.ds(place, 256)])
        total = after(chosen(first, one, two), chosen(first, two, one))
        out[:state, start : start + 256], out[state:, start : start + 256] = joined_state(*total)


def merge_kernel(group, slot, has_entering, last, info, *refs):
    members = refs[: 2**group]
    entering_out = refs[2**group + has_entering]
    rank = info[slot]
    state, half = entering_out.shape
    for start in range(0, half, 256):
        lanes = slice(start, start + 256)
        values = [split_state(member[:, lanes]) for member in members]
        before = (jnp.zeros((state, 256), F32), jnp.ones((1, 256), F32))
        whole = before
        for place in range(2**group):
            value = values[0]
            for code in range(1, 2**group):
                value = chosen((rank ^ code) == place, values[code], value)
            if place < 2**group - 1:
                before = chosen(place < rank, after(before, value), before)
            if not last:
                whole = after(whole, value)
        if has_entering:
            inside = refs[2**group][:, lanes].astype(F32)
            through = jnp.ones((1, 256), F32)
            before = after(before, (inside, through))
        entering_out[:, lanes] = before[0].astype(BF16)
        if not last:
            out = refs[-1]
            out[:state, lanes], out[state:, lanes] = joined_state(*whole)


def small_call(kernel, name, out_shape, info, *operands):
    return pl.pallas_call(
        kernel,
        in_specs=[pl.BlockSpec(memory_space=pltpu.SMEM)] + [whole_block(v.shape) for v in operands],
        out_specs=[whole_block(v.shape) for v in out_shape],
        out_shape=out_shape,
        compiler_params=pltpu.CompilerParams(vmem_limit_bytes=SMALL),
        cost_estimate=pl.CostEstimate(flops=10**6, bytes_accessed=10**6, transcendentals=0),
        name=name,
    )(info, *operands)


def settle_kernel(place, info, base, sent, other, *rest):
    section = info[place]
    rows = (base[...] + other[...].astype(F32)).astype(BF16)
    rows = jnp.where(section == 1, sent[...], rows)
    rest[-1][...] = jnp.where(section == 0, other[...], rows)


def settle(index, chunks, place, info, base, sent, other, finished):
    features = base.shape[1]
    length = chunks * CHUNK
    out_block = pl.BlockSpec((None, CHUNK, features), lambda j: (0, index, 0))
    passed = [] if finished is None else [finished]
    return pl.pallas_call(
        functools.partial(settle_kernel, place),
        grid=(1,),
        in_specs=[pl.BlockSpec(memory_space=pltpu.SMEM)]
        + [whole_block((CHUNK, features))] * 3
        + [pl.BlockSpec(memory_space=pl.ANY)] * len(passed),
        out_specs=out_block,
        out_shape=jax.ShapeDtypeStruct((1, length, features), BF16),
        input_output_aliases={4: 0} if passed else {},
        compiler_params=pltpu.CompilerParams(vmem_limit_bytes=SMALL),
        cost_estimate=pl.CostEstimate(flops=10**6, bytes_accessed=10**6, transcendentals=0),
        name="settle",
    )(info, base, sent, other, *passed)


def stages_of(seq_count):
    bits = seq_count.bit_length() - 1
    found = []
    bit = 1
    while bit < bits:
        group = min(2, bits - bit)
        found.append((bit, group))
        bit += group
    return found


def entering_state(packed, info, sections, seq_count, meanwhile):
    section_count = lax.axis_size("section")
    stages = stages_of(seq_count)

    def swap(value, mask):
        pairs = [
            (i * section_count + s, (i ^ mask) * section_count + s)
            for s in sections
            for i in range(seq_count)
        ]
        return lax.ppermute(value, ("seq", "section"), pairs)

    def forward(value, mask, low_bit):
        pairs = []
        for s in sections:
            for i in range(seq_count):
                later = (i ^ mask) >> low_bit > i >> low_bit
                if later == (s % 2 == 0):
                    pairs.append((i * section_count + s, (i ^ mask) * section_count + s))
        return lax.ppermute(value, ("seq", "section"), pairs)

    depth, inner = packed.shape
    half = jax.ShapeDtypeStruct((depth, inner // 2), BF16)
    states = jax.ShapeDtypeStruct((depth - HALO, inner // 2), BF16)
    partner = swap(packed, 1)
    (total,) = small_call(pair_kernel, "pair", [half], info, packed, partner)
    done = meanwhile(total)
    info, _ = lax.optimization_barrier((info, done[0]))
    entering = []
    for index, (bit, group) in enumerate(stages):
        last = index + 1 == len(stages)
        members = [total]
        for code in range(1, 2**group):
            mask = code << bit
            members.append(forward(total, mask, bit) if last else swap(total, mask))
        kernel = functools.partial(merge_kernel, group, RANKS + index, len(entering), last)
        shapes = [states] if last else [states, half]
        results = small_call(kernel, "merge", shapes, info, *members, *entering)
        entering = [results[0]]
        total = results[-1]
    return (entering[0], swap(entering[0], 1), partner), done


def per_device(
    tokens,
    input_gain,
    main_weight,
    side_weight,
    conv_kernel,
    step_bias,
    decay_rate,
    skip_gain,
    output_gain,
    output_weight,
):
    length, features = tokens.shape
    inner = main_weight.shape[2] // 2
    heads = decay_rate.shape[1]
    state = (side_weight.shape[2] - heads) // 2
    head_dim = inner // heads
    chunks = length // CHUNK
    seq_count = lax.axis_size("seq")
    section_count = lax.axis_size("section")
    section_index = lax.axis_index("section")
    seq_index = lax.axis_index("seq")
    reverse = section_index % 2
    shard = output_weight[0]
    expand = np.repeat(np.eye(heads, dtype=np.float32), head_dim, axis=1)
    spread = jnp.asarray(np.concatenate([expand, expand], axis=0), BF16)
    upper = seq_index % 2
    facts = [reverse, upper, (upper == reverse).astype(jnp.int32), seq_index]
    for bit, group in stages_of(seq_count):
        position = (seq_index >> bit) % 2**group
        facts.append(jnp.where(reverse == 1, 2**group - 1 - position, position))
    places = len(facts)
    rounds = section_count // 2
    for round_index in range(rounds):
        facts.append(section_index - 2 * round_index)
    info = jnp.stack([fact.astype(jnp.int32) for fact in facts])
    order = [chunks - 1, 0] + list(range(1, chunks - 1))

    def edges(first_rows, last_rows, first_wanted, sources, targets):
        pairs = []
        for source, target in zip(sources, targets):
            for i in range(seq_count):
                beside = i + 1 if target % 2 == 0 else i - 1
                if 0 <= beside < seq_count:
                    pairs.append((i * section_count + source, beside * section_count + target))
        value = jnp.where(first_wanted, first_rows, last_rows)
        return lax.ppermute(value, ("seq", "section"), pairs)

    current = tokens
    halo = edges(tokens[:HALO], tokens[length - HALO :], reverse == 1, (0, 1), (0, 1))
    previous = None
    shards = None
    if seq_count == 8:
        halo, shard = lax.optimization_barrier((halo, shard))
        shards = [shard, seq_swap(shard, 2), seq_swap(shard, 4)]
        pieces = None
    else:
        whole = lax.all_gather(shard, "seq", axis=0, tiled=True)
        pieces = [(whole, [(None, 0, 0, inner)])]
    main = main_weight
    params = [
        input_gain, jnp.swapaxes(side_weight, 1, 2), conv_kernel, step_bias, decay_rate, spread,
        skip_gain, output_gain,
    ]
    for round_index in range(rounds):
        active = (2 * round_index, 2 * round_index + 1)
        normed, x, b, c_rows, cumulative, shifted, reach, local, packed = prep(
            info,
            current,
            halo,
            params,
            main,
            inner,
            state,
            round_index > 0,
        )
        early = round_index == 0 and shards
        if early:
            packed, *shards[1:] = lax.optimization_barrier((packed, *shards[1:]))

        def meanwhile(total, normed=normed):
            nonlocal pieces
            if early:
                *parts, _ = lax.optimization_barrier((*shards, total))
                rows = parts[0].shape[0] // 2
                up, down, three = stacked(
                    [
                        [(parts[2], 0, rows)],
                        [(parts[1], 1, rows)],
                        [(part, 0, 2 * rows) for part in parts],
                    ]
                )
                halves = [seq_swap(up, 2), seq_swap(down, 4)]
                swapped = seq_swap(three, 1)
            ready, _ = lax.optimization_barrier((normed, total))
            y, gate = mid(
                ready, main, x, b, c_rows, cumulative, shifted, params, inner,
                round_index > 0,
            )
            if early:
                *halves, _ = lax.optimization_barrier((*halves, y))
                rows = halves[0].shape[0]
                (joined,) = stacked([[(half, 0, rows) for half in halves]])
                diagonal = seq_swap(joined, 1)
                pieces = [(value, [(mask, 0, 0, 2 * rows)]) for value, mask in zip(shards, (0, 2, 4))]
                pieces += [(half, [(6, 0, i * rows, rows)]) for i, half in enumerate(halves)]
                pieces.append((swapped, [(m, i * 2 * rows, 0, 2 * rows) for i, m in enumerate((1, 3, 5))]))
                pieces.append((diagonal, [(7, 0, 0, 2 * rows)]))
            return y, gate

        state_parts, (y, gate) = entering_state(packed, info, active, seq_count, meanwhile)
        last_round = round_index + 1 == rounds
        low, high = active
        place = section_index - low
        terms = {}
        bases = {}
        for members in (order[: chunks // 2], order[chunks // 2 :]):
            outs = finish(
                tuple(members), members[0] == order[0], places if last_round else places + round_index, last_round, info,
                current, y, gate, c_rows, reach, local, state_parts, params, pieces,
                [previous[member] for member in members] if last_round else [],
            )
            for i, member in enumerate(members):
                terms[member] = outs[i]
                bases[member] = outs[len(members) + i]
        if last_round:
            break
        received = []
        values = []
        direct = None
        for step in range(chunks + 2 * SKEW - 1):
            pairs = [(low + hop, low + hop + 1) for hop in range(3) if 0 <= step - hop * SKEW < chunks]
            value = terms[order[step]] if step < chunks else None
            if step >= SKEW:
                passed = received[step - SKEW]
                if step - SKEW < chunks:
                    total = bases[order[step - SKEW]] + passed.astype(F32)
                    total = total if value is None else total + value.astype(F32)
                    passed = total.astype(BF16)
                value = passed
            values.append(value)
            received.append(lax.ppermute(value, "section", pairs))
            if step == chunks + SKEW - 1:
                direct = lax.ppermute(value, "section", [(low + 1, low + 3)])
        received.append(direct)
        trigger, _ = lax.optimization_barrier((values[chunks + SKEW - 1], received[2 * SKEW]))
        main, pieces, *params = hold(info, trigger, main_weight, pieces, params, inner)
        last_rows = jnp.where(place == 3, received[2 * SKEW], received[SKEW])[CHUNK - HALO :]
        first_rows = jnp.where(place == 3, received[2 * SKEW + 1], received[SKEW + 1])[:HALO]
        halo = edges(first_rows, last_rows, reverse == 1, (low + 2, high + 2), (low + 2, high + 2))
        received[-1], received[-2], halo = lax.optimization_barrier((received[-1], received[-2], halo))
        layer_rows = [None] * chunks
        next_rows = [None] * chunks
        for step, index in enumerate(order):
            layer_rows[index] = values[step + SKEW]
            next_rows[index] = jnp.where(place == 3, received[step + 2 * SKEW], received[step + SKEW])
        previous = layer_rows
        current = jnp.concatenate(next_rows, axis=0)
    finished = None
    for index in order:
        other = lax.ppermute(terms[index], "section", [(low, high), (high, low), (1, 0)])
        finished = settle(index, chunks, places, info, bases[index], terms[index], other, finished)
    return finished


def solution(mesh):
    placed = (
        P("seq", None),
        P("section", None),
        P("section", None, None),
        P("section", None, None),
        P("section", None, None),
        P("section", None),
        P("section", None),
        P("section", None),
        P("section", None),
        P("section", "seq", None),
    )
    return jax.shard_map(
        per_device, mesh=mesh, in_specs=placed, out_specs=P("section", "seq", None), check_vma=False
    )
```

```python
import functools

import jax
import jax.numpy as jnp
import numpy as np
from jax import lax
from jax.experimental import pallas as pl
from jax.experimental.pallas import tpu as pltpu
from jax.sharding import PartitionSpec as P

EPSILON = 1e-05
CHUNK = 128
WIDTH = (512, 2048)
HALO = 16
EDGE = 32
LIMIT = 28 * 2**20
SMALL = 8 * 2**20
SKEW = 2
REVERSE, UPPER, FIRST, SEQ, RANKS = 0, 1, 2, 3, 4
LOG2E = 1.4426950408889634
F32 = jnp.float32
BF16 = jnp.bfloat16


def silu(value):
    half = 0.5 * value
    return half + half * jnp.tanh(half)


def dot(left, right):
    return jnp.dot(left, right, preferred_element_type=F32)


def time_of(index):
    row = index & (CHUNK - 1)
    return (index - row) + ((row & 7) << 4) + (row >> 3)


def order_matrix(size, reverse, back=False):
    place = lax.broadcasted_iota(jnp.int32, (size, size), 1 if back else 0)
    token = lax.broadcasted_iota(jnp.int32, (size, size), 0 if back else 1)
    time = time_of(place)
    target = jnp.where(reverse == 1, size - 1 - time, time)
    return jnp.where(token == target, 1.0, 0.0).astype(BF16)


def edge_matrix(margin, reverse):
    row = lax.broadcasted_iota(jnp.int32, (EDGE, HALO), 0)
    column = lax.broadcasted_iota(jnp.int32, (EDGE, HALO), 1)
    step = (row >> 3) - (EDGE // 8 - margin)
    source = jnp.where(reverse == 1, margin - 1 - step, HALO - margin + step)
    wanted = (step >= 0) & ((row & 7) == 7) & (column == source)
    return jnp.where(wanted, 1.0, 0.0).astype(BF16)


def high_low(value):
    high = value.astype(BF16)
    low = (value - high.astype(F32)).astype(BF16)
    return jnp.concatenate([high, low], axis=1)


def norm_block(values, gain_row):
    widened = values.astype(F32)
    inverse_rms = lax.rsqrt(jnp.mean(widened * widened, axis=-1, keepdims=True) + EPSILON)
    return (widened * inverse_rms * gain_row).astype(BF16)


def prep_kernel(
    info,
    rows,
    halo,
    gain,
    wide,
    side_weight,
    taps,
    side_taps,
    bias,
    decay,
    spread,
    normed_out,
    x_out,
    b_out,
    c_out,
    cum_out,
    shifted_out,
    reach_out,
    local_out,
    state_out,
    extended,
    buffer,
    turned,
    shares,
    wide_shares,
    running,
):
    step_index = pl.program_id(0)
    reverse = info[REVERSE]
    length = rows.shape[0]
    heads = bias.shape[1]
    state = b_out.shape[1]
    chunks = length // CHUNK
    margin = taps.shape[0] - 1
    width = wide.shape[1]

    def filtered(kernel, c, lanes):
        start = EDGE + c * CHUNK
        tail = 8 * margin
        ending = buffer[start + CHUNK - tail : start + CHUNK, lanes]
        previous = buffer[start - tail : start, lanes]
        leading = lax.broadcasted_iota(jnp.int32, ending.shape, 0) & 7 == 0
        entry = jnp.where(
            leading, pltpu.roll(previous, tail - 7, axis=0), pltpu.roll(ending, 1, axis=0)
        )
        region = jnp.concatenate([entry, buffer[start : start + CHUNK, lanes]], axis=0)
        total = None
        for k in range(margin + 1):
            term = kernel[k : k + 1, lanes] * region[8 * k : 8 * k + CHUNK]
            total = term if total is None else total + term
        return silu(total).astype(BF16)

    @pl.when(step_index == 0)
    def _():
        turn = order_matrix(2 * CHUNK, reverse)
        edge = norm_block(halo[...], gain[...])
        extended[0:EDGE] = dot(edge_matrix(margin, reverse), edge).astype(BF16)
        pairs = length // (2 * CHUNK)
        for pair in range(pairs):
            source = jnp.where(reverse == 1, pairs - 1 - pair, pair) * (2 * CHUNK)
            source = pl.multiple_of(source, 2 * CHUNK)
            piece = norm_block(rows[pl.ds(source, 2 * CHUNK), :], gain[...])
            start = EDGE + pair * 2 * CHUNK
            extended[start : start + 2 * CHUNK] = dot(turn, piece).astype(BF16)
        normed_out[...] = extended[EDGE:]
        side = lax.dot_general(
            extended[...], side_weight[...], (((1,), (1,)), ((), ())), preferred_element_type=F32
        )
        side = side.astype(BF16).astype(F32)
        buffer[:, 0 : 2 * state] = side[:, 0 : 2 * state]
        raw = side[EDGE:, 2 * state :] + bias[...]
        step = jnp.maximum(raw, 0.0) + jnp.log1p(jnp.exp(-jnp.abs(raw)))
        change = step * (decay[...] * (-LOG2E))
        row = lax.broadcasted_iota(jnp.int32, (CHUNK, CHUNK), 0)
        column = lax.broadcasted_iota(jnp.int32, (CHUNK, CHUNK), 1)
        triangle = jnp.where(time_of(row) >= time_of(column), 1.0, 0.0).astype(F32)
        before = jnp.zeros((1, heads), F32)
        totals = []
        befores = []
        for c in range(chunks):
            here = slice(c * CHUNK, (c + 1) * CHUNK)
            cumulative = jnp.dot(
                triangle, change[here], preferred_element_type=F32, precision=lax.Precision.HIGHEST
            )
            last = cumulative[CHUNK - 1 :, :]
            befores.append(before)
            totals.append(last)
            before = before + last
            moved = cumulative - jnp.log2(step[here])
            blank = jnp.zeros((CHUNK, 128 - 2 * heads), F32)
            flipped = jnp.concatenate([cumulative, moved, blank], axis=1).T
            cum_out[:, here] = flipped[0:heads]
            shifted_out[:, here] = flipped[heads : 2 * heads]
            shares[here, :] = high_low(jnp.exp2(last - cumulative) * step[here])
            reach_out[here, :] = high_low(jnp.exp2(cumulative))
        befores.append(before)
        zero_rows = jnp.zeros((HALO - chunks, heads), F32)
        shares[length:, :] = high_low(jnp.exp2(jnp.concatenate(totals + [zero_rows], axis=0)))
        zero_rows = jnp.zeros((HALO - chunks - 1, heads), F32)
        reach_out[length:, :] = high_low(jnp.exp2(jnp.concatenate(befores + [zero_rows], axis=0)))
        for c in range(chunks):
            start = c * CHUNK
            here = slice(start, start + CHUNK)
            in_part = filtered(side_taps, c, slice(0, state))
            b_out[here] = in_part
            flipped = in_part.astype(F32).T.astype(BF16)
            blank = jnp.zeros_like(flipped)
            turned[0:state, here] = flipped if c % 2 == 0 else blank
            turned[state:, here] = blank if c % 2 == 0 else flipped
            c_out[here] = filtered(side_taps, c, slice(state, 2 * state))

    buffer[...] = dot(extended[...], wide[...]).astype(BF16).astype(F32)
    wide_shares[...] = dot(shares[...], spread[...])
    running[...] = jnp.zeros_like(running)
    for pair in range(chunks // 2):
        both = slice(2 * pair * CHUNK, (2 * pair + 2) * CHUNK)
        for lane in range(0, width, 256):
            lanes = slice(lane, lane + 256)
            columns = []
            for inside in (slice(lane, lane + 128), slice(lane + 128, lane + 256)):
                weighted = []
                for c in (2 * pair, 2 * pair + 1):
                    here = slice(c * CHUNK, (c + 1) * CHUNK)
                    piece = filtered(taps, c, inside)
                    x_out[here, inside] = piece
                    weighted.append((piece.astype(F32) * wide_shares[here, inside]).astype(BF16))
                columns.append(jnp.concatenate(weighted, axis=0))
            states = dot(turned[:, both], jnp.concatenate(columns, axis=1))
            entering = running[:, lanes]
            for i, c in enumerate((2 * pair, 2 * pair + 1)):
                local_out[c, :, lanes] = entering.astype(BF16)
                total = wide_shares[length + c : length + c + 1, lanes]
                entering = total * entering + states[i * state : (i + 1) * state]
            running[:, lanes] = entering
    state_out[0:state, :] = running[...].astype(BF16)
    through = wide_shares[length : length + 1, :]
    for c in range(1, chunks):
        through = through * wide_shares[length + c : length + c + 1, :]
    high = through.astype(BF16)
    low = (through - high.astype(F32)).astype(BF16)
    tail = jnp.concatenate(
        [high.astype(F32), low.astype(F32), jnp.zeros((HALO - 2, width), F32)], axis=0
    )
    state_out[state:, :] = tail.astype(BF16)


def mid_kernel(
    normed, gate_weight, x, b, c_rows, cumulative, shifted, skip, spread, y_out, gate_out, scores
):
    step_index = pl.program_id(0)
    length = x.shape[0]
    chunks = length // CHUNK
    heads_here = cumulative.shape[0]
    head_dim = x.shape[1] // heads_here
    row = lax.broadcasted_iota(jnp.int32, (CHUNK, CHUNK), 0)
    column = lax.broadcasted_iota(jnp.int32, (CHUNK, CHUNK), 1)
    causal = time_of(row) >= time_of(column)
    lane = lax.broadcasted_iota(jnp.int32, (CHUNK, 2 * head_dim), 1)

    @pl.when(step_index == 0)
    def _():
        for c in range(chunks):
            here = slice(c * CHUNK, (c + 1) * CHUNK)
            scores[here, :] = lax.dot_general(
                c_rows[here, :], b[here, :], (((1,), (1,)), ((), ())), preferred_element_type=F32
            )

    gate_out[...] = dot(normed[...], gate_weight[...]).astype(BF16)
    skip_rows = jnp.broadcast_to(skip[...], (HALO, skip.shape[1]))
    skips = dot(high_low(skip_rows), spread[...])[0:1]
    for c in range(chunks):
        here = slice(c * CHUNK, (c + 1) * CHUNK)
        score = scores[here, :]
        blank = jnp.zeros((128 - heads_here, CHUNK), F32)
        columns = jnp.concatenate([cumulative[:, here], blank], axis=0).T
        for pair in range(heads_here // 2):
            lanes = slice(2 * pair * head_dim, (2 * pair + 2) * head_dim)
            parts = []
            for h in (2 * pair, 2 * pair + 1):
                gap = columns[:, h : h + 1] - shifted[h : h + 1, here]
                parts.append((score * jnp.exp2(jnp.where(causal, gap, -jnp.inf))).astype(BF16))
            values = x[here, lanes]
            zero = jnp.zeros_like(values)
            stacked = jnp.concatenate(
                [jnp.where(lane < head_dim, values, zero), jnp.where(lane < head_dim, zero, values)],
                axis=0,
            )
            within = dot(jnp.concatenate(parts, axis=1), stacked)
            y_out[here, lanes] = within + skips[:, lanes] * values.astype(F32)


def finish_kernel(plan, shard_rows, members, leading, place_slot, last, info, *refs):
    count = len(members)
    rows, y_all, gate_all, c_all, reach_all, local_all = refs[:6]
    mine, other, partner, gain, spread = refs[6:11]
    rest = refs[11:]
    if plan:
        far_pieces = rest[: len(plan)]
        outs = rest[len(plan) : -4]
        normed, entering, weight, arrived = rest[-4:]
    else:
        weight = rest[0]
        outs = rest[1:-2]
        normed, entering = rest[-2:]
    reverse = info[REVERSE]
    inner = weight.shape[0]
    length = y_all.shape[0]
    state = mine.shape[0]
    block = 256
    fetches = []
    if plan:
        fetches = piece_copies(plan, shard_rows, info, far_pieces, weight, arrived, 0)
    for fetch in fetches:
        fetch.start()
    half = inner // 2
    upper = info[UPPER] == 1
    first = info[FIRST] == 1
    for start in range(0, inner, block):
        lanes = slice(start, start + block)
        inside = slice(start % half, start % half + block)
        pair = (other, mine) if start < half else (mine, other)
        full = jnp.where(upper, pair[0][:, inside], pair[1][:, inside])
        tail = partner[state:, lanes].astype(F32)
        through = tail[0:1] + tail[1:2]
        moved = (through * full.astype(F32) + partner[:state, lanes].astype(F32)).astype(BF16)
        entering[:, lanes] = jnp.where(first, full, moved)
    tail = dot(reach_all[length:, :], spread[...])
    index_row = lax.broadcasted_iota(jnp.int32, (HALO, 1), 0)
    turn = order_matrix(CHUNK, reverse, back=True)
    for i, member in enumerate(members):
        position = jnp.where(reverse == 1, length // CHUNK - 1 - member, member)
        here = pl.ds(pl.multiple_of(position * CHUNK, CHUNK), CHUNK)
        c_rows, reach, local = c_all[here, :], reach_all[here, :], local_all.at[position]
        before = jnp.sum(jnp.where(index_row == position, tail, 0.0), axis=0, keepdims=True)
        squares = jnp.zeros((CHUNK, 1), F32)
        gated = []
        for start in range(0, inner, block):
            lanes = slice(start, start + block)
            full = local[:, lanes].astype(F32) + before[:, lanes] * entering[:, lanes].astype(F32)
            carried = dot(c_rows, full.astype(BF16)) * dot(reach, spread[:, lanes])
            part = (y_all[here, lanes] + carried) * silu(gate_all[here, lanes].astype(F32))
            squares = squares + jnp.sum(part * part, axis=-1, keepdims=True)
            gated.append(part)
        inverse_rms = lax.rsqrt(squares * (1.0 / inner) + EPSILON)
        for index, start in enumerate(range(0, inner, block)):
            lanes = slice(start, start + block)
            piece = (gated[index] * inverse_rms * gain[:, lanes]).astype(BF16)
            normed[i * CHUNK : (i + 1) * CHUNK, lanes] = dot(turn, piece).astype(BF16)
    for fetch in fetches:
        fetch.wait()
    place = info[place_slot]

    def columns(j, carry):
        lanes = pl.ds(j * block if leading else pl.multiple_of(j * block, block), block)
        total = dot(normed[...], weight[:, lanes])
        for i in range(count):
            term = total[i * CHUNK : (i + 1) * CHUNK]
            own = rows[members[i] * CHUNK : (members[i] + 1) * CHUNK, lanes]
            base = own.astype(F32) + term
            if last:
                earlier, sent, base_out = outs[i], outs[count + i], outs[2 * count + i]
                sent[:, lanes] = jnp.where(place == 1, earlier[:, lanes], term.astype(BF16))
                base_out[:, lanes] = base
            else:
                outs[i][:, lanes] = jnp.where(place == 0, term, 0.0).astype(BF16)
                outs[count + i][:, lanes] = jnp.where(place == 1, base, 0.0)
        return carry

    if leading:
        for j in range(weight.shape[1] // block):
            columns(j, 0)
    else:
        lax.fori_loop(0, weight.shape[1] // block, columns, 0)


def kept(shape, dtype):
    return pltpu.VMEM(shape, dtype)


def near(*values):
    return tuple(pltpu.with_memory_space_constraint(v, pltpu.VMEM) for v in values)


def near_one(value):
    return near(value)[0]


def far(value):
    return pltpu.with_memory_space_constraint(value, pltpu.HBM)


def whole_block(shape):
    return pl.BlockSpec(shape, lambda *_: (0,) * len(shape))


def prep(info, rows, halo, params, main, inner, state, resident=False):
    place = near_one if resident else far
    width = min(WIDTH[int(resident)], inner)
    main = place(main)
    gain, side, conv, bias, decay, spread = [place(v) for v in params[:6]]
    length, features = rows.shape
    heads = bias.shape[1]
    steps = inner // width
    chunks = length // CHUNK
    margin = conv.shape[1]
    side_width = 2 * state
    grid_spec = pltpu.PrefetchScalarGridSpec(
        num_scalar_prefetch=1,
        grid=(steps,),
        in_specs=[
            whole_block((length, features)),
            whole_block((HALO, features)),
            whole_block((1, features)),
            pl.BlockSpec((None, features, width), lambda j, _: (0, 0, steps + j)),
            pl.BlockSpec((None, side.shape[1], features), lambda j, _: (0, 0, 0)),
            pl.BlockSpec((None, margin, width), lambda j, _: (0, 0, j)),
            pl.BlockSpec((None, margin, side_width), lambda j, _: (0, 0, inner // side_width)),
            whole_block((1, heads)),
            whole_block((1, heads)),
            pl.BlockSpec((2 * heads, width), lambda j, _: (0, j)),
        ],
        out_specs=[
            whole_block((length, features)),
            pl.BlockSpec((length, width), lambda j, _: (0, j)),
            whole_block((length, state)),
            whole_block((length, state)),
            whole_block((heads, length)),
            whole_block((heads, length)),
            whole_block((length + HALO, 2 * heads)),
            pl.BlockSpec((chunks, state, width), lambda j, _: (0, 0, j)),
            pl.BlockSpec((state + HALO, width), lambda j, _: (0, j)),
        ],
        scratch_shapes=[
            pltpu.VMEM((length + EDGE, features), BF16),
            pltpu.VMEM((length + EDGE, width), F32),
            pltpu.VMEM((2 * state, length), BF16),
            pltpu.VMEM((length + HALO, 2 * heads), BF16),
            pltpu.VMEM((length + HALO, width), F32),
            pltpu.VMEM((state, width), F32),
        ],
    )
    shape = jax.ShapeDtypeStruct
    return pl.pallas_call(
        prep_kernel,
        grid_spec=grid_spec,
        out_shape=[
            kept((length, features), BF16),
            kept((length, inner), BF16),
            kept((length, state), BF16),
            kept((length, state), BF16),
            kept((heads, length), F32),
            kept((heads, length), F32),
            kept((length + HALO, 2 * heads), BF16),
            kept((chunks, state, inner), BF16),
            shape((state + HALO, inner), BF16),
        ],
        compiler_params=pltpu.CompilerParams(
            vmem_limit_bytes=LIMIT, dimension_semantics=("arbitrary",)
        ),
        cost_estimate=pl.CostEstimate(
            flops=2 * length * features * inner, bytes_accessed=12 * 2**20, transcendentals=0
        ),
        name="prep",
    )(info, place(rows), halo, gain, main, side, conv, conv, bias, decay, spread)


def mid(normed, main, x, b, c_rows, cumulative, shifted, params, inner, resident=False):
    place = near_one if resident else far
    width = min(WIDTH[0], inner)
    main, spread, skip = place(main), place(params[5]), place(params[6])
    length, features = normed.shape
    state = b.shape[1]
    steps = inner // width
    heads_here = cumulative.shape[0] // steps
    return pl.pallas_call(
        mid_kernel,
        grid=(steps,),
        in_specs=[
            whole_block((length, features)),
            pl.BlockSpec((None, features, width), lambda j: (0, 0, j)),
            pl.BlockSpec((length, width), lambda j: (0, j)),
            whole_block((length, state)),
            whole_block((length, state)),
            pl.BlockSpec((heads_here, length), lambda j: (j, 0)),
            pl.BlockSpec((heads_here, length), lambda j: (j, 0)),
            whole_block(skip.shape),
            pl.BlockSpec((spread.shape[0], width), lambda j: (0, j)),
        ],
        out_specs=[
            pl.BlockSpec((length, width), lambda j: (0, j)),
            pl.BlockSpec((length, width), lambda j: (0, j)),
        ],
        out_shape=[
            kept((length, inner), F32),
            kept((length, inner), BF16),
        ],
        scratch_shapes=[pltpu.VMEM((length, CHUNK), F32)],
        compiler_params=pltpu.CompilerParams(
            vmem_limit_bytes=LIMIT, dimension_semantics=("arbitrary",)
        ),
        cost_estimate=pl.CostEstimate(
            flops=2 * length * features * inner, bytes_accessed=12 * 2**20, transcendentals=0
        ),
        name="mid",
    )(*near(normed), main, *near(x, b, c_rows, cumulative, shifted), skip, spread)


def finish(
    members, leading, place_slot, last, info, rows, y, gate, c_rows, reach, local, state_parts,
    params, pieces, earlier,
):
    features = rows.shape[1]
    length, inner = y.shape
    state = c_rows.shape[1]
    mine, other, partner = state_parts
    resident = not isinstance(pieces, list)
    place = near_one if resident else far
    spread, gain = place(params[5]), place(params[7])
    if resident:
        mine, other, partner = near(mine, other, partner)
    plan = [] if resident else [ranges for _, ranges in pieces]
    shard_rows = inner // lax.axis_size("seq")
    count = len(members)
    whole = pl.BlockSpec(memory_space=pltpu.VMEM)
    in_specs = [pl.BlockSpec(memory_space=pltpu.SMEM)]
    in_specs += [whole] * 11
    operands = [rows, *near(y, gate, c_rows, reach, local)]
    in_specs += [whole] if resident else [pl.BlockSpec(memory_space=pl.ANY)] * len(pieces)
    in_specs += [whole] * len(earlier)
    operands += [mine, other, partner, gain, spread]
    operands += [*near(pieces)] if resident else [far(piece) for piece, _ in pieces]
    operands += list(earlier)
    scratch = [pltpu.VMEM((count * CHUNK, inner), BF16), pltpu.VMEM((state, inner), BF16)]
    if not resident:
        scratch.append(pltpu.VMEM((inner, features), BF16))
        scratch.append(pltpu.SemaphoreType.DMA((sum(len(ranges) for ranges in plan),)))
    shape = (CHUNK, features)
    return pl.pallas_call(
        functools.partial(finish_kernel, plan, shard_rows, members, leading, place_slot, last),
        in_specs=in_specs,
        out_specs=[whole] * (2 * count),
        scratch_shapes=scratch,
        out_shape=[jax.ShapeDtypeStruct(shape, BF16)] * count + [kept(shape, F32)] * count,
        compiler_params=pltpu.CompilerParams(
            vmem_limit_bytes=LIMIT
        ),
        cost_estimate=pl.CostEstimate(
            flops=2 * count * CHUNK * features * inner, bytes_accessed=8 * 2**20, transcendentals=0
        ),
        name="finish",
    )(info, *operands)


def hold_kernel(plan, shard_rows, extras, info, *refs):
    main = refs[1]
    far_pieces = refs[2 : 2 + len(plan)]
    small = refs[2 + len(plan) : 2 + len(plan) + extras]
    main_out, weight_out, *small_out, arrived = refs[2 + len(plan) + extras :]
    parts = 4
    rows = main.shape[1] // parts
    copies = []
    for i in range(parts):
        here = pl.ds(i * rows, rows)
        copies.append(
            pltpu.make_async_copy(main.at[0, here], main_out.at[0, here], arrived.at[len(copies)])
        )
    for source, target in zip(small, small_out):
        copies.append(pltpu.make_async_copy(source, target, arrived.at[len(copies)]))
    copies += piece_copies(plan, shard_rows, info, far_pieces, weight_out, arrived, len(copies))
    for copy in copies:
        copy.start()
    for copy in copies:
        copy.wait()


def hold(info, trigger, main, pieces, extras, inner):
    plan = [ranges for _, ranges in pieces]
    features = main.shape[1]
    anywhere = pl.BlockSpec(memory_space=pl.ANY)
    whole = pl.BlockSpec(memory_space=pltpu.VMEM)
    count = 4 + len(extras) + sum(len(ranges) for ranges in plan)
    return pl.pallas_call(
        functools.partial(hold_kernel, plan, inner // lax.axis_size("seq"), len(extras)),
        in_specs=[pl.BlockSpec(memory_space=pltpu.SMEM)]
        + [anywhere] * (2 + len(pieces) + len(extras)),
        out_specs=[whole] * (2 + len(extras)),
        out_shape=[kept(main.shape, BF16), kept((inner, features), BF16)]
        + [kept(v.shape, v.dtype) for v in extras],
        scratch_shapes=[pltpu.SemaphoreType.DMA((count,))],
        compiler_params=pltpu.CompilerParams(vmem_limit_bytes=SMALL),
        cost_estimate=pl.CostEstimate(flops=10**6, bytes_accessed=24 * 2**20, transcendentals=0),
        name="hold",
    )(info, far(trigger), far(main), *[far(piece) for piece, _ in pieces], *[far(v) for v in extras])


def piece_copies(plan, shard_rows, info, far_pieces, weight, arrived, base):
    copies = []
    for piece, ranges in zip(far_pieces, plan):
        for mask, source, offset, extent in ranges:
            place = 0
            if mask is not None:
                place = pl.multiple_of((info[SEQ] ^ mask) * shard_rows + offset, 16)
            copies.append(
                pltpu.make_async_copy(
                    piece.at[source : source + extent],
                    weight.at[pl.ds(place, extent)],
                    arrived.at[base + len(copies)],
                )
            )
    return copies


def stack_kernel(counts, *refs):
    sources, outs = refs[: -len(counts)], refs[-len(counts) :]
    position = 0
    for out, count in zip(outs, counts):
        start = 0
        for source in sources[position : position + count]:
            out[start : start + source.shape[0]] = source[...]
            start += source.shape[0]
        position += count


def stacked(groups):
    operands = []
    specs = []
    out_shape = []
    for group in groups:
        total = 0
        for value, index, rows in group:
            operands.append(value)
            specs.append(pl.BlockSpec((rows, value.shape[1] // 2), lambda j, index=index: (index, j)))
            total += rows
        out_shape.append(pltpu.HBM((total, group[0][0].shape[1]), BF16))
    return pl.pallas_call(
        functools.partial(stack_kernel, [len(group) for group in groups]),
        grid=(2,),
        in_specs=specs,
        out_specs=[
            pl.BlockSpec((shape.shape[0], shape.shape[1] // 2), lambda j: (0, j)) for shape in out_shape
        ],
        out_shape=out_shape,
        compiler_params=pltpu.CompilerParams(vmem_limit_bytes=16 * 2**20),
        cost_estimate=pl.CostEstimate(flops=10**6, bytes_accessed=10**6, transcendentals=0),
        name="stack",
    )(*[far(value) for value in operands])


def seq_swap(value, mask):
    count = lax.axis_size("seq")
    return lax.ppermute(value, "seq", [(i, i ^ mask) for i in range(count)])


def split_state(packed):
    state = packed.shape[0] - HALO
    values = packed[:state].astype(F32)
    tail = packed[state:].astype(F32)
    return values, tail[0:1] + tail[1:2]


def joined_state(values, through):
    high = through.astype(BF16)
    low = (through - high.astype(F32)).astype(BF16)
    rest = jnp.zeros((HALO - 2, through.shape[1]), F32)
    tail = jnp.concatenate([high.astype(F32), low.astype(F32), rest], axis=0)
    return values.astype(BF16), tail.astype(BF16)


def after(earlier, later):
    return later[1] * earlier[0] + later[0], earlier[1] * later[1]


def chosen(condition, first, second):
    return tuple(jnp.where(condition, a, b) for a, b in zip(first, second))


def pair_kernel(info, mine, partner, out):
    half = out.shape[1]
    first = info[FIRST] == 1
    state = out.shape[0] - HALO
    for start in range(0, half, 256):
        place = pl.multiple_of(info[UPPER] * half + start, 256)
        one = split_state(mine[:, pl.ds(place, 256)])
        two = split_state(partner[:, pl.ds(place, 256)])
        total = after(chosen(first, one, two), chosen(first, two, one))
        out[:state, start : start + 256], out[state:, start : start + 256] = joined_state(*total)


def merge_kernel(group, slot, has_entering, last, info, *refs):
    members = refs[: 2**group]
    entering_out = refs[2**group + has_entering]
    rank = info[slot]
    state, half = entering_out.shape
    for start in range(0, half, 256):
        lanes = slice(start, start + 256)
        values = [split_state(member[:, lanes]) for member in members]
        before = (jnp.zeros((state, 256), F32), jnp.ones((1, 256), F32))
        whole = before
        for place in range(2**group):
            value = values[0]
            for code in range(1, 2**group):
                value = chosen((rank ^ code) == place, values[code], value)
            if place < 2**group - 1:
                before = chosen(place < rank, after(before, value), before)
            if not last:
                whole = after(whole, value)
        if has_entering:
            inside = refs[2**group][:, lanes].astype(F32)
            through = jnp.ones((1, 256), F32)
            before = after(before, (inside, through))
        entering_out[:, lanes] = before[0].astype(BF16)
        if not last:
            out = refs[-1]
            out[:state, lanes], out[state:, lanes] = joined_state(*whole)


def small_call(kernel, name, out_shape, info, *operands):
    return pl.pallas_call(
        kernel,
        in_specs=[pl.BlockSpec(memory_space=pltpu.SMEM)] + [whole_block(v.shape) for v in operands],
        out_specs=[whole_block(v.shape) for v in out_shape],
        out_shape=out_shape,
        compiler_params=pltpu.CompilerParams(vmem_limit_bytes=SMALL),
        cost_estimate=pl.CostEstimate(flops=10**6, bytes_accessed=10**6, transcendentals=0),
        name=name,
    )(info, *operands)


def settle_kernel(place, info, base, sent, other, *rest):
    section = info[place]
    rows = (base[...] + other[...].astype(F32)).astype(BF16)
    rows = jnp.where(section == 1, sent[...], rows)
    rest[-1][...] = jnp.where(section == 0, other[...], rows)


def settle(index, chunks, place, info, base, sent, other, finished):
    features = base.shape[1]
    length = chunks * CHUNK
    out_block = pl.BlockSpec((None, CHUNK, features), lambda j: (0, index, 0))
    passed = [] if finished is None else [finished]
    return pl.pallas_call(
        functools.partial(settle_kernel, place),
        grid=(1,),
        in_specs=[pl.BlockSpec(memory_space=pltpu.SMEM)]
        + [whole_block((CHUNK, features))] * 3
        + [pl.BlockSpec(memory_space=pl.ANY)] * len(passed),
        out_specs=out_block,
        out_shape=jax.ShapeDtypeStruct((1, length, features), BF16),
        input_output_aliases={4: 0} if passed else {},
        compiler_params=pltpu.CompilerParams(vmem_limit_bytes=SMALL),
        cost_estimate=pl.CostEstimate(flops=10**6, bytes_accessed=10**6, transcendentals=0),
        name="settle",
    )(info, base, sent, other, *passed)


def stages_of(seq_count):
    bits = seq_count.bit_length() - 1
    found = []
    bit = 1
    while bit < bits:
        group = min(2, bits - bit)
        found.append((bit, group))
        bit += group
    return found


def entering_state(packed, info, sections, seq_count, meanwhile):
    section_count = lax.axis_size("section")
    stages = stages_of(seq_count)

    def swap(value, mask):
        pairs = [
            (i * section_count + s, (i ^ mask) * section_count + s)
            for s in sections
            for i in range(seq_count)
        ]
        return lax.ppermute(value, ("seq", "section"), pairs)

    def forward(value, mask, low_bit):
        pairs = []
        for s in sections:
            for i in range(seq_count):
                later = (i ^ mask) >> low_bit > i >> low_bit
                if later == (s % 2 == 0):
                    pairs.append((i * section_count + s, (i ^ mask) * section_count + s))
        return lax.ppermute(value, ("seq", "section"), pairs)

    depth, inner = packed.shape
    half = jax.ShapeDtypeStruct((depth, inner // 2), BF16)
    states = jax.ShapeDtypeStruct((depth - HALO, inner // 2), BF16)
    partner = swap(packed, 1)
    (total,) = small_call(pair_kernel, "pair", [half], info, packed, partner)
    done = meanwhile(total)
    info, _ = lax.optimization_barrier((info, done[0]))
    entering = []
    for index, (bit, group) in enumerate(stages):
        last = index + 1 == len(stages)
        members = [total]
        for code in range(1, 2**group):
            mask = code << bit
            members.append(forward(total, mask, bit) if last else swap(total, mask))
        kernel = functools.partial(merge_kernel, group, RANKS + index, len(entering), last)
        shapes = [states] if last else [states, half]
        results = small_call(kernel, "merge", shapes, info, *members, *entering)
        entering = [results[0]]
        total = results[-1]
    return (entering[0], swap(entering[0], 1), partner), done


def per_device(
    tokens,
    input_gain,
    main_weight,
    side_weight,
    conv_kernel,
    step_bias,
    decay_rate,
    skip_gain,
    output_gain,
    output_weight,
):
    length, features = tokens.shape
    inner = main_weight.shape[2] // 2
    heads = decay_rate.shape[1]
    state = (side_weight.shape[2] - heads) // 2
    head_dim = inner // heads
    chunks = length // CHUNK
    seq_count = lax.axis_size("seq")
    section_count = lax.axis_size("section")
    section_index = lax.axis_index("section")
    seq_index = lax.axis_index("seq")
    reverse = section_index % 2
    shard = output_weight[0]
    expand = np.repeat(np.eye(heads, dtype=np.float32), head_dim, axis=1)
    spread = jnp.asarray(np.concatenate([expand, expand], axis=0), BF16)
    upper = seq_index % 2
    facts = [reverse, upper, (upper == reverse).astype(jnp.int32), seq_index]
    for bit, group in stages_of(seq_count):
        position = (seq_index >> bit) % 2**group
        facts.append(jnp.where(reverse == 1, 2**group - 1 - position, position))
    places = len(facts)
    rounds = section_count // 2
    for round_index in range(rounds):
        facts.append(section_index - 2 * round_index)
    info = jnp.stack([fact.astype(jnp.int32) for fact in facts])
    order = [chunks - 1, 0] + list(range(1, chunks - 1))

    def edges(first_rows, last_rows, first_wanted, sources, targets):
        pairs = []
        for source, target in zip(sources, targets):
            for i in range(seq_count):
                beside = i + 1 if target % 2 == 0 else i - 1
                if 0 <= beside < seq_count:
                    pairs.append((i * section_count + source, beside * section_count + target))
        value = jnp.where(first_wanted, first_rows, last_rows)
        return lax.ppermute(value, ("seq", "section"), pairs)

    current = tokens
    halo = edges(tokens[:HALO], tokens[length - HALO :], reverse == 1, (0, 1), (0, 1))
    previous = None
    shards = None
    if seq_count == 8:
        halo, shard = lax.optimization_barrier((halo, shard))
        shards = [shard, seq_swap(shard, 2), seq_swap(shard, 4)]
        pieces = None
    else:
        whole = lax.all_gather(shard, "seq", axis=0, tiled=True)
        pieces = [(whole, [(None, 0, 0, inner)])]
    main = main_weight
    params = [
        input_gain, jnp.swapaxes(side_weight, 1, 2), conv_kernel, step_bias, decay_rate, spread,
        skip_gain, output_gain,
    ]
    for round_index in range(rounds):
        active = (2 * round_index, 2 * round_index + 1)
        normed, x, b, c_rows, cumulative, shifted, reach, local, packed = prep(
            info,
            current,
            halo,
            params,
            main,
            inner,
            state,
            round_index > 0,
        )
        early = round_index == 0 and shards
        if early:
            packed, *shards[1:] = lax.optimization_barrier((packed, *shards[1:]))

        def meanwhile(total, normed=normed):
            nonlocal pieces
            if early:
                *parts, _ = lax.optimization_barrier((*shards, total))
                rows = parts[0].shape[0] // 2
                up, down, three = stacked(
                    [
                        [(parts[2], 0, rows)],
                        [(parts[1], 1, rows)],
                        [(part, 0, 2 * rows) for part in parts],
                    ]
                )
                halves = [seq_swap(up, 2), seq_swap(down, 4)]
                swapped = seq_swap(three, 1)
            ready, _ = lax.optimization_barrier((normed, total))
            y, gate = mid(
                ready, main, x, b, c_rows, cumulative, shifted, params, inner,
                round_index > 0,
            )
            if early:
                *halves, _ = lax.optimization_barrier((*halves, y))
                rows = halves[0].shape[0]
                (joined,) = stacked([[(half, 0, rows) for half in halves]])
                diagonal = seq_swap(joined, 1)
                pieces = [(value, [(mask, 0, 0, 2 * rows)]) for value, mask in zip(shards, (0, 2, 4))]
                pieces += [(half, [(6, 0, i * rows, rows)]) for i, half in enumerate(halves)]
                pieces.append((swapped, [(m, i * 2 * rows, 0, 2 * rows) for i, m in enumerate((1, 3, 5))]))
                pieces.append((diagonal, [(7, 0, 0, 2 * rows)]))
            return y, gate

        state_parts, (y, gate) = entering_state(packed, info, active, seq_count, meanwhile)
        last_round = round_index + 1 == rounds
        low, high = active
        place = section_index - low
        terms = {}
        bases = {}
        for members in (order[: chunks // 2], order[chunks // 2 :]):
            outs = finish(
                tuple(members), members[0] == order[0], places if last_round else places + round_index, last_round, info,
                current, y, gate, c_rows, reach, local, state_parts, params, pieces,
                [previous[member] for member in members] if last_round else [],
            )
            for i, member in enumerate(members):
                terms[member] = outs[i]
                bases[member] = outs[len(members) + i]
        if last_round:
            break
        received = []
        values = []
        direct = None
        for step in range(chunks + 2 * SKEW - 1):
            pairs = [(low + hop, low + hop + 1) for hop in range(3) if 0 <= step - hop * SKEW < chunks]
            value = terms[order[step]] if step < chunks else None
            if step >= SKEW:
                passed = received[step - SKEW]
                if step - SKEW < chunks:
                    total = bases[order[step - SKEW]] + passed.astype(F32)
                    total = total if value is None else total + value.astype(F32)
                    passed = total.astype(BF16)
                value = passed
            values.append(value)
            received.append(lax.ppermute(value, "section", pairs))
            if step == chunks + SKEW - 1:
                direct = lax.ppermute(value, "section", [(low + 1, low + 3)])
        received.append(direct)
        trigger, _ = lax.optimization_barrier((values[chunks + SKEW - 1], received[2 * SKEW]))
        main, pieces, *params = hold(info, trigger, main_weight, pieces, params, inner)
        last_rows = jnp.where(place == 3, received[2 * SKEW], received[SKEW])[CHUNK - HALO :]
        first_rows = jnp.where(place == 3, received[2 * SKEW + 1], received[SKEW + 1])[:HALO]
        halo = edges(first_rows, last_rows, reverse == 1, (low + 2, high + 2), (low + 2, high + 2))
        received[-1], received[-2], halo = lax.optimization_barrier((received[-1], received[-2], halo))
        layer_rows = [None] * chunks
        next_rows = [None] * chunks
        for step, index in enumerate(order):
            layer_rows[index] = values[step + SKEW]
            next_rows[index] = jnp.where(place == 3, received[step + 2 * SKEW], received[step + SKEW])
        previous = layer_rows
        current = jnp.concatenate(next_rows, axis=0)
    finished = None
    for index in order:
        other = lax.ppermute(terms[index], "section", [(low, high), (high, low), (1, 0)])
        finished = settle(index, chunks, places, info, bases[index], terms[index], other, finished)
    return finished


def solution(mesh):
    placed = (
        P("seq", None),
        P("section", None),
        P("section", None, None),
        P("section", None, None),
        P("section", None, None),
        P("section", None),
        P("section", None),
        P("section", None),
        P("section", None),
        P("section", "seq", None),
    )
    return jax.shard_map(
        per_device, mesh=mesh, in_specs=placed, out_specs=P("section", "seq", None), check_vma=False
    )
```
